32 devices in a mesh: case: 4 (over y, core), mod: 8 (over z, x).
Axes of the slice: x: 2, y: 2, z: 4, core: 2. Of those that a mesh axis runs over, the one named last changes fastest.
Arguments:
- turbulence: float32 [4, 256, 256], P('case'), may hold values from -6 to 6
- pupil_amp: float32 [256, 256], replicated, may hold values from 0.3 to 1
- mod_points: int32 [8], P('mod'), may hold values from 0 to 255
- valid_pix: int32 [8192], P('mod'), may hold values from 0 to 262143, as said below
- recon: bfloat16 [5120, 8192], P('case', 'mod'), may hold values from -0.0625 to 0.0625
- gx: float32 [256, 64], replicated, may hold values from -1.2 to 1.2
- gy: float32 [256, 80], replicated, may hold values from -1.2 to 1.2
- act_map: int32 [5120], replicated, may hold values from 0 to 5119, each once
Outputs:
- command_total: float32 [4, 5120], P('case')
- frame: float32 [4, 512, 512], P('case', 'mod')
The draws below stay inside these ranges and needn't reach their ends.
Inputs may be any that keep to these rules, and one draw needn't show every extreme that they name: `valid_pix`: entries k * 1024 to (k + 1) * 1024 - 1 are flat indices (row times 512 plus column) of pixels in detector rows k * 64 to (k + 1) * 64 - 1.
All inputs are finite; a program needn't handle non-finite values.
Results may differ from the reference program's by a relative error of at most 0.0058.
Values may be sent and summed in bfloat16 or wider, within the bound.
No kernel may reach another device: no remote copies, remote signals or barrier semaphores. Data moves between devices by JAX's collectives and lax.ppermute only.
A program may use at most 64 MiB of HBM per device.

```python
import math
import jax
import jax.numpy as jnp
from jax import lax

PUPIL = 256
NF = 512
AY = 64
AX = 80
SIG_DEV = 1024
STEPS = 2
CASES = 4
MODS = 8
NACT = 5120
NSIG = 8192
ROWBLK = 64


def draw_valid_pix(key, part):
    block_pixels = ROWBLK * NF
    keys = jax.random.split(jax.random.fold_in(key, 7), MODS)

    def one_block(block_key):
        return jax.random.permutation(block_key, block_pixels)[:SIG_DEV].astype(jnp.int32)
    picks = jax.vmap(one_block)(keys)
    base = jnp.arange(MODS, dtype=jnp.int32)[:, None] * block_pixels
    flat = (picks + base).reshape(-1).astype(jnp.int32)
    flat = flat.at[0].set(0)
    flat = flat.at[-1].set(NF * NF - 1)
    return flat


def plant(entries, rng, smallest, largest):
    spot = [jax.random.randint(jax.random.fold_in(rng, axis), (), 0, length) for axis, length in enumerate(entries.shape)]
    longest = entries.shape.index(max(entries.shape))
    next_to = spot[:longest] + [(spot[longest] + 1) % entries.shape[longest]] + spot[longest + 1:]
    return entries.at[tuple(spot)].set(smallest).at[tuple(next_to)].set(largest)


def levels(rng, dims, pieces, low, largest):
    def one(dim, parts):
        draws = jax.random.uniform(jax.random.fold_in(jax.random.fold_in(rng, 6), dim), (parts,), jnp.float32, low / len(pieces), largest / len(pieces))
        return jnp.repeat(jnp.exp(draws), dims[dim] // parts).reshape((-1,) + (1,) * (len(dims) - dim - 1))

    loudness = one(*pieces[0])
    for cut in pieces[1:]:
        loudness = loudness * one(*cut)
    return loudness


def bell_draw(key, dims, deviation, reach, pieces=(), kind=jnp.bfloat16):
    values = jax.random.normal(key, dims, jnp.float32) * deviation
    if len(pieces) > 0:
        values = levels(key, dims, pieces, -0.22, 0.18) * values
    return jnp.clip(values, min=-reach, max=reach).astype(kind)


def setup_inputs(seed: int = 0) -> dict:
    streams_of = jax.random.split(jax.random.key(seed), 9)
    return {
        "turbulence": bell_draw(streams_of[0], (CASES, PUPIL, PUPIL), 1.0, 6.0, ((0, 4),), jnp.float32),
        "pupil_amp": jnp.clip(jax.random.uniform(streams_of[1], (PUPIL, PUPIL), jnp.float32, 0.3, 1.0), 0.3, 1.0),
        "mod_points": plant(jax.random.randint(streams_of[2], (MODS,), 0, 256), jax.random.fold_in(streams_of[2], 1), 0, 255).astype(jnp.int32),
        "valid_pix": draw_valid_pix(jax.random.fold_in(streams_of[8], 71), 0),
        "recon": bell_draw(streams_of[4], (NACT, NSIG), NSIG ** -0.5, 0.0625, ((0, 4), (1, 8))),
        "gx": bell_draw(streams_of[5], (PUPIL, AY), 0.2, 1.2, (), jnp.float32),
        "gy": bell_draw(streams_of[6], (PUPIL, AX), 0.2, 1.2, (), jnp.float32),
        "act_map": jax.random.permutation(streams_of[7], NACT).astype(jnp.int32),
    }


loop_gain = 0.5
radius_pixels = 6.0
point_count = 256

def product(left, right):
    return jnp.dot(left.astype(jnp.float32), right.astype(jnp.float32), preferred_element_type=jnp.float32)

def phase_table(length, pupil_width, sign_factor):
    centred = jnp.arange(length, dtype=jnp.int32) - length // 2
    position = jnp.arange(pupil_width, dtype=jnp.int32)
    wrapped = jnp.mod(centred[:, None] * position[None, :], length).astype(jnp.float32)
    angles = 2.0 * math.pi / length * wrapped
    factor = 1.0 / math.sqrt(length)
    return (jnp.cos(angles) * factor, sign_factor * jnp.sin(angles) * factor)

def optics_tables(pupil_size, length):
    fwd_cos, fwd_sin = phase_table(length, pupil_size, -1.0)
    inv_cos, inv_sin = phase_table(length, length, 1.0)
    inv_cos = inv_cos.T
    inv_sin = inv_sin.T
    table_one = jnp.concatenate([fwd_cos, fwd_sin], 0).astype(jnp.bfloat16)
    table_two = jnp.concatenate([jnp.concatenate([fwd_cos.T, fwd_sin.T], 1), jnp.concatenate([-fwd_sin.T, fwd_cos.T], 1)], 0).astype(jnp.bfloat16)
    table_three = jnp.concatenate([inv_cos, inv_sin], 0).astype(jnp.bfloat16)
    table_four = jnp.concatenate([jnp.concatenate([inv_cos.T, inv_sin.T], 1), jnp.concatenate([-inv_sin.T, inv_cos.T], 1)], 0).astype(jnp.bfloat16)
    offset = jnp.abs(jnp.arange(length, dtype=jnp.float32) - length // 2)
    mask_angle = 0.5 * math.pi * (offset[:, None] + offset[None, :])
    return (table_one, table_two, table_three, table_four, jnp.cos(mask_angle), jnp.sin(mask_angle))

def detector_frame(pupil_phase, amplitude, mod_point, tables):
    table_one, table_two, table_three, table_four, mask_cos, mask_sin = tables
    pupil_size = pupil_phase.shape[0]
    length = mask_cos.shape[0]
    centred = jnp.arange(pupil_size, dtype=jnp.float32) - pupil_size // 2
    tilt_angle = 2.0 * math.pi / point_count * mod_point.astype(jnp.float32)
    tilt_phase = 2.0 * math.pi * radius_pixels / length * (centred[:, None] * jnp.cos(tilt_angle) + centred[None, :] * jnp.sin(tilt_angle))
    total_phase = pupil_phase + tilt_phase
    pupil_field = jnp.concatenate([amplitude * jnp.cos(total_phase), amplitude * jnp.sin(total_phase)], 1).astype(jnp.bfloat16)
    section_one = product(table_one, pupil_field)
    real_part = section_one[:length, :pupil_size] - section_one[length:, pupil_size:]
    imag_part = section_one[:length, pupil_size:] + section_one[length:, :pupil_size]
    focal_half = jnp.concatenate([real_part, imag_part], 1).astype(jnp.bfloat16)
    focal_field = product(focal_half, table_two)
    focal_real = focal_field[:, :length]
    focal_imag = focal_field[:, length:]
    masked = jnp.concatenate([focal_real * mask_cos - focal_imag * mask_sin, focal_real * mask_sin + focal_imag * mask_cos], 1).astype(jnp.bfloat16)
    section_three = product(table_three, masked)
    inverse_half = jnp.concatenate([section_three[:length, :length] - section_three[length:, length:], section_three[:length, length:] + section_three[length:, :length]], 1).astype(jnp.bfloat16)
    detector_field = product(inverse_half, table_four)
    return detector_field[:, :length] ** 2 + detector_field[:, length:] ** 2

def mirror_surface(commands, act_map, gx, gy):
    actuator_grid = commands[act_map].reshape(gx.shape[1], gy.shape[1])
    rows_mapped = jnp.dot(gx, actuator_grid, precision=lax.Precision.HIGHEST, preferred_element_type=jnp.float32)
    return jnp.dot(rows_mapped, gy.T, precision=lax.Precision.HIGHEST, preferred_element_type=jnp.float32)

def reference(turbulence, pupil_amp, mod_points, valid_pix, recon, gx, gy, act_map):
    tables = optics_tables(PUPIL, NF)

    def case_frame(pupil_phase):

        def add_point(running, mod_point):
            return (running + detector_frame(pupil_phase, pupil_amp, mod_point, tables) / MODS, None)
        summed, unused = lax.scan(add_point, jnp.zeros((NF, NF), jnp.float32), mod_points)
        return summed
    command_total = jnp.zeros((CASES, NACT), jnp.float32)
    pupil_phase = turbulence
    frames = jnp.zeros((CASES, NF, NF), jnp.float32)
    for iteration in range(STEPS):
        frames = lax.map(case_frame, pupil_phase)
        signals = frames.reshape(CASES, NF * NF)[:, valid_pix].astype(jnp.bfloat16)
        commands = product(signals, recon.T)
        command_total = command_total + loop_gain * commands
        if iteration + 1 < STEPS:
            surfaces = jax.vmap(lambda single: mirror_surface(single, act_map, gx, gy))(command_total)
            pupil_phase = turbulence - surfaces
    return (command_total, frames)
```

```python
import math

import jax
import jax.numpy as jnp
import numpy as np
from jax import lax
from jax.experimental import pallas as pl
from jax.experimental.pallas import tpu as pltpu
from jax.sharding import PartitionSpec as P

STEPS = 2


loop_gain = 0.5
radius_pixels = 6.0
point_count = 256
LANES = 128
VMEM_LIMIT = 32 * 1024 * 1024


def rounded_table(angle, length, sign):
    scale = 1.0 / math.sqrt(length)
    real = (np.cos(angle) * scale).astype(np.float32).astype(jnp.bfloat16).astype(np.float64)
    imag = (sign * np.sin(angle) * scale).astype(np.float32).astype(jnp.bfloat16).astype(np.float64)
    return real + 1j * imag


def pyramid_table(pupil_size, length):
    centred = np.arange(length) - length // 2
    forward = np.mod(centred[:, None] * np.arange(pupil_size)[None, :], length) * (2.0 * math.pi / length)
    inverse = np.mod(np.arange(length)[:, None] * centred[None, :], length) * (2.0 * math.pi / length)
    mask = np.array([1, 1j, -1, -1j])[np.abs(centred) % 4]
    return rounded_table(inverse, length, 1.0) @ (mask[:, None] * rounded_table(forward, length, -1.0))


def sin_cos(angle):
    turns = jnp.floor(angle * (2.0 / math.pi) + 0.5)
    rest = angle - turns * 1.5703125
    rest = rest - turns * 4.837512969970703125e-4
    rest = rest - turns * 7.54978995489188216e-8
    square = rest * rest
    sine = rest + rest * square * (-1.6666654611e-1 + square * (8.3321608736e-3 - square * 1.9515295891e-4))
    cosine = (
        1.0
        - 0.5 * square
        + square * square * (4.166664568298827e-2 + square * (-1.388731625493765e-3 + square * 2.443315711809948e-5))
    )
    quarter = turns.astype(jnp.int32)
    swap = (quarter & 1) == 1
    sin_out = jnp.where(swap, cosine, sine)
    cos_out = jnp.where(swap, sine, cosine)
    sin_out = jnp.where((quarter & 2) == 2, -sin_out, sin_out)
    cos_out = jnp.where(((quarter + 1) & 2) == 2, -cos_out, cos_out)
    return sin_out, cos_out


def field_matrix(phase, amplitude):
    sine, cosine = sin_cos(phase)
    real, imag = amplitude * cosine, amplitude * sine
    top = jnp.concatenate([real, imag], 1)
    bottom = jnp.concatenate([-imag, real], 1)
    return jnp.concatenate([top, bottom], 0).astype(jnp.bfloat16)


def field_kernel(phase_ref, amp_ref, out_ref):
    out_ref[...] = field_matrix(phase_ref[...], amp_ref[...])


def look_up(rows, index):
    count, row = rows
    high = index >> 7
    low = index & (LANES - 1)
    sums = [jnp.zeros(index.shape, jnp.float32) for _ in range(4)]
    for i in range(count):
        spread = jnp.broadcast_to(row(i), index.shape)
        picked = jnp.take_along_axis(spread, low, axis=1, mode="promise_in_bounds")
        sums[i % 4] = jnp.where(high == i, picked, sums[i % 4])
    return (sums[0] + sums[1]) + (sums[2] + sums[3])


def optics(points, field, rows_table, full_table, frame_ref, sums_axis):
    row_count = rows_table.shape[0]
    pupil = rows_table.shape[1] // 2
    length = full_table.shape[1] // 2
    count = points.shape[0]
    angle = points.astype(jnp.float32) * (2.0 * math.pi / point_count)
    sin_a, cos_a = sin_cos(angle)
    spread = pupil // LANES
    sin_a = jnp.concatenate([sin_a] * spread, 1)
    cos_a = jnp.concatenate([cos_a] * spread, 1)
    place = (lax.broadcasted_iota(jnp.int32, (count, pupil), 1) - pupil // 2).astype(jnp.float32)
    place = place * (2.0 * math.pi * radius_pixels / length)
    s1, c1 = sin_cos(place * cos_a)
    s2, c2 = sin_cos(place * sin_a)
    real, imag = rows_table[:, :pupil][None], rows_table[:, pupil:][None]
    s1, c1 = s1[:, None, :], c1[:, None, :]
    left = jnp.concatenate([real * c1 - imag * s1, real * s1 + imag * c1], 2)
    left = left.reshape(count * row_count, 2 * pupil).astype(jnp.bfloat16)
    half = jnp.dot(left, field, preferred_element_type=jnp.float32)
    half = half.reshape(count, row_count, 2 * pupil)
    real, imag = half[:, :, :pupil], half[:, :, pupil:]
    s2, c2 = s2[:, None, :], c2[:, None, :]
    half = jnp.concatenate([real * c2 - imag * s2, real * s2 + imag * c2], 2)
    half = half.reshape(count * row_count, 2 * pupil).astype(jnp.bfloat16)
    detector = jnp.dot(half, full_table, preferred_element_type=jnp.float32)
    real, imag = detector[:, :length], detector[:, length:]
    intensity = (real * real + imag * imag).reshape(count, row_count, length)
    frame_ref[...] = jnp.sum(intensity, 0) * (1.0 / count)


def read_signals(frame_ref, pixels):
    row_count, length = frame_ref.shape
    per_row = length // LANES

    def row(i):
        column = (i % per_row) * LANES
        return frame_ref[i // per_row : i // per_row + 1, column : column + LANES]

    picked = look_up((row_count * per_row, row), pixels)
    return picked.astype(jnp.bfloat16).astype(jnp.float32)


def first_kernel(points_ref, field_ref, rows_ref, full_ref, pixels_ref, frame_ref, signal_ref):
    optics(points_ref[...], field_ref[...], rows_ref[...], full_ref[...], frame_ref, None)
    signal_ref[...] = read_signals(frame_ref, pixels_ref[...])


def summed_commands(parts_ref, cases):
    parts = parts_ref[...].astype(jnp.float32)
    return jnp.sum(parts.reshape(cases, parts.shape[0] // cases, parts.shape[1]), 1)


def later_kernel(
    parts_ref, total_ref, map_ref, gx_ref, gyt_ref, phase_ref, amp_ref, points_ref, rows_ref, full_ref, pixels_ref,
    frame_ref, signal_ref, new_total_ref,
):
    cases, block = total_ref.shape
    total = total_ref[...] + loop_gain * summed_commands(parts_ref, cases)
    new_total_ref[...] = total
    per_case = block // LANES

    def row(i):
        column = (i % per_case) * LANES
        return total[i // per_case : i // per_case + 1, column : column + LANES]

    grid = look_up((cases * per_case, row), map_ref[...])
    rows_mapped = jnp.dot(gx_ref[...], grid, precision=lax.Precision.HIGHEST, preferred_element_type=jnp.float32)
    surface = jnp.dot(
        rows_mapped, gyt_ref[...], precision=lax.Precision.HIGHEST, preferred_element_type=jnp.float32
    )
    field = field_matrix(phase_ref[...] - surface, amp_ref[...])
    optics(points_ref[...], field, rows_ref[...], full_ref[...], frame_ref, None)
    signal_ref[...] = read_signals(frame_ref, pixels_ref[...])


def command_kernel(own_case_ref, *refs):
    signal_refs, recon_ref, out_ref = refs[:-2], refs[-2], refs[-1]
    cases = len(signal_refs)
    own_case = own_case_ref[0]
    received = [ref[...] for ref in signal_refs]
    ordered = []
    for case in range(cases):
        values = received[0]
        for j in range(1, cases):
            values = jnp.where((own_case ^ j) == case, received[j], values)
        ordered.append(values)
    groups = received[0].shape[0]
    signals = jnp.concatenate(
        [jnp.concatenate([values[g : g + 1] for values in ordered], 0) for g in range(groups)], 1
    ).astype(jnp.bfloat16)
    partial = lax.dot_general(
        signals, recon_ref[...], (((1,), (1,)), ((), ())), preferred_element_type=jnp.float32
    )
    copies = out_ref.shape[0] // cases
    spread = jnp.concatenate([jnp.broadcast_to(partial[c : c + 1], (copies, partial.shape[1])) for c in range(cases)], 0)
    out_ref[...] = spread.astype(jnp.bfloat16)


def last_kernel(parts_ref, total_ref, out_ref):
    cases, block = total_ref.shape
    total = total_ref[...] + loop_gain * summed_commands(parts_ref, cases)
    for case in range(cases):
        out_ref[:, case * block : (case + 1) * block] = total[case : case + 1]


def body(turbulence, pupil_amp, mod_points, valid_pix, recon, gx, gy, act_map):
    pupil = pupil_amp.shape[0]
    length = 2 * pupil
    cases = lax.axis_size("case")
    devices_mod = lax.axis_size("mod")
    per_device = mod_points.shape[0]
    count = devices_mod * per_device
    row_count = length // devices_mod
    block = recon.shape[0]
    signal_rows = valid_pix.shape[0] // LANES
    own_mod = lax.axis_index("mod")
    own_case = lax.axis_index("case")
    screen = turbulence[0]
    params = pltpu.CompilerParams(vmem_limit_bytes=VMEM_LIMIT)

    table = pyramid_table(pupil, length)
    rows_all = jnp.asarray(np.concatenate([table.real, table.imag], 1).astype(np.float32))
    full = np.concatenate(
        [
            np.concatenate([table.real.T, table.imag.T], 1),
            np.concatenate([-table.imag.T, table.real.T], 1),
        ],
        0,
    )
    full_table = jnp.asarray(full.astype(np.float32)).astype(jnp.bfloat16)
    rows_table = lax.dynamic_slice_in_dim(rows_all, own_mod * row_count, row_count, 0)

    with jax.named_scope("modulation_points"):
        points = jnp.broadcast_to(mod_points[None, :, None], (devices_mod, per_device, LANES))
        points = lax.all_to_all(points, "mod", 0, 0, tiled=True).reshape(count, LANES)
    pixels = (valid_pix - own_mod * (row_count * length)).reshape(signal_rows, LANES)
    grid_rows, grid_columns = gx.shape[1], gy.shape[1]
    cell_map = jnp.pad(act_map.reshape(grid_rows, grid_columns), ((0, 0), (0, LANES - grid_columns)))
    gy_t = jnp.pad(gy.T, ((0, LANES - grid_columns), (0, 0)))

    frame_shape = jax.ShapeDtypeStruct((row_count, length), jnp.float32)
    signal_shape = jax.ShapeDtypeStruct((signal_rows, LANES), jnp.float32)
    total_shape = jax.ShapeDtypeStruct((cases, block), jnp.float32)

    def commands(signal):
        signals = [signal]
        for j in range(1, cases):
            signals.append(lax.ppermute(signal, "case", [(i, i ^ j) for i in range(cases)]))
        partial = pl.pallas_call(
            command_kernel,
            out_shape=jax.ShapeDtypeStruct((cases * devices_mod, block), jnp.bfloat16),
            in_specs=[pl.BlockSpec(memory_space=pltpu.SMEM)] + [pl.BlockSpec(memory_space=pltpu.VMEM)] * (cases + 1),
            compiler_params=params,
            name="commands",
        )(own_case.reshape(1), *signals, recon)
        return lax.all_to_all(partial, ("case", "mod"), 0, 0, tiled=True)

    field = pl.pallas_call(
        field_kernel,
        out_shape=jax.ShapeDtypeStruct((2 * pupil, 2 * pupil), jnp.bfloat16),
        compiler_params=params,
        name="field",
    )(screen, pupil_amp)
    frame, signal = pl.pallas_call(
        first_kernel,
        out_shape=(frame_shape, signal_shape),
        compiler_params=params,
        name="first_frame",
    )(points, field, rows_table, full_table, pixels)
    total = jnp.zeros((cases, block), jnp.float32)
    for iteration in range(1, STEPS):
        parts = commands(signal)
        frame, signal, total = pl.pallas_call(
            later_kernel,
            out_shape=(frame_shape, signal_shape, total_shape),
            compiler_params=params,
            name="next_frame",
        )(parts, total, cell_map, gx, gy_t, screen, pupil_amp, points, rows_table, full_table, pixels)
    parts = commands(signal)
    command_total = pl.pallas_call(
        last_kernel,
        out_shape=jax.ShapeDtypeStruct((1, cases * block), jnp.float32),
        compiler_params=params,
        name="total",
    )(parts, total)
    return (command_total, frame[None])


def solution(mesh):
    return jax.shard_map(
        body,
        mesh=mesh,
        in_specs=(P("case", None, None), P(), P("mod"), P("mod"), P("case", "mod"), P(), P(), P()),
        out_specs=(P("case", None), P("case", "mod", None)),
        check_vma=False,
    )
```

```python
import math

import jax
import jax.numpy as jnp
import numpy as np
from jax import lax
from jax.experimental import pallas as pl
from jax.experimental.pallas import tpu as pltpu
from jax.sharding import PartitionSpec as P

STEPS = 2


loop_gain = 0.5
radius_pixels = 6.0
point_count = 256
LANES = 128
VMEM_LIMIT = 16 * 1024 * 1024


def rounded_table(angle, length, sign):
    scale = 1.0 / math.sqrt(length)
    real = (np.cos(angle) * scale).astype(np.float32).astype(jnp.bfloat16).astype(np.float64)
    imag = (sign * np.sin(angle) * scale).astype(np.float32).astype(jnp.bfloat16).astype(np.float64)
    return real + 1j * imag


def pyramid_table(pupil_size, length):
    centred = np.arange(length) - length // 2
    forward = np.mod(centred[:, None] * np.arange(pupil_size)[None, :], length) * (2.0 * math.pi / length)
    inverse = np.mod(np.arange(length)[:, None] * centred[None, :], length) * (2.0 * math.pi / length)
    mask = np.array([1, 1j, -1, -1j])[np.abs(centred) % 4]
    return rounded_table(inverse, length, 1.0) @ (mask[:, None] * rounded_table(forward, length, -1.0))


def sin_cos(angle):
    turns = jnp.floor(angle * (2.0 / math.pi) + 0.5)
    rest = angle - turns * 1.5703125
    rest = rest - turns * 4.837512969970703125e-4
    rest = rest - turns * 7.54978995489188216e-8
    square = rest * rest
    sine = rest + rest * square * (-1.6666654611e-1 + square * (8.3321608736e-3 - square * 1.9515295891e-4))
    cosine = (
        1.0
        - 0.5 * square
        + square * square * (4.166664568298827e-2 + square * (-1.388731625493765e-3 + square * 2.443315711809948e-5))
    )
    quarter = turns.astype(jnp.int32)
    swap = (quarter & 1) == 1
    sin_out = jnp.where(swap, cosine, sine)
    cos_out = jnp.where(swap, sine, cosine)
    sin_out = jnp.where((quarter & 2) == 2, -sin_out, sin_out)
    cos_out = jnp.where(((quarter + 1) & 2) == 2, -cos_out, cos_out)
    return sin_out, cos_out


def field_matrix(phase, amplitude):
    sine, cosine = sin_cos(phase)
    real, imag = amplitude * cosine, amplitude * sine
    top = jnp.concatenate([real, imag], 1)
    bottom = jnp.concatenate([-imag, real], 1)
    return jnp.concatenate([top, bottom], 0).astype(jnp.bfloat16)


def halves(values):
    high = values.astype(jnp.bfloat16)
    low = (values - high.astype(jnp.float32)).astype(jnp.bfloat16)
    return high, low


def look_up(count, row, index):
    high = index >> 7
    low = index & (LANES - 1)
    sums = [jnp.zeros(index.shape, jnp.float32) for _ in range(4)]
    for i in range(count):
        spread = jnp.broadcast_to(row(i), index.shape)
        picked = jnp.take_along_axis(spread, low, axis=1, mode="promise_in_bounds")
        sums[i % 4] = jnp.where(high == i, picked, sums[i % 4])
    return (sums[0] + sums[1]) + (sums[2] + sums[3])


def runs(ref):
    per_row = ref.shape[1] // LANES

    def row(i):
        column = (i % per_row) * LANES
        return ref[i // per_row : i // per_row + 1, column : column + LANES]

    return ref.shape[0] * per_row, row


def prepare_kernel(
    phase_ref, amp_ref, table_ref, map_ref, gxt_ref, gyt_ref,
    field_ref, full_ref, cells_ref, gx_out_ref, gy_out_ref, floats,
):
    field_ref[...] = field_matrix(phase_ref[...], amp_ref[...])
    full_ref[...] = table_ref[...]
    floats[...] = map_ref[...].astype(jnp.float32)
    grid_rows, grid_columns = gxt_ref.shape[0], gyt_ref.shape[0]
    cell = lax.broadcasted_iota(jnp.int32, cells_ref.shape, 0) * grid_columns
    column = lax.broadcasted_iota(jnp.int32, cells_ref.shape, 1)
    cell = jnp.where(column < grid_columns, cell + column, 0)
    cells_ref[...] = look_up(*runs(floats), cell).astype(jnp.int32)
    high, low = halves(gxt_ref[...].T)
    gx_out_ref[...] = jnp.concatenate([high, low, high], 1)
    gyt = jnp.concatenate(
        [gyt_ref[...], jnp.zeros((LANES - grid_columns, gyt_ref.shape[1]), jnp.float32)], 0
    )
    high, low = halves(gyt)
    gy_out_ref[...] = jnp.concatenate([high, high, low], 0)


def tilt_factors(angles_ref, pupil, length):
    sin_a, cos_a = sin_cos(angles_ref[...])
    spread = pupil // LANES
    sin_a = jnp.concatenate([sin_a] * spread, 1)
    cos_a = jnp.concatenate([cos_a] * spread, 1)
    place = (lax.broadcasted_iota(jnp.int32, sin_a.shape, 1) - pupil // 2).astype(jnp.float32)
    place = place * (2.0 * math.pi * radius_pixels / length)
    return sin_cos(place * cos_a), sin_cos(place * sin_a)


def turned(real, imag, sine, cosine):
    sine, cosine = sine[:, None, :], cosine[:, None, :]
    return jnp.concatenate([real * cosine - imag * sine, real * sine + imag * cosine], 2)


def optics(left, field, full_table, sine, cosine):
    count, pupil = sine.shape
    row_count = left.shape[0] // count
    length = full_table.shape[1] // 2
    half = jnp.dot(left, field, preferred_element_type=jnp.float32)
    half = half.reshape(count, row_count, 2 * pupil)
    half = turned(half[:, :, :pupil], half[:, :, pupil:], sine, cosine)
    half = half.reshape(count * row_count, 2 * pupil).astype(jnp.bfloat16)
    detector = jnp.dot(half, full_table, preferred_element_type=jnp.float32)
    real, imag = detector[:, :length], detector[:, length:]
    intensity = (real * real + imag * imag).reshape(count, row_count, length)
    return jnp.sum(intensity, 0) * (1.0 / count)


def read_signals(frame_ref, pixels):
    return look_up(*runs(frame_ref), pixels).astype(jnp.bfloat16).astype(jnp.float32)


def first_kernel(
    angles_ref, field_ref, rows_ref, full_ref, pixels_ref,
    signal_ref, left_ref, sine_ref, cosine_ref, frame_ref,
):
    pupil = rows_ref.shape[1] // 2
    (s1, c1), (s2, c2) = tilt_factors(angles_ref, pupil, full_ref.shape[1] // 2)
    rows = rows_ref[...]
    left = turned(rows[None, :, :pupil], rows[None, :, pupil:], s1, c1)
    left = left.reshape(left_ref.shape).astype(jnp.bfloat16)
    left_ref[...] = left
    sine_ref[...] = s2
    cosine_ref[...] = c2
    frame_ref[...] = optics(left, field_ref[...], full_ref[...], s2, c2)
    signal_ref[...] = read_signals(frame_ref, pixels_ref[...])


def add_commands(parts_ref, total_ref, out_ref):
    cases = out_ref.shape[0]
    each = parts_ref.shape[0] // cases
    for case in range(cases):
        sums = jnp.sum(parts_ref[case * each : (case + 1) * each].astype(jnp.float32), 0)
        out_ref[case] = loop_gain * sums if total_ref is None else total_ref[case] + loop_gain * sums


def later_kernel(
    parts_ref, cells_ref, gx_ref, gy_ref, phase_ref, amp_ref, left_ref, sine_ref, cosine_ref, full_ref, pixels_ref,
    *refs,
):
    frame_out_ref, signal_ref, new_total_ref, frame_ref, frame_done = refs[-5:]
    add_commands(parts_ref, refs[0] if len(refs) > 5 else None, new_total_ref)
    cases, pieces, width = new_total_ref.shape
    per_piece = width // LANES

    def row(i):
        column = (i % per_piece) * LANES
        piece = i // per_piece
        return new_total_ref[piece // pieces, piece % pieces : piece % pieces + 1, column : column + LANES]

    grid = look_up(cases * pieces * per_piece, row, cells_ref[...])
    high, low = halves(grid)
    rows_mapped = jnp.dot(
        gx_ref[...], jnp.concatenate([high, high, low], 0), preferred_element_type=jnp.float32
    )
    high, low = halves(rows_mapped)
    surface = jnp.dot(
        jnp.concatenate([high, low, high], 1), gy_ref[...], preferred_element_type=jnp.float32
    )
    field = field_matrix(phase_ref[...] - surface, amp_ref[...])
    frame_ref[...] = optics(left_ref[...], field, full_ref[...], sine_ref[...], cosine_ref[...])
    copy = pltpu.make_async_copy(frame_ref, frame_out_ref, frame_done)
    copy.start()
    signal_ref[...] = read_signals(frame_ref, pixels_ref[...])
    copy.wait()


def command_kernel(own_case_ref, *refs):
    signal_refs, recon_ref, out_ref = refs[:-2], refs[-2], refs[-1]
    cases = len(signal_refs)
    own_case = own_case_ref[0]
    received = [ref[...] for ref in signal_refs]
    ordered = []
    for case in range(cases):
        values = received[0]
        for j in range(1, cases):
            values = jnp.where((own_case ^ j) == case, received[j], values)
        ordered.append(values)
    groups = received[0].shape[0]
    signals = jnp.concatenate(
        [jnp.concatenate([values[g : g + 1] for values in ordered], 0) for g in range(groups)], 1
    ).astype(jnp.bfloat16)
    partial = lax.dot_general(
        signals, recon_ref[...], (((1,), (1,)), ((), ())), preferred_element_type=jnp.float32
    )
    messages, pieces, width = out_ref.shape
    copies = messages // cases
    for case in range(cases):
        message = jnp.concatenate(
            [partial[case : case + 1, i * width : (i + 1) * width] for i in range(pieces)], 0
        ).astype(jnp.bfloat16)
        for i in range(copies):
            out_ref[case * copies + i] = message


def last_kernel(parts_ref, total_ref, out_ref, sums_ref):
    add_commands(parts_ref, total_ref, sums_ref)
    cases, pieces, width = sums_ref.shape
    for case in range(cases):
        for i in range(pieces):
            start = (case * pieces + i) * width
            out_ref[:, start : start + width] = sums_ref[case, i : i + 1, :]


def body(turbulence, pupil_amp, mod_points, valid_pix, recon, gx, gy, act_map):
    pupil = pupil_amp.shape[0]
    length = 2 * pupil
    cases = lax.axis_size("case")
    devices_mod = lax.axis_size("mod")
    per_device = mod_points.shape[0]
    count = devices_mod * per_device
    row_count = length // devices_mod
    block = recon.shape[0]
    pieces = 2
    signal_rows = valid_pix.shape[0] // LANES
    own_mod = lax.axis_index("mod")
    own_case = lax.axis_index("case")
    screen = turbulence[0]

    def call(kernel, name, out_shape, scratch=(), **specs):
        return pl.pallas_call(
            kernel,
            out_shape=out_shape,
            scratch_shapes=scratch,
            compiler_params=pltpu.CompilerParams(vmem_limit_bytes=VMEM_LIMIT),
            name=name,
            **specs,
        )

    table = pyramid_table(pupil, length)
    rows_all = jnp.asarray(np.concatenate([table.real, table.imag], 1).astype(np.float32))
    full_table = jnp.asarray(
        np.concatenate(
            [
                np.concatenate([table.real.T, table.imag.T], 1),
                np.concatenate([-table.imag.T, table.real.T], 1),
            ],
            0,
        ).astype(jnp.bfloat16)
    )
    rows_table = lax.dynamic_slice_in_dim(rows_all, own_mod * row_count, row_count, 0)

    with jax.named_scope("modulation_angles"):
        angles = mod_points.astype(jnp.float32) * (2.0 * math.pi / point_count)
        angles = jnp.broadcast_to(angles[None, :, None], (devices_mod, per_device, LANES))
        angles = lax.all_to_all(angles, "mod", 0, 0, tiled=True).reshape(count, LANES)
    pixels = (valid_pix - own_mod * (row_count * length)).reshape(signal_rows, LANES)
    grid_rows = gx.shape[1]

    f32, bf16 = jnp.float32, jnp.bfloat16
    shape = jax.ShapeDtypeStruct
    field, full_table, cells, gx_parts, gy_parts = call(
        prepare_kernel,
        "prepare",
        (
            shape((2 * pupil, 2 * pupil), bf16),
            shape(full_table.shape, bf16),
            shape((grid_rows, LANES), jnp.int32),
            shape((pupil, 3 * grid_rows), bf16),
            shape((3 * LANES, pupil), bf16),
        ),
        [pltpu.VMEM((act_map.shape[0] // LANES, LANES), f32)],
    )(screen, pupil_amp, full_table, act_map.reshape(-1, LANES), gx.T, gy.T)

    def commands(signal):
        signals = [signal]
        for j in range(1, cases):
            signals.append(lax.ppermute(signal, "case", [(i, i ^ j) for i in range(cases)]))
        partial = call(
            command_kernel,
            "commands",
            shape((cases * devices_mod, pieces, block // pieces), bf16),
            in_specs=[pl.BlockSpec(memory_space=pltpu.SMEM)] + [pl.BlockSpec(memory_space=pltpu.VMEM)] * (cases + 1),
        )(own_case.reshape(1), *signals, recon)
        return lax.all_to_all(partial, ("case", "mod"), 0, 0, tiled=True)

    signal, left, sine, cosine = call(
        first_kernel,
        "first_frame",
        (
            shape((signal_rows, LANES), f32),
            shape((count * row_count, 2 * pupil), bf16),
            shape((count, pupil), f32),
            shape((count, pupil), f32),
        ),
        [pltpu.VMEM((row_count, length), f32)],
    )(angles, field, rows_table, full_table, pixels)
    total_shape = shape((cases, pieces, block // pieces), f32)
    totals = ()
    for iteration in range(1, STEPS):
        parts = commands(signal)
        frame, signal, *totals = call(
            later_kernel,
            "next_frame",
            (
                shape((row_count, length), f32),
                shape((signal_rows, LANES), f32),
                total_shape,
            ),
            [pltpu.VMEM((row_count, length), f32), pltpu.SemaphoreType.DMA(())],
            out_specs=(
                pl.BlockSpec(memory_space=pl.ANY),
                pl.BlockSpec(memory_space=pltpu.VMEM),
                pl.BlockSpec(memory_space=pltpu.VMEM),
            ),
        )(parts, cells, gx_parts, gy_parts, screen, pupil_amp, left, sine, cosine, full_table, pixels, *totals)
    parts = commands(signal)
    command_total = call(
        last_kernel,
        "total",
        shape((1, cases * block), f32),
        [pltpu.VMEM(total_shape.shape, f32)],
    )(parts, *totals)
    return (command_total, frame[None])


def solution(mesh):
    return jax.shard_map(
        body,
        mesh=mesh,
        in_specs=(P("case", None, None), P(), P("mod"), P("mod"), P("case", "mod"), P(), P(), P()),
        out_specs=(P("case", None), P("case", "mod", None)),
        check_vma=False,
    )
```

```python
import math

import jax
import jax.numpy as jnp
import numpy as np
from jax import lax
from jax.experimental import pallas as pl
from jax.experimental.pallas import tpu as pltpu
from jax.sharding import PartitionSpec as P

STEPS = 2


loop_gain = 0.5
radius_pixels = 6.0
point_count = 256
LANES = 128
VMEM_LIMIT = 16 * 1024 * 1024


def rounded_table(angle, length, sign):
    scale = 1.0 / math.sqrt(length)
    real = (np.cos(angle) * scale).astype(np.float32).astype(jnp.bfloat16).astype(np.float64)
    imag = (sign * np.sin(angle) * scale).astype(np.float32).astype(jnp.bfloat16).astype(np.float64)
    return real + 1j * imag


def pyramid_table(pupil_size, length):
    centred = np.arange(length) - length // 2
    forward = np.mod(centred[:, None] * np.arange(pupil_size)[None, :], length) * (2.0 * math.pi / length)
    inverse = np.mod(np.arange(length)[:, None] * centred[None, :], length) * (2.0 * math.pi / length)
    mask = np.array([1, 1j, -1, -1j])[np.abs(centred) % 4]
    return rounded_table(inverse, length, 1.0) @ (mask[:, None] * rounded_table(forward, length, -1.0))


def sin_cos(angle):
    turns = jnp.floor(angle * (2.0 / math.pi) + 0.5)
    rest = angle - turns * 1.5703125
    rest = rest - turns * 4.837512969970703125e-4
    rest = rest - turns * 7.54978995489188216e-8
    square = rest * rest
    sine = rest + rest * square * (-1.6666654611e-1 + square * (8.3321608736e-3 - square * 1.9515295891e-4))
    cosine = (
        1.0
        - 0.5 * square
        + square * square * (4.166664568298827e-2 + square * (-1.388731625493765e-3 + square * 2.443315711809948e-5))
    )
    quarter = turns.astype(jnp.int32)
    swap = (quarter & 1) == 1
    sin_out = jnp.where(swap, cosine, sine)
    cos_out = jnp.where(swap, sine, cosine)
    sin_out = jnp.where((quarter & 2) == 2, -sin_out, sin_out)
    cos_out = jnp.where(((quarter + 1) & 2) == 2, -cos_out, cos_out)
    return sin_out, cos_out


def field_matrix(real, imag):
    return jnp.concatenate([jnp.concatenate([real, imag], 1), jnp.concatenate([-imag, real], 1)], 0)


def halves(values):
    high = values.astype(jnp.bfloat16)
    low = (values - high.astype(jnp.float32)).astype(jnp.bfloat16)
    return high, low


def look_up(count, row, index):
    high = index >> 7
    low = index & (LANES - 1)
    sums = [jnp.zeros(index.shape, jnp.float32) for _ in range(4)]
    for i in range(count):
        spread = jnp.broadcast_to(row(i), index.shape)
        picked = jnp.take_along_axis(spread, low, axis=1, mode="promise_in_bounds")
        sums[i % 4] = jnp.where(high == i, picked, sums[i % 4])
    return (sums[0] + sums[1]) + (sums[2] + sums[3])


def runs(ref):
    per_row = ref.shape[1] // LANES

    def row(i):
        column = (i % per_row) * LANES
        return ref[i // per_row : i // per_row + 1, column : column + LANES]

    return ref.shape[0] * per_row, row


def copies(pairs, semaphores):
    started = [pltpu.make_async_copy(*pair, semaphores.at[i]) for i, pair in enumerate(pairs)]
    for copy in started:
        copy.start()
    return started


def spread_kernel(point_ref, angles_ref):
    angle = point_ref[0].astype(jnp.float32) * (2.0 * math.pi / point_count)
    angles_ref[...] = jnp.full(angles_ref.shape, angle, jnp.float32)


def prepare_kernel(
    phase_hbm, amp_hbm, map_hbm, gxt_hbm, gyt_hbm, field_ref, cells_hbm, gx_hbm, gy_hbm,
    phase_ref, amp_ref, map_ref, gxt_ref, gyt_ref, floats, cells_ref, gx_ref, gy_ref, semaphores,
):
    phase, amp, actuators, gxt, gyt = copies(
        [(phase_hbm, phase_ref), (amp_hbm, amp_ref), (map_hbm, map_ref), (gxt_hbm, gxt_ref), (gyt_hbm, gyt_ref)],
        semaphores,
    )
    actuators.wait()
    floats[...] = map_ref[...].astype(jnp.float32)
    grid_rows, grid_columns = gxt_ref.shape[0], gyt_ref.shape[0]
    cell = lax.broadcasted_iota(jnp.int32, cells_ref.shape, 0) * grid_columns
    column = lax.broadcasted_iota(jnp.int32, cells_ref.shape, 1)
    cell = jnp.where(column < grid_columns, cell + column, 0)
    cells_ref[...] = look_up(*runs(floats), cell).astype(jnp.int32)
    gxt.wait()
    high, low = halves(gxt_ref[...].T)
    gx_ref[...] = jnp.concatenate([high, low, high], 1)
    gyt.wait()
    padded = jnp.concatenate(
        [gyt_ref[...], jnp.zeros((LANES - grid_columns, gyt_ref.shape[1]), jnp.float32)], 0
    )
    high, low = halves(padded)
    gy_ref[...] = jnp.concatenate([high, high, low], 0)
    phase.wait()
    amp.wait()
    out = copies([(cells_ref, cells_hbm), (gx_ref, gx_hbm), (gy_ref, gy_hbm)], semaphores)
    sine, cosine = sin_cos(phase_ref[...])
    amplitude = amp_ref[...]
    field_ref[...] = jnp.concatenate([amplitude * cosine, amplitude * sine], 1).astype(jnp.bfloat16)
    for copy in out:
        copy.wait()


def tilt_factors(angles_ref, pupil, length):
    sin_a, cos_a = sin_cos(angles_ref[...])
    spread = pupil // LANES
    sin_a = jnp.concatenate([sin_a] * spread, 1)
    cos_a = jnp.concatenate([cos_a] * spread, 1)
    place = (lax.broadcasted_iota(jnp.int32, sin_a.shape, 1) - pupil // 2).astype(jnp.float32)
    place = place * (2.0 * math.pi * radius_pixels / length)
    return sin_cos(place * cos_a), sin_cos(place * sin_a)


def turned(real, imag, sine, cosine):
    sine, cosine = sine[:, None, :], cosine[:, None, :]
    return jnp.concatenate([real * cosine - imag * sine, real * sine + imag * cosine], 2)


def first_half(left, field, sine, cosine):
    count, pupil = sine.shape
    half = jnp.dot(left, field, preferred_element_type=jnp.float32)
    half = half.reshape(count, left.shape[0] // count, 2 * pupil)
    half = turned(half[:, :, :pupil], half[:, :, pupil:], sine, cosine)
    return half.reshape(left.shape).astype(jnp.bfloat16)


def second_half(half, full_table, count):
    length = full_table.shape[1] // 2
    detector = jnp.dot(half, full_table, preferred_element_type=jnp.float32)
    real, imag = detector[:, :length], detector[:, length:]
    intensity = (real * real + imag * imag).reshape(count, half.shape[0] // count, length)
    return jnp.sum(intensity, 0) * (1.0 / count)


def read_signals(frame_ref, pixels):
    return look_up(*runs(frame_ref), pixels).astype(jnp.bfloat16).astype(jnp.float32)


def own_pixels(pixels_ref, row_count, length):
    return pixels_ref[...] - lax.axis_index("mod") * (row_count * length)


def first_kernel(
    angles_ref, field_ref, rows_hbm, full_hbm, pixels_hbm, signal_ref, left_hbm, tilt_ref,
    rows_ref, full_ref, pixels_ref, left_ref, frame_ref, semaphores,
):
    row_count, length = frame_ref.shape
    count, pupil = angles_ref.shape[0], length // 2
    own_rows = pl.ds(pl.multiple_of(lax.axis_index("mod") * row_count, row_count), row_count)
    rows, full, pixels = copies(
        [(rows_hbm.at[own_rows], rows_ref), (full_hbm, full_ref), (pixels_hbm, pixels_ref)], semaphores
    )
    (s1, c1), (s2, c2) = tilt_factors(angles_ref, pupil, length)
    tilt_ref[:count] = s2
    tilt_ref[count:] = c2
    rows.wait()
    own = rows_ref[...]
    left = turned(own[None, :, :pupil], own[None, :, pupil:], s1, c1)
    left = left.reshape(left_ref.shape).astype(jnp.bfloat16)
    left_ref[...] = left
    left_out = pltpu.make_async_copy(left_ref, left_hbm, semaphores.at[0])
    left_out.start()
    field = field_matrix(field_ref[:, :pupil], field_ref[:, pupil:])
    half = first_half(left, field, s2, c2)
    full.wait()
    frame_ref[...] = second_half(half, full_ref[...], count)
    pixels.wait()
    signal_ref[...] = read_signals(frame_ref, own_pixels(pixels_ref, row_count, length))
    left_out.wait()


def add_commands(parts_ref, total_ref, out_ref):
    cases = out_ref.shape[0]
    each = parts_ref.shape[0] // cases
    for case in range(cases):
        sums = jnp.sum(parts_ref[case * each : (case + 1) * each].astype(jnp.float32), 0)
        out_ref[case] = loop_gain * sums if total_ref is None else total_ref[case] + loop_gain * sums


def later_kernel(
    parts_ref, tilt_ref, cells_hbm, gx_hbm, gy_hbm, phase_hbm, amp_hbm, left_hbm, full_hbm, pixels_hbm, *refs
):
    old_total, refs = (None, refs) if len(refs) == 13 else (refs[0], refs[1:])
    frame_hbm, signal_ref, new_total_ref, frame_ref = refs[:4]
    cells_ref, gx_ref, gy_ref, phase_ref, amp_ref, left_ref, full_ref, pixels_ref = refs[4:12]
    semaphores = refs[12]
    cells, gx, gy, phase, amp, left, full, pixels = copies(
        [
            (cells_hbm, cells_ref), (gx_hbm, gx_ref), (gy_hbm, gy_ref), (phase_hbm, phase_ref), (amp_hbm, amp_ref),
            (left_hbm, left_ref), (full_hbm, full_ref), (pixels_hbm, pixels_ref),
        ],
        semaphores,
    )
    row_count, length = frame_ref.shape
    count = tilt_ref.shape[0] // 2
    add_commands(parts_ref, old_total, new_total_ref)
    cases, pieces, width = new_total_ref.shape
    per_piece = width // LANES

    def row(i):
        column = (i % per_piece) * LANES
        piece = i // per_piece
        return new_total_ref[piece // pieces, piece % pieces : piece % pieces + 1, column : column + LANES]

    cells.wait()
    grid = look_up(cases * pieces * per_piece, row, cells_ref[...])
    high, low = halves(grid)
    gx.wait()
    rows_mapped = jnp.dot(
        gx_ref[...], jnp.concatenate([high, high, low], 0), preferred_element_type=jnp.float32
    )
    high, low = halves(rows_mapped)
    gy.wait()
    surface = jnp.dot(
        jnp.concatenate([high, low, high], 1), gy_ref[...], preferred_element_type=jnp.float32
    )
    phase.wait()
    sine, cosine = sin_cos(phase_ref[...] - surface)
    amp.wait()
    amplitude = amp_ref[...]
    field = field_matrix((amplitude * cosine).astype(jnp.bfloat16), (amplitude * sine).astype(jnp.bfloat16))
    left.wait()
    half = first_half(left_ref[...], field, tilt_ref[:count], tilt_ref[count:])
    full.wait()
    frame_ref[...] = second_half(half, full_ref[...], count)
    frame_out = pltpu.make_async_copy(frame_ref, frame_hbm, semaphores.at[0])
    frame_out.start()
    pixels.wait()
    signal_ref[...] = read_signals(frame_ref, own_pixels(pixels_ref, row_count, length))
    frame_out.wait()


def command_kernel(*refs):
    signal_refs, recon_ref, out_ref = refs[:-2], refs[-2], refs[-1]
    cases = len(signal_refs)
    own_case = lax.axis_index("case")
    received = [ref[...] for ref in signal_refs]
    ordered = []
    for case in range(cases):
        values = received[0]
        for j in range(1, cases):
            values = jnp.where((own_case ^ j) == case, received[j], values)
        ordered.append(values)
    groups = received[0].shape[0]
    signals = jnp.concatenate(
        [jnp.concatenate([values[g : g + 1] for values in ordered], 0) for g in range(groups)], 1
    ).astype(jnp.bfloat16)
    partial = lax.dot_general(
        signals, recon_ref[...], (((1,), (1,)), ((), ())), preferred_element_type=jnp.float32
    )
    messages, pieces, width = out_ref.shape
    copies = messages // cases
    for case in range(cases):
        message = jnp.concatenate(
            [partial[case : case + 1, i * width : (i + 1) * width] for i in range(pieces)], 0
        ).astype(jnp.bfloat16)
        for i in range(copies):
            out_ref[case * copies + i] = message


def last_kernel(parts_ref, total_ref, out_ref, sums_ref):
    add_commands(parts_ref, total_ref, sums_ref)
    cases, pieces, width = sums_ref.shape
    for case in range(cases):
        for i in range(pieces):
            start = (case * pieces + i) * width
            out_ref[:, start : start + width] = sums_ref[case, i : i + 1, :]


def body(turbulence, pupil_amp, mod_points, valid_pix, recon, gx, gy, act_map):
    pupil = pupil_amp.shape[0]
    length = 2 * pupil
    cases = lax.axis_size("case")
    devices_mod = lax.axis_size("mod")
    count = devices_mod * mod_points.shape[0]
    row_count = length // devices_mod
    block = recon.shape[0]
    pieces = 2
    signal_rows = valid_pix.shape[0] // LANES
    grid_rows = gx.shape[1]
    screen = turbulence[0]
    pixels = valid_pix.reshape(signal_rows, LANES)
    f32, bf16 = jnp.float32, jnp.bfloat16
    shape = jax.ShapeDtypeStruct
    hbm = pl.BlockSpec(memory_space=pltpu.HBM)
    vmem = pl.BlockSpec(memory_space=pltpu.VMEM)
    smem = pl.BlockSpec(memory_space=pltpu.SMEM)

    def call(kernel, name, outs, out_specs, in_specs, scratch, *operands):
        operands = [
            pltpu.with_memory_space_constraint(operand, pltpu.HBM) if spec is hbm else operand
            for operand, spec in zip(operands, in_specs)
        ]
        if isinstance(outs, tuple):
            outs = tuple(
                pltpu.HBM(out.shape, out.dtype) if spec is hbm else out for out, spec in zip(outs, out_specs)
            )
        return pl.pallas_call(
            kernel,
            out_shape=outs,
            in_specs=in_specs,
            out_specs=out_specs,
            scratch_shapes=scratch,
            compiler_params=pltpu.CompilerParams(vmem_limit_bytes=VMEM_LIMIT),
            name=name,
        )(*operands)

    def like(*arrays):
        return [pltpu.VMEM(array.shape, array.dtype) for array in arrays]

    def done(count):
        return pltpu.SemaphoreType.DMA((count,))

    table = pyramid_table(pupil, length)
    rows_table = jnp.asarray(np.concatenate([table.real, table.imag], 1).astype(np.float32))
    full_table = jnp.asarray(
        np.concatenate(
            [
                np.concatenate([table.real.T, table.imag.T], 1),
                np.concatenate([-table.imag.T, table.real.T], 1),
            ],
            0,
        ).astype(jnp.bfloat16)
    )

    with jax.named_scope("modulation_angles"):
        angles = call(
            spread_kernel, "spread", shape((devices_mod, 1, LANES), f32), vmem, [smem], [], mod_points
        )
        angles = lax.all_to_all(angles, "mod", 0, 0, tiled=True).reshape(count, LANES)

    field, cells, gx_parts, gy_parts = call(
        prepare_kernel,
        "prepare",
        (
            shape((pupil, 2 * pupil), bf16),
            shape((grid_rows, LANES), jnp.int32),
            shape((pupil, 3 * grid_rows), bf16),
            shape((3 * LANES, pupil), bf16),
        ),
        (vmem, hbm, hbm, hbm),
        [hbm] * 5,
        like(screen, pupil_amp)
        + [
            pltpu.VMEM((act_map.shape[0] // LANES, LANES), jnp.int32),
            pltpu.VMEM(gx.shape[::-1], f32),
            pltpu.VMEM(gy.shape[::-1], f32),
            pltpu.VMEM((act_map.shape[0] // LANES, LANES), f32),
            pltpu.VMEM((grid_rows, LANES), jnp.int32),
            pltpu.VMEM((pupil, 3 * grid_rows), bf16),
            pltpu.VMEM((3 * LANES, pupil), bf16),
            done(5),
        ],
        screen, pupil_amp, act_map.reshape(-1, LANES), gx.T, gy.T,
    )

    def commands(signal):
        signals = [signal]
        for j in range(1, cases):
            signals.append(lax.ppermute(signal, "case", [(i, i ^ j) for i in range(cases)]))
        partial = call(
            command_kernel, "commands", shape((cases * devices_mod, pieces, block // pieces), bf16), vmem,
            [vmem] * (cases + 1), [], *signals, recon,
        )
        return lax.all_to_all(partial, ("case", "mod"), 0, 0, tiled=True)

    frame_shape = shape((row_count, length), f32)
    signal_shape = shape((signal_rows, LANES), f32)
    left_shape = shape((count * row_count, 2 * pupil), bf16)
    total_shape = shape((cases, pieces, block // pieces), f32)
    signal, left, tilt = call(
        first_kernel,
        "first_frame",
        (signal_shape, left_shape, shape((2 * count, pupil), f32)),
        (vmem, hbm, vmem),
        [vmem, vmem, hbm, hbm, hbm],
        [pltpu.VMEM((row_count, 2 * pupil), f32)] + like(full_table, pixels, left_shape, frame_shape) + [done(3)],
        angles, field, rows_table, full_table, pixels,
    )
    totals = ()
    for iteration in range(1, STEPS):
        parts = commands(signal)
        held = (cells, gx_parts, gy_parts, screen, pupil_amp, left, full_table, pixels)
        frame, signal, *totals = call(
            later_kernel,
            "next_frame",
            (frame_shape, signal_shape, total_shape),
            (hbm, vmem, vmem),
            [vmem, vmem] + [hbm] * len(held) + [vmem] * len(totals),
            like(frame_shape, *held) + [done(len(held))],
            parts, tilt, *held, *totals,
        )
    parts = commands(signal)
    command_total = call(
        last_kernel, "total", shape((1, cases * block), f32), vmem, [vmem, vmem], like(total_shape), parts, *totals
    )
    return (command_total, frame[None])


def solution(mesh):
    return jax.shard_map(
        body,
        mesh=mesh,
        in_specs=(P("case", None, None), P(), P("mod"), P("mod"), P("case", "mod"), P(), P(), P()),
        out_specs=(P("case", None), P("case", "mod", None)),
        check_vma=False,
    )
```

```python
import math

import jax
import jax.numpy as jnp
import numpy as np
from jax import lax
from jax.experimental import pallas as pl
from jax.experimental.pallas import tpu as pltpu
from jax.sharding import PartitionSpec as P

STEPS = 2


loop_gain = 0.5
radius_pixels = 6.0
point_count = 256
LANES = 128
VMEM_LIMIT = 16 * 1024 * 1024


def rounded_table(angle, length, sign):
    scale = 1.0 / math.sqrt(length)
    real = (np.cos(angle) * scale).astype(np.float32).astype(jnp.bfloat16).astype(np.float64)
    imag = (sign * np.sin(angle) * scale).astype(np.float32).astype(jnp.bfloat16).astype(np.float64)
    return real + 1j * imag


def pyramid_table(pupil_size, length):
    centred = np.arange(length) - length // 2
    forward = np.mod(centred[:, None] * np.arange(pupil_size)[None, :], length) * (2.0 * math.pi / length)
    inverse = np.mod(np.arange(length)[:, None] * centred[None, :], length) * (2.0 * math.pi / length)
    mask = np.array([1, 1j, -1, -1j])[np.abs(centred) % 4]
    return rounded_table(inverse, length, 1.0) @ (mask[:, None] * rounded_table(forward, length, -1.0))


def sin_cos(angle):
    turns = jnp.floor(angle * (2.0 / math.pi) + 0.5)
    rest = angle - turns * 1.5703125
    rest = rest - turns * 4.837512969970703125e-4
    rest = rest - turns * 7.54978995489188216e-8
    square = rest * rest
    sine = rest + rest * square * (-1.6666654611e-1 + square * (8.3321608736e-3 - square * 1.9515295891e-4))
    cosine = (
        1.0
        - 0.5 * square
        + square * square * (4.166664568298827e-2 + square * (-1.388731625493765e-3 + square * 2.443315711809948e-5))
    )
    quarter = turns.astype(jnp.int32)
    swap = (quarter & 1) == 1
    sin_out = jnp.where(swap, cosine, sine)
    cos_out = jnp.where(swap, sine, cosine)
    sin_out = jnp.where((quarter & 2) == 2, -sin_out, sin_out)
    cos_out = jnp.where(((quarter + 1) & 2) == 2, -cos_out, cos_out)
    return sin_out, cos_out


def field_matrix(real, imag):
    return jnp.concatenate([jnp.concatenate([real, imag], 1), jnp.concatenate([-imag, real], 1)], 0)


def halves(values):
    high = values.astype(jnp.bfloat16)
    low = (values - high.astype(jnp.float32)).astype(jnp.bfloat16)
    return high, low


def look_up(count, row, index):
    high = index >> 7
    low = index & (LANES - 1)
    sums = [jnp.zeros(index.shape, jnp.float32) for _ in range(4)]
    for i in range(count):
        spread = jnp.broadcast_to(row(i), index.shape)
        picked = jnp.take_along_axis(spread, low, axis=1, mode="promise_in_bounds")
        sums[i % 4] = jnp.where(high == i, picked, sums[i % 4])
    return (sums[0] + sums[1]) + (sums[2] + sums[3])


def runs(ref):
    per_row = ref.shape[1] // LANES

    def row(i):
        column = (i % per_row) * LANES
        return ref[i // per_row : i // per_row + 1, column : column + LANES]

    return ref.shape[0] * per_row, row


def copies(pairs, semaphores):
    started = [pltpu.make_async_copy(*pair, semaphores.at[i]) for i, pair in enumerate(pairs)]
    for copy in started:
        copy.start()
    return started


def spread_kernel(point_ref, angles_ref):
    angle = point_ref[0].astype(jnp.float32) * (2.0 * math.pi / point_count)
    angles_ref[...] = jnp.full(angles_ref.shape, angle, jnp.float32)


def prepare_kernel(
    phase_hbm, amp_hbm, map_hbm, gxt_hbm, gyt_hbm, rows_hbm, full_hbm,
    field_ref, rows_ref, full_ref, cells_ref, gx_ref, gy_ref,
    phase_ref, amp_ref, map_ref, gxt_ref, gyt_ref, floats, semaphores,
):
    row_count = rows_ref.shape[0]
    own_rows = pl.ds(pl.multiple_of(lax.axis_index("mod") * row_count, row_count), row_count)
    actuators, gxt, gyt, phase, amp, rows, full = copies(
        [
            (map_hbm, map_ref), (gxt_hbm, gxt_ref), (gyt_hbm, gyt_ref), (phase_hbm, phase_ref), (amp_hbm, amp_ref),
            (rows_hbm.at[own_rows], rows_ref), (full_hbm, full_ref),
        ],
        semaphores,
    )
    actuators.wait()
    floats[...] = map_ref[...].astype(jnp.float32)
    grid_rows, grid_columns = gxt_ref.shape[0], gyt_ref.shape[0]
    cell = lax.broadcasted_iota(jnp.int32, cells_ref.shape, 0) * grid_columns
    column = lax.broadcasted_iota(jnp.int32, cells_ref.shape, 1)
    cell = jnp.where(column < grid_columns, cell + column, 0)
    cells_ref[...] = look_up(*runs(floats), cell).astype(jnp.int32)
    gxt.wait()
    high, low = halves(gxt_ref[...].T)
    gx_ref[...] = jnp.concatenate([high, low], 1)
    gyt.wait()
    high, low = halves(gyt_ref[...])
    gy_ref[...] = jnp.concatenate([high, high, low], 0)
    phase.wait()
    sine, cosine = sin_cos(phase_ref[...])
    amp.wait()
    amplitude = amp_ref[...]
    field_ref[...] = jnp.concatenate([amplitude * cosine, amplitude * sine], 1).astype(jnp.bfloat16)
    rows.wait()
    full.wait()


def tilt_factors(angles_ref, pupil, length):
    sin_a, cos_a = sin_cos(angles_ref[...])
    spread = pupil // LANES
    sin_a = jnp.concatenate([sin_a] * spread, 1)
    cos_a = jnp.concatenate([cos_a] * spread, 1)
    place = (lax.broadcasted_iota(jnp.int32, sin_a.shape, 1) - pupil // 2).astype(jnp.float32)
    place = place * (2.0 * math.pi * radius_pixels / length)
    return sin_cos(place * cos_a), sin_cos(place * sin_a)


def turned(real, imag, sine, cosine):
    sine, cosine = sine[:, None, :], cosine[:, None, :]
    return jnp.concatenate([real * cosine - imag * sine, real * sine + imag * cosine], 2)


def first_half(left, field, sine, cosine):
    count, pupil = sine.shape
    half = jnp.dot(left, field, preferred_element_type=jnp.float32)
    half = half.reshape(count, left.shape[0] // count, 2 * pupil)
    half = turned(half[:, :, :pupil], half[:, :, pupil:], sine, cosine)
    return half.reshape(left.shape).astype(jnp.bfloat16)


def second_half(half, full_table, count):
    length = full_table.shape[1] // 2
    detector = jnp.dot(half, full_table, preferred_element_type=jnp.float32)
    real, imag = detector[:, :length], detector[:, length:]
    intensity = (real * real + imag * imag).reshape(count, half.shape[0] // count, length)
    return jnp.sum(intensity, 0) * (1.0 / count)


def read_signals(frame_ref, pixels):
    return look_up(*runs(frame_ref), pixels).astype(jnp.bfloat16).astype(jnp.float32)


def own_pixels(pixels_ref, row_count, length):
    return pixels_ref[...] - lax.axis_index("mod") * (row_count * length)


def first_kernel(
    angles_ref, field_ref, rows_ref, full_ref, pixels_hbm, recon_hbm, signal_ref, left_hbm, tilt_ref, recon_ref,
    pixels_ref, left_ref, frame_ref, semaphores,
):
    row_count, length = frame_ref.shape
    count, pupil = angles_ref.shape[0], length // 2
    pixels, recon = copies([(pixels_hbm, pixels_ref), (recon_hbm, recon_ref)], semaphores)
    (s1, c1), (s2, c2) = tilt_factors(angles_ref, pupil, length)
    tilt_ref[:count] = s2
    tilt_ref[count:] = c2
    own = rows_ref[...]
    left = turned(own[None, :, :pupil], own[None, :, pupil:], s1, c1)
    left = left.reshape(left_ref.shape).astype(jnp.bfloat16)
    left_ref[...] = left
    left_out = pltpu.make_async_copy(left_ref, left_hbm, semaphores.at[2])
    left_out.start()
    field = field_matrix(field_ref[:, :pupil], field_ref[:, pupil:])
    half = first_half(left, field, s2, c2)
    frame_ref[...] = second_half(half, full_ref[...], count)
    pixels.wait()
    signal_ref[...] = read_signals(frame_ref, own_pixels(pixels_ref, row_count, length))
    left_out.wait()
    recon.wait()


def add_commands(parts_ref, total_ref, out_ref):
    cases = out_ref.shape[0]
    each = parts_ref.shape[0] // cases
    for case in range(cases):
        sums = jnp.sum(parts_ref[case * each : (case + 1) * each].astype(jnp.float32), 0)
        out_ref[case] = loop_gain * sums if total_ref is None else total_ref[case] + loop_gain * sums


def later_kernel(
    parts_ref, tilt_ref, cells_ref, gx_ref, gy_ref, phase_hbm, amp_hbm, left_hbm, full_hbm, pixels_hbm, *refs
):
    old_total, refs = (None, refs) if len(refs) == 10 else (refs[0], refs[1:])
    frame_hbm, signal_ref, new_total_ref, frame_ref = refs[:4]
    phase_ref, amp_ref, left_ref, full_ref, pixels_ref, semaphores = refs[4:]
    phase, amp, left, full, pixels = copies(
        [
            (phase_hbm, phase_ref), (amp_hbm, amp_ref), (left_hbm, left_ref), (full_hbm, full_ref),
            (pixels_hbm, pixels_ref),
        ],
        semaphores,
    )
    row_count, length = frame_ref.shape
    count = tilt_ref.shape[0] // 2
    add_commands(parts_ref, old_total, new_total_ref)
    cases, pieces, width = new_total_ref.shape
    per_piece = width // LANES

    def row(i):
        column = (i % per_piece) * LANES
        piece = i // per_piece
        return new_total_ref[piece // pieces, piece % pieces : piece % pieces + 1, column : column + LANES]

    grid = look_up(cases * pieces * per_piece, row, cells_ref[...])
    high, low = halves(grid)
    grid_rows = grid.shape[0]
    gx_high, gx_low = gx_ref[:, :grid_rows], gx_ref[:, grid_rows:]
    rows_mapped = jnp.dot(
        jnp.concatenate([gx_high, gx_low, gx_high], 1),
        jnp.concatenate([high, high, low], 0),
        preferred_element_type=jnp.float32,
    )
    high, low = halves(rows_mapped[:, : gy_ref.shape[0] // 3])
    surface = jnp.dot(
        jnp.concatenate([high, low, high], 1), gy_ref[...], preferred_element_type=jnp.float32
    )
    phase.wait()
    sine, cosine = sin_cos(phase_ref[...] - surface)
    amp.wait()
    amplitude = amp_ref[...]
    field = field_matrix((amplitude * cosine).astype(jnp.bfloat16), (amplitude * sine).astype(jnp.bfloat16))
    left.wait()
    half = first_half(left_ref[...], field, tilt_ref[:count], tilt_ref[count:])
    full.wait()
    frame_ref[...] = second_half(half, full_ref[...], count)
    frame_out = pltpu.make_async_copy(frame_ref, frame_hbm, semaphores.at[0])
    frame_out.start()
    pixels.wait()
    signal_ref[...] = read_signals(frame_ref, own_pixels(pixels_ref, row_count, length))
    frame_out.wait()


def command_kernel(*refs):
    signal_refs, recon_ref, out_ref = refs[:-2], refs[-2], refs[-1]
    cases = len(signal_refs)
    own_case = lax.axis_index("case")
    received = [ref[...] for ref in signal_refs]
    ordered = []
    for case in range(cases):
        values = received[0]
        for j in range(1, cases):
            values = jnp.where((own_case ^ j) == case, received[j], values)
        ordered.append(values)
    groups = received[0].shape[0]
    signals = jnp.concatenate(
        [jnp.concatenate([values[g : g + 1] for values in ordered], 0) for g in range(groups)], 1
    ).astype(jnp.bfloat16)
    partial = lax.dot_general(
        signals, recon_ref[...], (((1,), (1,)), ((), ())), preferred_element_type=jnp.float32
    )
    messages, pieces, width = out_ref.shape
    copies = messages // cases
    for case in range(cases):
        message = jnp.concatenate(
            [partial[case : case + 1, i * width : (i + 1) * width] for i in range(pieces)], 0
        ).astype(jnp.bfloat16)
        for i in range(copies):
            out_ref[case * copies + i] = message


def last_kernel(parts_ref, total_ref, out_ref, sums_ref):
    add_commands(parts_ref, total_ref, sums_ref)
    cases, pieces, width = sums_ref.shape
    for case in range(cases):
        for i in range(pieces):
            start = (case * pieces + i) * width
            out_ref[:, start : start + width] = sums_ref[case, i : i + 1, :]


def body(turbulence, pupil_amp, mod_points, valid_pix, recon, gx, gy, act_map):
    pupil = pupil_amp.shape[0]
    length = 2 * pupil
    cases = lax.axis_size("case")
    devices_mod = lax.axis_size("mod")
    count = devices_mod * mod_points.shape[0]
    row_count = length // devices_mod
    block = recon.shape[0]
    pieces = 2
    signal_rows = valid_pix.shape[0] // LANES
    grid_rows = gx.shape[1]
    screen = turbulence[0]
    pixels = valid_pix.reshape(signal_rows, LANES)
    f32, bf16 = jnp.float32, jnp.bfloat16
    shape = jax.ShapeDtypeStruct
    hbm = pl.BlockSpec(memory_space=pltpu.HBM)
    vmem = pl.BlockSpec(memory_space=pltpu.VMEM)
    smem = pl.BlockSpec(memory_space=pltpu.SMEM)

    def call(kernel, name, outs, out_specs, in_specs, scratch, *operands):
        operands = [
            pltpu.with_memory_space_constraint(operand, pltpu.HBM) if spec is hbm else operand
            for operand, spec in zip(operands, in_specs)
        ]
        if isinstance(outs, tuple):
            outs = tuple(
                pltpu.HBM(out.shape, out.dtype) if spec is hbm else out for out, spec in zip(outs, out_specs)
            )
        return pl.pallas_call(
            kernel,
            out_shape=outs,
            in_specs=in_specs,
            out_specs=out_specs,
            scratch_shapes=scratch,
            compiler_params=pltpu.CompilerParams(vmem_limit_bytes=VMEM_LIMIT),
            name=name,
        )(*operands)

    def like(*arrays):
        return [pltpu.VMEM(array.shape, array.dtype) for array in arrays]

    def done(count):
        return pltpu.SemaphoreType.DMA((count,))

    table = pyramid_table(pupil, length)
    rows_table = jnp.asarray(np.concatenate([table.real, table.imag], 1).astype(np.float32))
    full_table = jnp.asarray(
        np.concatenate(
            [
                np.concatenate([table.real.T, table.imag.T], 1),
                np.concatenate([-table.imag.T, table.real.T], 1),
            ],
            0,
        ).astype(jnp.bfloat16)
    )

    with jax.named_scope("modulation_angles"):
        angles = call(
            spread_kernel, "spread", shape((devices_mod, 1, LANES), f32), vmem, [smem], [], mod_points
        )
        angles = lax.all_to_all(angles, "mod", 0, 0, tiled=True).reshape(count, LANES)

    field, rows, full, cells, gx_parts, gy_parts = call(
        prepare_kernel,
        "prepare",
        (
            shape((pupil, 2 * pupil), bf16),
            shape((row_count, 2 * pupil), f32),
            shape(full_table.shape, bf16),
            shape((grid_rows, LANES), jnp.int32),
            shape((pupil, 2 * grid_rows), bf16),
            shape((3 * gy.shape[1], pupil), bf16),
        ),
        (vmem,) * 6,
        [hbm] * 7,
        like(screen, pupil_amp)
        + [
            pltpu.VMEM((act_map.shape[0] // LANES, LANES), jnp.int32),
            pltpu.VMEM(gx.shape[::-1], f32),
            pltpu.VMEM(gy.shape[::-1], f32),
            pltpu.VMEM((act_map.shape[0] // LANES, LANES), f32),
            done(7),
        ],
        screen, pupil_amp, act_map.reshape(-1, LANES), gx.T, gy.T, rows_table, full_table,
    )

    def commands(signal, recon):
        signals = [signal]
        for j in range(1, cases):
            signals.append(lax.ppermute(signal, "case", [(i, i ^ j) for i in range(cases)]))
        partial = call(
            command_kernel, "commands", shape((cases * devices_mod, pieces, block // pieces), bf16), vmem,
            [vmem] * (cases + 1), [], *signals, recon,
        )
        return lax.all_to_all(partial, ("case", "mod"), 0, 0, tiled=True)

    frame_shape = shape((row_count, length), f32)
    signal_shape = shape((signal_rows, LANES), f32)
    left_shape = shape((count * row_count, 2 * pupil), bf16)
    total_shape = shape((cases, pieces, block // pieces), f32)
    signal, left, tilt, recon = call(
        first_kernel,
        "first_frame",
        (signal_shape, left_shape, shape((2 * count, pupil), f32), shape(recon.shape, bf16)),
        (vmem, hbm, vmem, vmem),
        [vmem, vmem, vmem, vmem, hbm, hbm],
        like(pixels, left_shape, frame_shape) + [done(3)],
        angles, field, rows, full, pixels, recon,
    )
    totals = ()
    for iteration in range(1, STEPS):
        parts = commands(signal, recon)
        held = (screen, pupil_amp, left, full_table, pixels)
        frame, signal, *totals = call(
            later_kernel,
            "next_frame",
            (frame_shape, signal_shape, total_shape),
            (hbm, vmem, vmem),
            [vmem] * 5 + [hbm] * len(held) + [vmem] * len(totals),
            like(frame_shape, *held) + [done(len(held))],
            parts, tilt, cells, gx_parts, gy_parts, *held, *totals,
        )
    parts = commands(signal, recon)
    command_total = call(
        last_kernel, "total", shape((1, cases * block), f32), vmem, [vmem, vmem], like(total_shape), parts, *totals
    )
    return (command_total, frame[None])


def solution(mesh):
    return jax.shard_map(
        body,
        mesh=mesh,
        in_specs=(P("case", None, None), P(), P("mod"), P("mod"), P("case", "mod"), P(), P(), P()),
        out_specs=(P("case", None), P("case", "mod", None)),
        check_vma=False,
    )
```

```python
import functools
import math

import jax
import jax.numpy as jnp
import numpy as np
from jax import lax
from jax.experimental import pallas as pl
from jax.experimental.pallas import tpu as pltpu
from jax.sharding import PartitionSpec as P

STEPS = 2


loop_gain = 0.5
radius_pixels = 6.0
point_count = 256
LANES = 128
VMEM_LIMIT = 16 * 1024 * 1024


def rounded_table(angle, length, sign):
    scale = 1.0 / math.sqrt(length)
    real = (np.cos(angle) * scale).astype(np.float32).astype(jnp.bfloat16).astype(np.float64)
    imag = (sign * np.sin(angle) * scale).astype(np.float32).astype(jnp.bfloat16).astype(np.float64)
    return real + 1j * imag


def pyramid_table(pupil_size, length):
    centred = np.arange(length) - length // 2
    forward = np.mod(centred[:, None] * np.arange(pupil_size)[None, :], length) * (2.0 * math.pi / length)
    inverse = np.mod(np.arange(length)[:, None] * centred[None, :], length) * (2.0 * math.pi / length)
    mask = np.array([1, 1j, -1, -1j])[np.abs(centred) % 4]
    return rounded_table(inverse, length, 1.0) @ (mask[:, None] * rounded_table(forward, length, -1.0))


def half_angle(angle):
    turns = angle * (0.5 / math.pi)
    rest = turns - jnp.floor(turns + 0.5)
    square = rest * rest
    sine = rest * polynomial(square, (4.442867756, -7.307443618, 3.594788074, -0.784373999))
    cosine = polynomial(square, (1.414213538, -6.978850841, 5.739460945, -1.883563042, 0.310698181))
    return sine, cosine


def sin_cos(angle):
    sine, cosine = half_angle(angle)
    return sine * cosine, 1.0 - sine * sine


def field_parts(phase, amplitude):
    sine, cosine = half_angle(phase)
    lead = amplitude * sine
    return (amplitude - lead * sine).astype(jnp.bfloat16), (lead * cosine).astype(jnp.bfloat16)


def polynomial(x, coefficients):
    value = coefficients[-1]
    for coefficient in coefficients[-2::-1]:
        value = value * x + coefficient
    return value


def field_matrix(real, imag):
    return jnp.concatenate([jnp.concatenate([real, imag], 1), jnp.concatenate([-imag, real], 1)], 0)


def halves(values):
    high = values.astype(jnp.bfloat16)
    low = (values - high.astype(jnp.float32)).astype(jnp.bfloat16)
    return high, low


def look_up(count, row, index):
    blocks = []
    for start in range(0, index.shape[0], 8):
        block = index[start : start + 8]
        high = block >> 7
        low = block & (LANES - 1)
        sums = [jnp.zeros(block.shape, jnp.float32) for _ in range(2)]
        for i in range(count):
            spread = jnp.broadcast_to(row(i), block.shape)
            picked = jnp.take_along_axis(spread, low, axis=1, mode="promise_in_bounds")
            sums[i % 2] = jnp.where(high == i, picked, sums[i % 2])
        blocks.append(sums[0] + sums[1])
    return jnp.concatenate(blocks, 0) if len(blocks) > 1 else blocks[0]


def runs(ref):
    per_row = ref.shape[1] // LANES

    def row(i):
        column = (i % per_row) * LANES
        return ref[i // per_row : i // per_row + 1, column : column + LANES]

    return ref.shape[0] * per_row, row


def copies(pairs, semaphores):
    started = [pltpu.make_async_copy(*pair, semaphores.at[i]) for i, pair in enumerate(pairs)]
    for copy in started:
        copy.start()
    return started


def own_rows(rows_hbm, row_count):
    start = pl.multiple_of(lax.axis_index("mod") * row_count, row_count)
    return rows_hbm.at[pl.ds(start, row_count)]


def spread_kernel(point_ref, angles_ref):
    angle = point_ref[0].astype(jnp.float32) * (2.0 * math.pi / point_count)
    angles_ref[...] = jnp.full(angles_ref.shape, angle, jnp.float32)


def prepare_kernel(
    phase_hbm, amp_hbm, map_hbm, gxt_hbm, gyt_hbm, rows_hbm, full_hbm, recon_hbm,
    field_ref, rows_ref, full_ref, cells_ref, gx_ref, gy_ref, recon_ref,
    phase_ref, amp_ref, map_ref, gxt_ref, gyt_ref, floats, semaphores,
):
    actuators, gxt, gyt, phase, amp, rows, full, recon = copies(
        [
            (map_hbm, map_ref), (gxt_hbm, gxt_ref), (gyt_hbm, gyt_ref), (phase_hbm, phase_ref), (amp_hbm, amp_ref),
            (own_rows(rows_hbm, rows_ref.shape[0]), rows_ref), (full_hbm, full_ref),
            (recon_hbm.at[: recon_ref.shape[0]], recon_ref),
        ],
        semaphores,
    )
    grid_rows, grid_columns = gxt_ref.shape[0], gyt_ref.shape[0]
    packed = cells_ref.shape[0]
    actuators.wait()
    floats[...] = map_ref[...].astype(jnp.float32)
    lane = lax.broadcasted_iota(jnp.int32, cells_ref.shape, 1)
    cell = (lane % grid_rows) * grid_columns + (lane // grid_rows) * packed
    cell = cell + lax.broadcasted_iota(jnp.int32, cells_ref.shape, 0)
    cells_ref[...] = look_up(*runs(floats), cell).astype(jnp.int32)
    gxt.wait()
    high, low = halves(gxt_ref[...].T)
    gx_ref[...] = jnp.concatenate([high, low, high, jnp.zeros_like(high)], 1)
    gyt.wait()
    high, low = halves(gyt_ref[...].T)
    gy_ref[...] = jnp.concatenate([high, low, high], 1)
    phase.wait()
    amp.wait()
    field_ref[...] = jnp.concatenate(field_parts(phase_ref[...], amp_ref[...]), 1)
    rows.wait()
    full.wait()
    recon.wait()


def mirror_surface(grid, gx_ref, gy_ref):
    f32 = jnp.float32
    lanes_used = gx_ref.shape[1] // 4
    if lanes_used == LANES:
        spread = [grid]
    else:
        lane = lax.broadcasted_iota(jnp.int32, grid.shape, 1)
        other = pltpu.roll(grid, lanes_used, 1)
        spread = [jnp.where(lane < lanes_used, grid, other), jnp.where(lane < lanes_used, other, grid)]
    transposed = jnp.concatenate(spread, 0)
    high = transposed.astype(jnp.bfloat16).astype(f32)
    parts = jnp.concatenate([high, high, transposed - high], 0).astype(jnp.bfloat16)
    high, low = halves(jnp.dot(gy_ref[...], parts, preferred_element_type=f32))
    return lax.dot_general(
        gx_ref[...], jnp.concatenate([high, low], 1), (((1,), (1,)), ((), ())), preferred_element_type=f32
    )


def tilt_factors(angles_ref, pupil, length):
    sin_a, cos_a = sin_cos(angles_ref[...])
    spread = pupil // LANES
    sin_a = jnp.concatenate([sin_a] * spread, 1)
    cos_a = jnp.concatenate([cos_a] * spread, 1)
    place = (lax.broadcasted_iota(jnp.int32, sin_a.shape, 1) - pupil // 2).astype(jnp.float32)
    place = place * (2.0 * math.pi * radius_pixels / length)
    return sin_cos(place * cos_a) + sin_cos(place * sin_a)


def turned(real, imag, sine, cosine):
    sine, cosine = sine[:, None, :], cosine[:, None, :]
    return real * cosine - imag * sine, real * sine + imag * cosine


def left_rows(rows, sine, cosine):
    count, pupil = sine.shape
    left = jnp.concatenate(turned(rows[None, :, :pupil], rows[None, :, pupil:], sine, cosine), 2)
    return left.reshape(count * rows.shape[0], 2 * pupil).astype(jnp.bfloat16)


def half_way(left, field, sine, cosine):
    count, pupil = sine.shape
    rows = left.shape[0]
    half = jnp.dot(left, field, preferred_element_type=jnp.float32)
    half = half.reshape(count, rows // count, 2 * pupil)
    real, imag = turned(half[:, :, :pupil], half[:, :, pupil:], sine, cosine)
    real = real.reshape(rows, pupil).astype(jnp.bfloat16)
    imag = imag.reshape(rows, pupil).astype(jnp.bfloat16)
    return jnp.concatenate([jnp.concatenate([real, -imag], 1), jnp.concatenate([imag, real], 1)], 0)


def detector_part(both, table, count):
    detector = jnp.dot(both, table, preferred_element_type=jnp.float32)
    squares = (detector * detector).reshape(2 * count, both.shape[0] // (2 * count), detector.shape[1])
    return jnp.sum(squares, 0) * (1.0 / count)


def detect(both, full_ref, pixels_ref, frame_ref, count):
    row_count, length = frame_ref.shape
    pixels = pixels_ref[...] - lax.axis_index("mod") * (row_count * length)
    high, low = pixels >> 7, pixels & (LANES - 1)
    per_row = length // LANES
    total = jnp.zeros(pixels.shape, jnp.float32)
    step = length // 2
    for start in range(0, length, step):
        columns = pl.ds(start, step)
        frame_ref[:, columns] = detector_part(both, full_ref[:, columns], count)
        for i in range(row_count):
            for j in range(start // LANES, (start + step) // LANES):
                spread = jnp.broadcast_to(frame_ref[i : i + 1, j * LANES : (j + 1) * LANES], pixels.shape)
                picked = jnp.take_along_axis(spread, low, axis=1, mode="promise_in_bounds")
                total = jnp.where(high == i * per_row + j, picked, total)
    return total.astype(jnp.bfloat16).astype(jnp.float32)


def first_kernel(
    angles_ref, field_ref, rows_ref, full_ref, pixels_hbm, recon_hbm, signal_ref, tilt_ref, left_ref, recon_ref,
    pixels_ref, frame_ref, semaphores,
):
    length = frame_ref.shape[1]
    pupil = length // 2
    pixels, recon = copies(
        [(pixels_hbm, pixels_ref), (recon_hbm.at[recon_hbm.shape[0] - recon_ref.shape[0] :], recon_ref)], semaphores
    )
    tilts = tilt_factors(angles_ref, pupil, length)
    tilt_ref[0], tilt_ref[1] = tilts[2:]
    left = left_rows(rows_ref[...], *tilts[:2])
    left_ref[...] = left
    field = field_matrix(field_ref[:, :pupil], field_ref[:, pupil:])
    both = half_way(left, field, *tilts[2:])
    pixels.wait()
    signal_ref[...] = detect(both, full_ref, pixels_ref, frame_ref, angles_ref.shape[0])
    recon.wait()


def add_commands(parts_ref, total_ref, out_ref):
    cases = out_ref.shape[0]
    each = parts_ref.shape[0] // cases
    for case in range(cases):
        sums = jnp.sum(parts_ref[case * each : (case + 1) * each].astype(jnp.float32), 0)
        out_ref[case] = loop_gain * sums if total_ref is None else total_ref[case] + loop_gain * sums


def later_kernel(
    parts_ref, tilt_ref, cells_ref, gx_ref, gy_ref, left_ref, full_ref, phase_hbm, amp_hbm, pixels_hbm, recon_hbm,
    *refs
):
    old_total, refs = (None, refs) if len(refs) == 8 else (refs[0], refs[1:])
    frame_ref, signal_ref, new_total_ref, recon_ref, phase_ref, amp_ref, pixels_ref, semaphores = refs
    phase, amp, pixels, recon = copies(
        [
            (phase_hbm, phase_ref), (amp_hbm, amp_ref), (pixels_hbm, pixels_ref),
            (recon_hbm.at[recon_hbm.shape[0] - recon_ref.shape[0] :], recon_ref),
        ],
        semaphores,
    )
    add_commands(parts_ref, old_total, new_total_ref)
    cases, pieces, width = new_total_ref.shape
    per_piece = width // LANES

    def row(i):
        column = (i % per_piece) * LANES
        piece = i // per_piece
        return new_total_ref[piece // pieces, piece % pieces : piece % pieces + 1, column : column + LANES]

    grid = look_up(cases * pieces * per_piece, row, cells_ref[...])
    surface = mirror_surface(grid, gx_ref, gy_ref)
    phase.wait()
    amp.wait()
    field = field_matrix(*field_parts(phase_ref[...] - surface, amp_ref[...]))

    both = half_way(left_ref[...], field, tilt_ref[0], tilt_ref[1])
    pixels.wait()
    signal_ref[...] = detect(both, full_ref, pixels_ref, frame_ref, tilt_ref.shape[1])
    recon.wait()


def command_kernel(cases, *refs):
    signal_refs, recon_refs, refs = refs[:cases], refs[cases : cases + 2], refs[cases + 2 :]
    out_ref = refs[0] if len(refs) == 1 else refs[1]
    frame_out = None if len(refs) == 1 else copies([(refs[0], refs[2])], refs[3])[0]
    own_case = lax.axis_index("case")
    received = [ref[...] for ref in signal_refs]
    ordered = []
    for case in range(cases):
        values = received[0]
        for j in range(1, cases):
            values = jnp.where((own_case ^ j) == case, received[j], values)
        ordered.append(values)
    groups = received[0].shape[0]
    signals = jnp.concatenate(
        [jnp.concatenate([values[g : g + 1] for values in ordered], 0) for g in range(groups)], 1
    ).astype(jnp.bfloat16)
    partial = jnp.concatenate(
        [
            lax.dot_general(signals, ref[...], (((1,), (1,)), ((), ())), preferred_element_type=jnp.float32)
            for ref in recon_refs
        ],
        1,
    )
    messages, pieces, width = out_ref.shape
    copies_each = messages // cases
    for case in range(cases):
        message = jnp.concatenate(
            [partial[case : case + 1, i * width : (i + 1) * width] for i in range(pieces)], 0
        ).astype(jnp.bfloat16)
        for i in range(copies_each):
            out_ref[case * copies_each + i] = message
    if frame_out is not None:
        frame_out.wait()


def last_kernel(parts_ref, total_ref, out_ref, sums_ref):
    add_commands(parts_ref, total_ref, sums_ref)
    cases, pieces, width = sums_ref.shape
    for case in range(cases):
        for i in range(pieces):
            start = (case * pieces + i) * width
            out_ref[:, start : start + width] = sums_ref[case, i : i + 1, :]


def body(turbulence, pupil_amp, mod_points, valid_pix, recon, gx, gy, act_map):
    pupil = pupil_amp.shape[0]
    length = 2 * pupil
    cases = lax.axis_size("case")
    devices_mod = lax.axis_size("mod")
    count = devices_mod * mod_points.shape[0]
    row_count = length // devices_mod
    block = recon.shape[0]
    pieces = 2
    width = block // pieces
    signal_rows = valid_pix.shape[0] // LANES
    grid_rows, grid_columns = gx.shape[1], gy.shape[1]
    packed = grid_columns * grid_rows // LANES
    screen = turbulence[0]
    pixels = valid_pix.reshape(signal_rows, LANES)
    f32, bf16 = jnp.float32, jnp.bfloat16
    shape = jax.ShapeDtypeStruct
    hbm = pl.BlockSpec(memory_space=pltpu.HBM)
    vmem = pl.BlockSpec(memory_space=pltpu.VMEM)
    smem = pl.BlockSpec(memory_space=pltpu.SMEM)

    def call(kernel, name, outs, out_specs, in_specs, scratch, *operands):
        operands = [
            pltpu.with_memory_space_constraint(operand, pltpu.HBM) if spec is hbm else operand
            for operand, spec in zip(operands, in_specs)
        ]
        if isinstance(outs, tuple):
            outs = tuple(
                pltpu.HBM(out.shape, out.dtype) if spec is hbm else out for out, spec in zip(outs, out_specs)
            )
        return pl.pallas_call(
            kernel,
            out_shape=outs,
            in_specs=in_specs,
            out_specs=out_specs,
            scratch_shapes=scratch,
            compiler_params=pltpu.CompilerParams(vmem_limit_bytes=VMEM_LIMIT),
            name=name,
        )(*operands)

    def like(*arrays):
        return [pltpu.VMEM(array.shape, array.dtype) for array in arrays]

    def done(count):
        return pltpu.SemaphoreType.DMA((count,))

    table = pyramid_table(pupil, length)
    rows_table = jnp.asarray(np.concatenate([table.real, table.imag], 1).astype(np.float32))
    full_table = jnp.asarray(np.concatenate([table.real.T, table.imag.T], 0).astype(jnp.bfloat16))

    with jax.named_scope("modulation_angles"):
        angles = call(
            spread_kernel, "spread", shape((devices_mod, 1, LANES), f32), vmem, [smem], [], mod_points
        )
        angles = lax.all_to_all(angles, "mod", 0, 0, tiled=True).reshape(count, LANES)

    recon_early = block // LANES * 6 // 10 * LANES
    late_shape = shape((block - recon_early, recon.shape[1]), bf16)
    map_shape = (act_map.shape[0] // LANES, LANES)
    field, rows, full, cells, gx_parts, gy_parts, recon_first = call(
        prepare_kernel,
        "prepare",
        (
            shape((pupil, 2 * pupil), bf16),
            shape((row_count, 2 * pupil), f32),
            shape(full_table.shape, bf16),
            shape((packed, LANES), jnp.int32),
            shape((pupil, 4 * grid_rows), bf16),
            shape((pupil, 3 * grid_columns), bf16),
            shape((recon_early, recon.shape[1]), bf16),
        ),
        (vmem,) * 7,
        [hbm] * 8,
        like(screen, pupil_amp)
        + [
            pltpu.VMEM(map_shape, jnp.int32),
            pltpu.VMEM(gx.shape[::-1], f32),
            pltpu.VMEM(gy.shape[::-1], f32),
            pltpu.VMEM(map_shape, f32),
            done(8),
        ],
        screen, pupil_amp, act_map.reshape(map_shape), gx.T, gy.T, rows_table, full_table, recon,
    )

    def commands(signal, recon_late, frame=None):
        signals = [signal]
        for j in range(1, cases):
            signals.append(lax.ppermute(signal, "case", [(i, i ^ j) for i in range(cases)]))
        messages = shape((cases * devices_mod, pieces, width), bf16)
        kernel = functools.partial(command_kernel, cases)
        operands = (*signals, recon_first, recon_late)
        if frame is None:
            partial = call(kernel, "commands", messages, vmem, [vmem] * (cases + 2), [], *operands)
            return lax.all_to_all(partial, ("case", "mod"), 0, 0, tiled=True)
        partial, frame = call(
            kernel, "last_commands", (messages, frame), (vmem, hbm), [vmem] * (cases + 3), [done(1)], *operands, frame
        )
        return lax.all_to_all(partial, ("case", "mod"), 0, 0, tiled=True), frame

    frame_shape = shape((row_count, length), f32)
    signal_shape = shape((signal_rows, LANES), f32)
    total_shape = shape((cases, pieces, width), f32)
    left_shape = shape((count * row_count, 2 * pupil), bf16)
    signal, tilts, left, recon_late = call(
        first_kernel,
        "first_frame",
        (signal_shape, shape((2, count, pupil), f32), left_shape, late_shape),
        (vmem, vmem, vmem, vmem),
        [vmem, vmem, vmem, vmem, hbm, hbm],
        like(pixels, frame_shape) + [done(2)],
        angles, field, rows, full, pixels, recon,
    )
    totals = ()
    for iteration in range(1, STEPS):
        parts = commands(signal, recon_late)
        held = (screen, pupil_amp, pixels)
        frame, signal, *totals, recon_late = call(
            later_kernel,
            "next_frame",
            (frame_shape, signal_shape, total_shape, late_shape),
            (vmem, vmem, vmem, vmem),
            [vmem] * 7 + [hbm] * 4 + [vmem] * len(totals),
            like(*held) + [done(4)],
            parts, tilts, cells, gx_parts, gy_parts, left, full, *held, recon, *totals,
        )
    parts, frame = commands(signal, recon_late, frame)
    command_total = call(
        last_kernel, "total", shape((1, cases * block), f32), vmem, [vmem, vmem], like(total_shape), parts, *totals
    )
    return (command_total, frame[None])


def solution(mesh):
    return jax.shard_map(
        body,
        mesh=mesh,
        in_specs=(P("case", None, None), P(), P("mod"), P("mod"), P("case", "mod"), P(), P(), P()),
        out_specs=(P("case", None), P("case", "mod", None)),
        check_vma=False,
    )
```

```python
import math

import jax
import jax.numpy as jnp
import numpy as np
from jax import lax
from jax.experimental import pallas as pl
from jax.experimental.pallas import tpu as pltpu
from jax.sharding import PartitionSpec as P

STEPS = 2


loop_gain = 0.5
radius_pixels = 6.0
point_count = 256
LANES = 128
VMEM_LIMIT = 16 * 1024 * 1024


def rounded_table(angle, length, sign):
    scale = 1.0 / math.sqrt(length)
    real = (np.cos(angle) * scale).astype(np.float32).astype(jnp.bfloat16).astype(np.float64)
    imag = (sign * np.sin(angle) * scale).astype(np.float32).astype(jnp.bfloat16).astype(np.float64)
    return real + 1j * imag


def pyramid_table(pupil_size, length):
    centred = np.arange(length) - length // 2
    forward = np.mod(centred[:, None] * np.arange(pupil_size)[None, :], length) * (2.0 * math.pi / length)
    inverse = np.mod(np.arange(length)[:, None] * centred[None, :], length) * (2.0 * math.pi / length)
    mask = np.array([1, 1j, -1, -1j])[np.abs(centred) % 4]
    return rounded_table(inverse, length, 1.0) @ (mask[:, None] * rounded_table(forward, length, -1.0))


def half_angle(angle):
    turns = angle * (0.5 / math.pi)
    rest = turns - jnp.floor(turns + 0.5)
    square = rest * rest
    sine = rest * polynomial(square, (4.442867756, -7.307443618, 3.594788074, -0.784373999))
    cosine = polynomial(square, (1.414213538, -6.978850841, 5.739460945, -1.883563042, 0.310698181))
    return sine, cosine


def sin_cos(angle):
    sine, cosine = half_angle(angle)
    return sine * cosine, 1.0 - sine * sine


def field_parts(phase, amplitude):
    sine, cosine = half_angle(phase)
    lead = amplitude * sine
    return (amplitude - lead * sine).astype(jnp.bfloat16), (lead * cosine).astype(jnp.bfloat16)


def polynomial(x, coefficients):
    value = coefficients[-1]
    for coefficient in coefficients[-2::-1]:
        value = value * x + coefficient
    return value


def field_matrix(real, imag):
    return jnp.concatenate([jnp.concatenate([real, imag], 1), jnp.concatenate([-imag, real], 1)], 0)


def halves(values):
    high = values.astype(jnp.bfloat16)
    low = (values - high.astype(jnp.float32)).astype(jnp.bfloat16)
    return high, low


def look_up(count, row, index):
    blocks = []
    for start in range(0, index.shape[0], 8):
        block = index[start : start + 8]
        high = block >> 7
        low = block & (LANES - 1)
        sums = [jnp.zeros(block.shape, jnp.float32) for _ in range(2)]
        for i in range(count):
            spread = jnp.broadcast_to(row(i), block.shape)
            picked = jnp.take_along_axis(spread, low, axis=1, mode="promise_in_bounds")
            sums[i % 2] = jnp.where(high == i, picked, sums[i % 2])
        blocks.append(sums[0] + sums[1])
    return jnp.concatenate(blocks, 0) if len(blocks) > 1 else blocks[0]


def runs(ref):
    per_row = ref.shape[1] // LANES

    def row(i):
        column = (i % per_row) * LANES
        return ref[i // per_row : i // per_row + 1, column : column + LANES]

    return ref.shape[0] * per_row, row


def copies(pairs, semaphores):
    started = [pltpu.make_async_copy(*pair, semaphores.at[i]) for i, pair in enumerate(pairs)]
    for copy in started:
        copy.start()
    return started


def own_rows(rows_hbm, row_count):
    start = pl.multiple_of(lax.axis_index("mod") * row_count, row_count)
    return rows_hbm.at[pl.ds(start, row_count)]


def spread_kernel(point_ref, angles_ref):
    angle = point_ref[0].astype(jnp.float32) * (2.0 * math.pi / point_count)
    angles_ref[...] = jnp.full(angles_ref.shape, angle, jnp.float32)


def prepare_kernel(
    phase_hbm, amp_hbm, map_hbm, gxt_hbm, gyt_hbm, rows_hbm, full_hbm, recon_hbm,
    field_ref, rows_ref, full_ref, cells_ref, gx_ref, gy_ref, recon_ref,
    phase_ref, amp_ref, map_ref, gxt_ref, gyt_ref, floats, semaphores,
):
    actuators, gxt, gyt, phase, amp, rows, full, recon = copies(
        [
            (map_hbm, map_ref), (gxt_hbm, gxt_ref), (gyt_hbm, gyt_ref), (phase_hbm, phase_ref), (amp_hbm, amp_ref),
            (own_rows(rows_hbm, rows_ref.shape[0]), rows_ref), (full_hbm, full_ref),
            (recon_hbm.at[: recon_ref.shape[0]], recon_ref),
        ],
        semaphores,
    )
    grid_rows, grid_columns = gxt_ref.shape[0], gyt_ref.shape[0]
    packed = cells_ref.shape[0]
    actuators.wait()
    floats[...] = map_ref[...].astype(jnp.float32)
    lane = lax.broadcasted_iota(jnp.int32, cells_ref.shape, 1)
    cell = (lane % grid_rows) * grid_columns + (lane // grid_rows) * packed
    cell = cell + lax.broadcasted_iota(jnp.int32, cells_ref.shape, 0)
    cells_ref[...] = look_up(*runs(floats), cell).astype(jnp.int32)
    gxt.wait()
    high, low = halves(gxt_ref[...].T)
    gx_ref[...] = jnp.concatenate([high, low, high, jnp.zeros_like(high)], 1)
    gyt.wait()
    high, low = halves(gyt_ref[...].T)
    gy_ref[...] = jnp.concatenate([high, low, high], 1)
    phase.wait()
    amp.wait()
    field_ref[...] = jnp.concatenate(field_parts(phase_ref[...], amp_ref[...]), 1)
    rows.wait()
    full.wait()
    recon.wait()


def mirror_surface(grid, gx_ref, gy_ref):
    f32 = jnp.float32
    lanes_used = gx_ref.shape[1] // 4
    if lanes_used == LANES:
        spread = [grid]
    else:
        lane = lax.broadcasted_iota(jnp.int32, grid.shape, 1)
        other = pltpu.roll(grid, lanes_used, 1)
        spread = [jnp.where(lane < lanes_used, grid, other), jnp.where(lane < lanes_used, other, grid)]
    transposed = jnp.concatenate(spread, 0)
    high = transposed.astype(jnp.bfloat16).astype(f32)
    parts = jnp.concatenate([high, high, transposed - high], 0).astype(jnp.bfloat16)
    high, low = halves(jnp.dot(gy_ref[...], parts, preferred_element_type=f32))
    return lax.dot_general(
        gx_ref[...], jnp.concatenate([high, low], 1), (((1,), (1,)), ((), ())), preferred_element_type=f32
    )


def tilt_factors(angles_ref, pupil, length):
    sin_a, cos_a = sin_cos(angles_ref[...])
    spread = pupil // LANES
    sin_a = jnp.concatenate([sin_a] * spread, 1)
    cos_a = jnp.concatenate([cos_a] * spread, 1)
    place = (lax.broadcasted_iota(jnp.int32, sin_a.shape, 1) - pupil // 2).astype(jnp.float32)
    place = place * (2.0 * math.pi * radius_pixels / length)
    return sin_cos(place * cos_a) + sin_cos(place * sin_a)


def turned(real, imag, sine, cosine):
    sine, cosine = sine[:, None, :], cosine[:, None, :]
    return real * cosine - imag * sine, real * sine + imag * cosine


def left_rows(rows, sine, cosine):
    count, pupil = sine.shape
    left = jnp.concatenate(turned(rows[None, :, :pupil], rows[None, :, pupil:], sine, cosine), 2)
    return left.reshape(count * rows.shape[0], 2 * pupil).astype(jnp.bfloat16)


def half_way(left, field, sine, cosine):
    count, pupil = sine.shape
    rows = left.shape[0]
    half = jnp.dot(left, field, preferred_element_type=jnp.float32)
    half = half.reshape(count, rows // count, 2 * pupil)
    real, imag = turned(half[:, :, :pupil], half[:, :, pupil:], sine, cosine)
    real = real.reshape(rows, pupil).astype(jnp.bfloat16)
    imag = imag.reshape(rows, pupil).astype(jnp.bfloat16)
    return jnp.concatenate([jnp.concatenate([real, -imag], 1), jnp.concatenate([imag, real], 1)], 0)


def detect(left, field, full_ref, sine, cosine, frame_ref):
    row_count, length = frame_ref.shape
    count = sine.shape[0]
    both = half_way(left, field, sine, cosine)
    detector = jnp.dot(both, full_ref[...], preferred_element_type=jnp.float32)
    squares = (detector * detector).reshape(2 * count, row_count, length)
    frame_ref[...] = jnp.sum(squares, 0) * (1.0 / count)


def read_signals(frame_ref, pixels):
    row_count, length = frame_ref.shape
    per_row = length // LANES
    own = pixels - lax.axis_index("mod") * (row_count * length)
    low = own & (LANES - 1)
    run = (own >> 7) & (per_row - 1)
    row = own >> (per_row * LANES).bit_length() - 1
    bits = [(run >> i) & 1 == 1 for i in range(per_row.bit_length() - 1)]
    total = jnp.zeros(pixels.shape, jnp.float32)
    for i in range(row_count):
        picked = []
        for j in range(per_row):
            spread = jnp.broadcast_to(frame_ref[i : i + 1, j * LANES : (j + 1) * LANES], pixels.shape)
            picked.append(jnp.take_along_axis(spread, low, axis=1, mode="promise_in_bounds"))
        for bit in bits:
            picked = [jnp.where(bit, picked[j + 1], picked[j]) for j in range(0, len(picked), 2)]
        total = jnp.where(row == i, picked[0], total)
    return total.astype(jnp.bfloat16).astype(jnp.float32)


def first_kernel(
    angles_ref, field_ref, rows_ref, full_ref, pixels_hbm, recon_hbm, signal_ref, tilt_ref, left_ref, recon_ref,
    pixels_ref, frame_ref, semaphores,
):
    length = frame_ref.shape[1]
    pupil = length // 2
    pixels, recon = copies(
        [(pixels_hbm, pixels_ref), (recon_hbm.at[recon_hbm.shape[0] - recon_ref.shape[0] :], recon_ref)], semaphores
    )
    tilts = tilt_factors(angles_ref, pupil, length)
    tilt_ref[0], tilt_ref[1] = tilts[2:]
    left = left_rows(rows_ref[...], *tilts[:2])
    left_ref[...] = left
    field = field_matrix(field_ref[:, :pupil], field_ref[:, pupil:])
    detect(left, field, full_ref, *tilts[2:], frame_ref)
    pixels.wait()
    signal_ref[...] = read_signals(frame_ref, pixels_ref[...])
    recon.wait()


def add_commands(parts_ref, total_ref, out_ref):
    cases = out_ref.shape[0]
    each = parts_ref.shape[0] // cases
    for case in range(cases):
        sums = jnp.sum(parts_ref[case * each : (case + 1) * each].astype(jnp.float32), 0)
        out_ref[case] = loop_gain * sums if total_ref is None else total_ref[case] + loop_gain * sums


def later_kernel(
    parts_ref, tilt_ref, cells_ref, gx_ref, gy_ref, left_ref, full_ref, phase_hbm, amp_hbm, pixels_hbm, recon_hbm,
    *refs
):
    old_total, refs = (None, refs) if len(refs) == 8 else (refs[0], refs[1:])
    frame_ref, signal_ref, new_total_ref, recon_ref, phase_ref, amp_ref, pixels_ref, semaphores = refs
    phase, amp, pixels, recon = copies(
        [
            (phase_hbm, phase_ref), (amp_hbm, amp_ref), (pixels_hbm, pixels_ref),
            (recon_hbm.at[recon_hbm.shape[0] - recon_ref.shape[0] :], recon_ref),
        ],
        semaphores,
    )
    add_commands(parts_ref, old_total, new_total_ref)
    cases, pieces, width = new_total_ref.shape
    per_piece = width // LANES

    def row(i):
        column = (i % per_piece) * LANES
        piece = i // per_piece
        return new_total_ref[piece // pieces, piece % pieces : piece % pieces + 1, column : column + LANES]

    grid = look_up(cases * pieces * per_piece, row, cells_ref[...])
    surface = mirror_surface(grid, gx_ref, gy_ref)
    phase.wait()
    amp.wait()
    field = field_matrix(*field_parts(phase_ref[...] - surface, amp_ref[...]))

    detect(left_ref[...], field, full_ref, tilt_ref[0], tilt_ref[1], frame_ref)
    pixels.wait()
    signal_ref[...] = read_signals(frame_ref, pixels_ref[...])
    recon.wait()


def command_kernel(*refs):
    signal_refs, recon_refs, out_ref = refs[:-3], refs[-3:-1], refs[-1]
    cases = len(signal_refs)
    own_case = lax.axis_index("case")
    received = [ref[...] for ref in signal_refs]
    ordered = []
    for case in range(cases):
        values = received[0]
        for j in range(1, cases):
            values = jnp.where((own_case ^ j) == case, received[j], values)
        ordered.append(values)
    groups = received[0].shape[0]
    signals = jnp.concatenate(
        [jnp.concatenate([values[g : g + 1] for values in ordered], 0) for g in range(groups)], 1
    ).astype(jnp.bfloat16)
    partial = jnp.concatenate(
        [
            lax.dot_general(signals, ref[...], (((1,), (1,)), ((), ())), preferred_element_type=jnp.float32)
            for ref in recon_refs
        ],
        1,
    )
    messages, pieces, width = out_ref.shape
    copies_each = messages // cases
    for case in range(cases):
        message = jnp.concatenate(
            [partial[case : case + 1, i * width : (i + 1) * width] for i in range(pieces)], 0
        ).astype(jnp.bfloat16)
        for i in range(copies_each):
            out_ref[case * copies_each + i] = message


def last_kernel(parts_ref, total_ref, frame_ref, total_hbm, frame_hbm, sums_ref, out_ref, semaphores):
    frame_out = pltpu.make_async_copy(frame_ref, frame_hbm, semaphores.at[0])
    frame_out.start()
    add_commands(parts_ref, total_ref, sums_ref)
    cases, pieces, width = sums_ref.shape
    for case in range(cases):
        for i in range(pieces):
            start = (case * pieces + i) * width
            out_ref[:, start : start + width] = sums_ref[case, i : i + 1, :]
    total_out = pltpu.make_async_copy(out_ref, total_hbm, semaphores.at[1])
    total_out.start()
    frame_out.wait()
    total_out.wait()


def body(turbulence, pupil_amp, mod_points, valid_pix, recon, gx, gy, act_map):
    pupil = pupil_amp.shape[0]
    length = 2 * pupil
    cases = lax.axis_size("case")
    devices_mod = lax.axis_size("mod")
    count = devices_mod * mod_points.shape[0]
    row_count = length // devices_mod
    block = recon.shape[0]
    pieces = 2
    width = block // pieces
    signal_rows = valid_pix.shape[0] // LANES
    grid_rows, grid_columns = gx.shape[1], gy.shape[1]
    packed = grid_columns * grid_rows // LANES
    screen = turbulence[0]
    pixels = valid_pix.reshape(signal_rows, LANES)
    f32, bf16 = jnp.float32, jnp.bfloat16
    shape = jax.ShapeDtypeStruct
    hbm = pl.BlockSpec(memory_space=pltpu.HBM)
    vmem = pl.BlockSpec(memory_space=pltpu.VMEM)
    smem = pl.BlockSpec(memory_space=pltpu.SMEM)

    def call(kernel, name, outs, out_specs, in_specs, scratch, *operands):
        operands = [
            pltpu.with_memory_space_constraint(operand, pltpu.HBM) if spec is hbm else operand
            for operand, spec in zip(operands, in_specs)
        ]
        if isinstance(outs, tuple):
            outs = tuple(
                pltpu.HBM(out.shape, out.dtype) if spec is hbm else out for out, spec in zip(outs, out_specs)
            )
        return pl.pallas_call(
            kernel,
            out_shape=outs,
            in_specs=in_specs,
            out_specs=out_specs,
            scratch_shapes=scratch,
            compiler_params=pltpu.CompilerParams(vmem_limit_bytes=VMEM_LIMIT),
            name=name,
        )(*operands)

    def like(*arrays):
        return [pltpu.VMEM(array.shape, array.dtype) for array in arrays]

    def done(count):
        return pltpu.SemaphoreType.DMA((count,))

    table = pyramid_table(pupil, length)
    rows_table = jnp.asarray(np.concatenate([table.real, table.imag], 1).astype(np.float32))
    full_table = jnp.asarray(np.concatenate([table.real.T, table.imag.T], 0).astype(jnp.bfloat16))

    with jax.named_scope("modulation_angles"):
        angles = call(
            spread_kernel, "spread", shape((devices_mod, 1, LANES), f32), vmem, [smem], [], mod_points
        )
        angles = lax.all_to_all(angles, "mod", 0, 0, tiled=True).reshape(count, LANES)

    recon_early = block // LANES * 6 // 10 * LANES
    late_shape = shape((block - recon_early, recon.shape[1]), bf16)
    map_shape = (act_map.shape[0] // LANES, LANES)
    field, rows, full, cells, gx_parts, gy_parts, recon_first = call(
        prepare_kernel,
        "prepare",
        (
            shape((pupil, 2 * pupil), bf16),
            shape((row_count, 2 * pupil), f32),
            shape(full_table.shape, bf16),
            shape((packed, LANES), jnp.int32),
            shape((pupil, 4 * grid_rows), bf16),
            shape((pupil, 3 * grid_columns), bf16),
            shape((recon_early, recon.shape[1]), bf16),
        ),
        (vmem,) * 7,
        [hbm] * 8,
        like(screen, pupil_amp)
        + [
            pltpu.VMEM(map_shape, jnp.int32),
            pltpu.VMEM(gx.shape[::-1], f32),
            pltpu.VMEM(gy.shape[::-1], f32),
            pltpu.VMEM(map_shape, f32),
            done(8),
        ],
        screen, pupil_amp, act_map.reshape(map_shape), gx.T, gy.T, rows_table, full_table, recon,
    )

    def commands(signal, recon_late):
        signals = [signal]
        for j in range(1, cases):
            signals.append(lax.ppermute(signal, "case", [(i, i ^ j) for i in range(cases)]))
        partial = call(
            command_kernel, "commands", shape((cases * devices_mod, pieces, width), bf16), vmem,
            [vmem] * (cases + 2), [], *signals, recon_first, recon_late,
        )
        return lax.all_to_all(partial, ("case", "mod"), 0, 0, tiled=True)

    frame_shape = shape((row_count, length), f32)
    signal_shape = shape((signal_rows, LANES), f32)
    total_shape = shape((cases, pieces, width), f32)
    left_shape = shape((count * row_count, 2 * pupil), bf16)
    signal, tilts, left, recon_late = call(
        first_kernel,
        "first_frame",
        (signal_shape, shape((2, count, pupil), f32), left_shape, late_shape),
        (vmem, vmem, vmem, vmem),
        [vmem, vmem, vmem, vmem, hbm, hbm],
        like(pixels, frame_shape) + [done(2)],
        angles, field, rows, full, pixels, recon,
    )
    totals = ()
    for iteration in range(1, STEPS):
        parts = commands(signal, recon_late)
        held = (screen, pupil_amp, pixels)
        frame, signal, *totals, recon_late = call(
            later_kernel,
            "next_frame",
            (frame_shape, signal_shape, total_shape, late_shape),
            (vmem, vmem, vmem, vmem),
            [vmem] * 7 + [hbm] * 4 + [vmem] * len(totals),
            like(*held) + [done(4)],
            parts, tilts, cells, gx_parts, gy_parts, left, full, *held, recon, *totals,
        )
    parts = commands(signal, recon_late)
    command_shape = shape((1, cases * block), f32)
    command_total, frame = call(
        last_kernel,
        "total",
        (command_shape, frame_shape),
        (hbm, hbm),
        [vmem, vmem, vmem],
        like(total_shape, command_shape) + [done(2)],
        parts, *totals, frame,
    )
    return (command_total, frame[None])


def solution(mesh):
    return jax.shard_map(
        body,
        mesh=mesh,
        in_specs=(P("case", None, None), P(), P("mod"), P("mod"), P("case", "mod"), P(), P(), P()),
        out_specs=(P("case", None), P("case", "mod", None)),
        check_vma=False,
    )
```

```python
import math

import jax
import jax.numpy as jnp
import numpy as np
from jax import lax
from jax.experimental import pallas as pl
from jax.experimental.pallas import tpu as pltpu
from jax.sharding import PartitionSpec as P

STEPS = 2


loop_gain = 0.5
radius_pixels = 6.0
point_count = 256
LANES = 128
VMEM_LIMIT = 16 * 1024 * 1024


def rounded_table(angle, length, sign):
    scale = 1.0 / math.sqrt(length)
    real = (np.cos(angle) * scale).astype(np.float32).astype(jnp.bfloat16).astype(np.float64)
    imag = (sign * np.sin(angle) * scale).astype(np.float32).astype(jnp.bfloat16).astype(np.float64)
    return real + 1j * imag


def pyramid_table(pupil_size, length):
    centred = np.arange(length) - length // 2
    forward = np.mod(centred[:, None] * np.arange(pupil_size)[None, :], length) * (2.0 * math.pi / length)
    inverse = np.mod(np.arange(length)[:, None] * centred[None, :], length) * (2.0 * math.pi / length)
    mask = np.array([1, 1j, -1, -1j])[np.abs(centred) % 4]
    return rounded_table(inverse, length, 1.0) @ (mask[:, None] * rounded_table(forward, length, -1.0))


def half_angle(angle):
    turns = angle * (0.5 / math.pi)
    rest = turns - jnp.floor(turns + 0.5)
    square = rest * rest
    sine = rest * polynomial(square, (4.442867756, -7.307443618, 3.594788074, -0.784373999))
    cosine = polynomial(square, (1.414213538, -6.978850841, 5.739460945, -1.883563042, 0.310698181))
    return sine, cosine


def sin_cos(angle):
    sine, cosine = half_angle(angle)
    return sine * cosine, 1.0 - sine * sine


def field_parts(phase, amplitude):
    sine, cosine = half_angle(phase)
    lead = amplitude * sine
    return (amplitude - lead * sine).astype(jnp.bfloat16), (lead * cosine).astype(jnp.bfloat16)


def polynomial(x, coefficients):
    value = coefficients[-1]
    for coefficient in coefficients[-2::-1]:
        value = value * x + coefficient
    return value


def field_matrix(real, imag):
    return jnp.concatenate([jnp.concatenate([real, imag], 1), jnp.concatenate([-imag, real], 1)], 0)


def halves(values):
    high = values.astype(jnp.bfloat16)
    low = (values - high.astype(jnp.float32)).astype(jnp.bfloat16)
    return high, low


def choose(picked, index):
    while len(picked) > 1:
        odd = index & 1 == 1
        rest = picked[len(picked) - 1 :] if len(picked) % 2 else []
        picked = [jnp.where(odd, picked[j + 1], picked[j]) for j in range(0, len(picked) - 1, 2)] + rest
        index = index >> 1
    return picked[0]


def look_up(count, row, index):
    blocks = []
    for start in range(0, index.shape[0], 8):
        block = index[start : start + 8]
        high = block >> 7
        low = block & (LANES - 1)
        picked = []
        for i in range(count):
            spread = jnp.broadcast_to(row(i), block.shape)
            picked.append(jnp.take_along_axis(spread, low, axis=1, mode="promise_in_bounds"))
        blocks.append(choose(picked, high))
    return jnp.concatenate(blocks, 0) if len(blocks) > 1 else blocks[0]


def runs(ref):
    per_row = ref.shape[1] // LANES

    def row(i):
        column = (i % per_row) * LANES
        return ref[i // per_row : i // per_row + 1, column : column + LANES]

    return ref.shape[0] * per_row, row


def copies(pairs, semaphores):
    started = [pltpu.make_async_copy(*pair, semaphores.at[i]) for i, pair in enumerate(pairs)]
    for copy in started:
        copy.start()
    return started


def own_rows(rows_hbm, row_count):
    start = pl.multiple_of(lax.axis_index("mod") * row_count, row_count)
    return rows_hbm.at[pl.ds(start, row_count)]


def spread_kernel(point_ref, angles_ref):
    angle = point_ref[0].astype(jnp.float32) * (2.0 * math.pi / point_count)
    angles_ref[...] = jnp.full(angles_ref.shape, angle, jnp.float32)


def prepare_kernel(
    phase_hbm, amp_hbm, map_hbm, gxt_hbm, gyt_hbm, rows_hbm, full_hbm, recon_hbm,
    field_ref, rows_ref, full_ref, cells_ref, gx_ref, gy_ref, recon_ref,
    phase_ref, amp_ref, map_ref, gxt_ref, gyt_ref, floats, semaphores,
):
    actuators, gxt, gyt, phase, amp, rows, full, recon = copies(
        [
            (map_hbm, map_ref), (gxt_hbm, gxt_ref), (gyt_hbm, gyt_ref), (phase_hbm, phase_ref), (amp_hbm, amp_ref),
            (own_rows(rows_hbm, rows_ref.shape[0]), rows_ref), (full_hbm, full_ref),
            (recon_hbm.at[: recon_ref.shape[0]], recon_ref),
        ],
        semaphores,
    )
    grid_rows, grid_columns = gxt_ref.shape[0], gyt_ref.shape[0]
    packed = cells_ref.shape[0]
    actuators.wait()
    floats[...] = map_ref[...].astype(jnp.float32)
    lane = lax.broadcasted_iota(jnp.int32, cells_ref.shape, 1)
    cell = (lane % grid_rows) * grid_columns + (lane // grid_rows) * packed
    cell = cell + lax.broadcasted_iota(jnp.int32, cells_ref.shape, 0)
    cells_ref[...] = look_up(*runs(floats), cell).astype(jnp.int32)
    gxt.wait()
    high, low = halves(gxt_ref[...].T)
    gx_ref[...] = jnp.concatenate([high, low, high, jnp.zeros_like(high)], 1)
    gyt.wait()
    high, low = halves(gyt_ref[...].T)
    gy_ref[...] = jnp.concatenate([high, low, high], 1)
    phase.wait()
    amp.wait()
    field_ref[...] = jnp.concatenate(field_parts(phase_ref[...], amp_ref[...]), 1)
    rows.wait()
    full.wait()
    recon.wait()


def mirror_surface(grid, gx_ref, gy_ref):
    f32 = jnp.float32
    lanes_used = gx_ref.shape[1] // 4
    if lanes_used == LANES:
        spread = [grid]
    else:
        lane = lax.broadcasted_iota(jnp.int32, grid.shape, 1)
        other = pltpu.roll(grid, lanes_used, 1)
        spread = [jnp.where(lane < lanes_used, grid, other), jnp.where(lane < lanes_used, other, grid)]
    transposed = jnp.concatenate(spread, 0)
    high = transposed.astype(jnp.bfloat16).astype(f32)
    parts = jnp.concatenate([high, high, transposed - high], 0).astype(jnp.bfloat16)
    high, low = halves(jnp.dot(gy_ref[...], parts, preferred_element_type=f32))
    return lax.dot_general(
        gx_ref[...], jnp.concatenate([high, low], 1), (((1,), (1,)), ((), ())), preferred_element_type=f32
    )


def tilt_factors(angles_ref, pupil, length):
    sin_a, cos_a = sin_cos(angles_ref[...])
    spread = pupil // LANES
    sin_a = jnp.concatenate([sin_a] * spread, 1)
    cos_a = jnp.concatenate([cos_a] * spread, 1)
    place = (lax.broadcasted_iota(jnp.int32, sin_a.shape, 1) - pupil // 2).astype(jnp.float32)
    place = place * (2.0 * math.pi * radius_pixels / length)
    return sin_cos(place * cos_a) + sin_cos(place * sin_a)


def turned(real, imag, sine, cosine):
    sine, cosine = sine[:, None, :], cosine[:, None, :]
    return real * cosine - imag * sine, real * sine + imag * cosine


def left_rows(rows, sine, cosine):
    count, pupil = sine.shape
    left = jnp.concatenate(turned(rows[None, :, :pupil], rows[None, :, pupil:], sine, cosine), 2)
    return left.reshape(count * rows.shape[0], 2 * pupil).astype(jnp.bfloat16)


def half_way(left, field, sine, cosine):
    count, pupil = sine.shape
    rows = left.shape[0]
    half = jnp.dot(left, field, preferred_element_type=jnp.float32)
    half = half.reshape(count, rows // count, 2 * pupil)
    real, imag = turned(half[:, :, :pupil], half[:, :, pupil:], sine, cosine)
    real = real.reshape(rows, pupil).astype(jnp.bfloat16)
    imag = imag.reshape(rows, pupil).astype(jnp.bfloat16)
    return jnp.concatenate([jnp.concatenate([real, -imag], 1), jnp.concatenate([imag, real], 1)], 0)


def detect(left, field, full_ref, sine, cosine, frame_ref):
    row_count, length = frame_ref.shape
    count = sine.shape[0]
    both = half_way(left, field, sine, cosine)
    detector = jnp.dot(both, full_ref[...], preferred_element_type=jnp.float32)
    squares = (detector * detector).reshape(2 * count, row_count, length)
    frame_ref[...] = jnp.sum(squares, 0) * (1.0 / count)


def read_signals(frame_ref, pixels):
    row_count, length = frame_ref.shape
    per_row = length // LANES
    own = pixels - lax.axis_index("mod") * (row_count * length)
    low = own & (LANES - 1)
    run = (own >> 7) & (per_row - 1)
    row = own >> (per_row * LANES).bit_length() - 1
    rows = []
    for i in range(row_count):
        picked = []
        for j in range(per_row):
            spread = jnp.broadcast_to(frame_ref[i : i + 1, j * LANES : (j + 1) * LANES], pixels.shape)
            picked.append(jnp.take_along_axis(spread, low, axis=1, mode="promise_in_bounds"))
        rows.append(choose(picked, run))
    total = choose(rows, row)
    return total.astype(jnp.bfloat16).astype(jnp.float32)


def first_kernel(
    angles_ref, field_ref, rows_ref, full_ref, pixels_hbm, recon_hbm, signal_ref, tilt_ref, left_ref, recon_ref,
    pixels_ref, frame_ref, semaphores,
):
    length = frame_ref.shape[1]
    pupil = length // 2
    pixels, recon = copies(
        [(pixels_hbm, pixels_ref), (recon_hbm.at[recon_hbm.shape[0] - recon_ref.shape[0] :], recon_ref)], semaphores
    )
    tilts = tilt_factors(angles_ref, pupil, length)
    tilt_ref[0], tilt_ref[1] = tilts[2:]
    left = left_rows(rows_ref[...], *tilts[:2])
    left_ref[...] = left
    field = field_matrix(field_ref[:, :pupil], field_ref[:, pupil:])
    detect(left, field, full_ref, *tilts[2:], frame_ref)
    pixels.wait()
    signal_ref[...] = read_signals(frame_ref, pixels_ref[...])
    recon.wait()


def add_commands(parts_ref, total_ref, out_ref):
    cases = out_ref.shape[0]
    each = parts_ref.shape[0] // cases
    for case in range(cases):
        sums = jnp.sum(parts_ref[case * each : (case + 1) * each].astype(jnp.float32), 0)
        out_ref[case] = loop_gain * sums if total_ref is None else total_ref[case] + loop_gain * sums


def later_kernel(
    parts_ref, tilt_ref, cells_ref, gx_ref, gy_ref, left_ref, full_ref, phase_hbm, amp_hbm, pixels_hbm, recon_hbm,
    *refs
):
    old_total, refs = (None, refs) if len(refs) == 8 else (refs[0], refs[1:])
    frame_ref, signal_ref, new_total_ref, recon_ref, phase_ref, amp_ref, pixels_ref, semaphores = refs
    phase, amp, pixels, recon = copies(
        [
            (phase_hbm, phase_ref), (amp_hbm, amp_ref), (pixels_hbm, pixels_ref),
            (recon_hbm.at[recon_hbm.shape[0] - recon_ref.shape[0] :], recon_ref),
        ],
        semaphores,
    )
    add_commands(parts_ref, old_total, new_total_ref)
    cases, pieces, width = new_total_ref.shape
    per_piece = width // LANES

    def row(i):
        column = (i % per_piece) * LANES
        piece = i // per_piece
        return new_total_ref[piece // pieces, piece % pieces : piece % pieces + 1, column : column + LANES]

    grid = look_up(cases * pieces * per_piece, row, cells_ref[...])
    surface = mirror_surface(grid, gx_ref, gy_ref)
    phase.wait()
    amp.wait()
    field = field_matrix(*field_parts(phase_ref[...] - surface, amp_ref[...]))

    detect(left_ref[...], field, full_ref, tilt_ref[0], tilt_ref[1], frame_ref)
    pixels.wait()
    signal_ref[...] = read_signals(frame_ref, pixels_ref[...])
    recon.wait()


def command_kernel(*refs):
    signal_refs, recon_refs, out_ref = refs[:-3], refs[-3:-1], refs[-1]
    cases = len(signal_refs)
    own_case = lax.axis_index("case")
    received = [ref[...] for ref in signal_refs]
    ordered = []
    for case in range(cases):
        values = received[0]
        for j in range(1, cases):
            values = jnp.where((own_case ^ j) == case, received[j], values)
        ordered.append(values)
    groups = received[0].shape[0]
    signals = jnp.concatenate(
        [jnp.concatenate([values[g : g + 1] for values in ordered], 0) for g in range(groups)], 1
    ).astype(jnp.bfloat16)
    partial = jnp.concatenate(
        [
            lax.dot_general(signals, ref[...], (((1,), (1,)), ((), ())), preferred_element_type=jnp.float32)
            for ref in recon_refs
        ],
        1,
    )
    messages, pieces, width = out_ref.shape
    copies_each = messages // cases
    for case in range(cases):
        message = jnp.concatenate(
            [partial[case : case + 1, i * width : (i + 1) * width] for i in range(pieces)], 0
        ).astype(jnp.bfloat16)
        for i in range(copies_each):
            out_ref[case * copies_each + i] = message


def last_kernel(parts_ref, total_ref, frame_ref, total_hbm, frame_hbm, sums_ref, out_ref, semaphores):
    frame_out = pltpu.make_async_copy(frame_ref, frame_hbm, semaphores.at[0])
    frame_out.start()
    add_commands(parts_ref, total_ref, sums_ref)
    cases, pieces, width = sums_ref.shape
    for case in range(cases):
        for i in range(pieces):
            start = (case * pieces + i) * width
            out_ref[:, start : start + width] = sums_ref[case, i : i + 1, :]
    total_out = pltpu.make_async_copy(out_ref, total_hbm, semaphores.at[1])
    total_out.start()
    frame_out.wait()
    total_out.wait()


def body(turbulence, pupil_amp, mod_points, valid_pix, recon, gx, gy, act_map):
    pupil = pupil_amp.shape[0]
    length = 2 * pupil
    cases = lax.axis_size("case")
    devices_mod = lax.axis_size("mod")
    count = devices_mod * mod_points.shape[0]
    row_count = length // devices_mod
    block = recon.shape[0]
    pieces = 2
    width = block // pieces
    signal_rows = valid_pix.shape[0] // LANES
    grid_rows, grid_columns = gx.shape[1], gy.shape[1]
    packed = grid_columns * grid_rows // LANES
    screen = turbulence[0]
    pixels = valid_pix.reshape(signal_rows, LANES)
    f32, bf16 = jnp.float32, jnp.bfloat16
    shape = jax.ShapeDtypeStruct
    hbm = pl.BlockSpec(memory_space=pltpu.HBM)
    vmem = pl.BlockSpec(memory_space=pltpu.VMEM)
    smem = pl.BlockSpec(memory_space=pltpu.SMEM)

    def call(kernel, name, outs, out_specs, in_specs, scratch, *operands):
        operands = [
            pltpu.with_memory_space_constraint(operand, pltpu.HBM) if spec is hbm else operand
            for operand, spec in zip(operands, in_specs)
        ]
        if isinstance(outs, tuple):
            outs = tuple(
                pltpu.HBM(out.shape, out.dtype) if spec is hbm else out for out, spec in zip(outs, out_specs)
            )
        return pl.pallas_call(
            kernel,
            out_shape=outs,
            in_specs=in_specs,
            out_specs=out_specs,
            scratch_shapes=scratch,
            compiler_params=pltpu.CompilerParams(vmem_limit_bytes=VMEM_LIMIT),
            name=name,
        )(*operands)

    def like(*arrays):
        return [pltpu.VMEM(array.shape, array.dtype) for array in arrays]

    def done(count):
        return pltpu.SemaphoreType.DMA((count,))

    table = pyramid_table(pupil, length)
    rows_table = jnp.asarray(np.concatenate([table.real, table.imag], 1).astype(np.float32))
    full_table = jnp.asarray(np.concatenate([table.real.T, table.imag.T], 0).astype(jnp.bfloat16))

    with jax.named_scope("modulation_angles"):
        angles = call(
            spread_kernel, "spread", shape((devices_mod, 1, LANES), f32), vmem, [smem], [], mod_points
        )
        angles = lax.all_to_all(angles, "mod", 0, 0, tiled=True).reshape(count, LANES)

    recon_early = block // LANES * 6 // 10 * LANES
    late_shape = shape((block - recon_early, recon.shape[1]), bf16)
    map_shape = (act_map.shape[0] // LANES, LANES)
    field, rows, full, cells, gx_parts, gy_parts, recon_first = call(
        prepare_kernel,
        "prepare",
        (
            shape((pupil, 2 * pupil), bf16),
            shape((row_count, 2 * pupil), f32),
            shape(full_table.shape, bf16),
            shape((packed, LANES), jnp.int32),
            shape((pupil, 4 * grid_rows), bf16),
            shape((pupil, 3 * grid_columns), bf16),
            shape((recon_early, recon.shape[1]), bf16),
        ),
        (vmem,) * 7,
        [hbm] * 8,
        like(screen, pupil_amp)
        + [
            pltpu.VMEM(map_shape, jnp.int32),
            pltpu.VMEM(gx.shape[::-1], f32),
            pltpu.VMEM(gy.shape[::-1], f32),
            pltpu.VMEM(map_shape, f32),
            done(8),
        ],
        screen, pupil_amp, act_map.reshape(map_shape), gx.T, gy.T, rows_table, full_table, recon,
    )

    def commands(signal, recon_late):
        signals = [signal]
        for j in range(1, cases):
            signals.append(lax.ppermute(signal, "case", [(i, i ^ j) for i in range(cases)]))
        partial = call(
            command_kernel, "commands", shape((cases * devices_mod, pieces, width), bf16), vmem,
            [vmem] * (cases + 2), [], *signals, recon_first, recon_late,
        )
        return lax.all_to_all(partial, ("case", "mod"), 0, 0, tiled=True)

    frame_shape = shape((row_count, length), f32)
    signal_shape = shape((signal_rows, LANES), f32)
    total_shape = shape((cases, pieces, width), f32)
    left_shape = shape((count * row_count, 2 * pupil), bf16)
    signal, tilts, left, recon_late = call(
        first_kernel,
        "first_frame",
        (signal_shape, shape((2, count, pupil), f32), left_shape, late_shape),
        (vmem, vmem, vmem, vmem),
        [vmem, vmem, vmem, vmem, hbm, hbm],
        like(pixels, frame_shape) + [done(2)],
        angles, field, rows, full, pixels, recon,
    )
    totals = ()
    for iteration in range(1, STEPS):
        parts = commands(signal, recon_late)
        held = (screen, pupil_amp, pixels)
        frame, signal, *totals, recon_late = call(
            later_kernel,
            "next_frame",
            (frame_shape, signal_shape, total_shape, late_shape),
            (vmem, vmem, vmem, vmem),
            [vmem] * 7 + [hbm] * 4 + [vmem] * len(totals),
            like(*held) + [done(4)],
            parts, tilts, cells, gx_parts, gy_parts, left, full, *held, recon, *totals,
        )
    parts = commands(signal, recon_late)
    command_shape = shape((1, cases * block), f32)
    command_total, frame = call(
        last_kernel,
        "total",
        (command_shape, frame_shape),
        (hbm, hbm),
        [vmem, vmem, vmem],
        like(total_shape, command_shape) + [done(2)],
        parts, *totals, frame,
    )
    return (command_total, frame[None])


def solution(mesh):
    return jax.shard_map(
        body,
        mesh=mesh,
        in_specs=(P("case", None, None), P(), P("mod"), P("mod"), P("case", "mod"), P(), P(), P()),
        out_specs=(P("case", None), P("case", "mod", None)),
        check_vma=False,
    )
```

```python
import math

import jax
import jax.numpy as jnp
import numpy as np
from jax import lax
from jax.experimental import pallas as pl
from jax.experimental.pallas import tpu as pltpu
from jax.sharding import PartitionSpec as P

STEPS = 2


loop_gain = 0.5
radius_pixels = 6.0
point_count = 256
LANES = 128
VMEM_LIMIT = 16 * 1024 * 1024


def rounded_table(angle, length, sign):
    scale = 1.0 / math.sqrt(length)
    real = (np.cos(angle) * scale).astype(np.float32).astype(jnp.bfloat16).astype(np.float64)
    imag = (sign * np.sin(angle) * scale).astype(np.float32).astype(jnp.bfloat16).astype(np.float64)
    return real + 1j * imag


def pyramid_table(pupil_size, length):
    centred = np.arange(length) - length // 2
    forward = np.mod(centred[:, None] * np.arange(pupil_size)[None, :], length) * (2.0 * math.pi / length)
    inverse = np.mod(np.arange(length)[:, None] * centred[None, :], length) * (2.0 * math.pi / length)
    mask = np.array([1, 1j, -1, -1j])[np.abs(centred) % 4]
    return rounded_table(inverse, length, 1.0) @ (mask[:, None] * rounded_table(forward, length, -1.0))


def half_angle(angle):
    turns = angle * (0.5 / math.pi)
    rest = turns - jnp.floor(turns + 0.5)
    square = rest * rest
    sine = rest * polynomial(square, (4.442867756, -7.307443618, 3.594788074, -0.784373999))
    cosine = polynomial(square, (1.414213538, -6.978850841, 5.739460945, -1.883563042, 0.310698181))
    return sine, cosine


def sin_cos(angle):
    sine, cosine = half_angle(angle)
    return sine * cosine, 1.0 - sine * sine


def field_parts(phase, amplitude):
    sine, cosine = half_angle(phase)
    lead = amplitude * sine
    return (amplitude - lead * sine).astype(jnp.bfloat16), (lead * cosine).astype(jnp.bfloat16)


def polynomial(x, coefficients):
    value = coefficients[-1]
    for coefficient in coefficients[-2::-1]:
        value = value * x + coefficient
    return value


def field_matrix(real, imag):
    return jnp.concatenate([jnp.concatenate([real, imag], 1), jnp.concatenate([-imag, real], 1)], 0)


def halves(values):
    high = values.astype(jnp.bfloat16)
    low = (values - high.astype(jnp.float32)).astype(jnp.bfloat16)
    return high, low


def choose(picked, index):
    while len(picked) > 1:
        odd = index & 1 == 1
        rest = picked[len(picked) - 1 :] if len(picked) % 2 else []
        picked = [jnp.where(odd, picked[j + 1], picked[j]) for j in range(0, len(picked) - 1, 2)] + rest
        index = index >> 1
    return picked[0]


def look_up(count, row, index):
    blocks = []
    for start in range(0, index.shape[0], 8):
        block = index[start : start + 8]
        high = block >> 7
        low = block & (LANES - 1)
        picked = []
        for i in range(count):
            spread = jnp.broadcast_to(row(i), block.shape)
            picked.append(jnp.take_along_axis(spread, low, axis=1, mode="promise_in_bounds"))
        blocks.append(choose(picked, high))
    return jnp.concatenate(blocks, 0) if len(blocks) > 1 else blocks[0]


def runs(ref):
    per_row = ref.shape[1] // LANES

    def row(i):
        column = (i % per_row) * LANES
        return ref[i // per_row : i // per_row + 1, column : column + LANES]

    return ref.shape[0] * per_row, row


def copies(pairs, semaphores):
    started = [pltpu.make_async_copy(*pair, semaphores.at[i]) for i, pair in enumerate(pairs)]
    for copy in started:
        copy.start()
    return started


def own_rows(rows_hbm, row_count):
    start = pl.multiple_of(lax.axis_index("mod") * row_count, row_count)
    return rows_hbm.at[pl.ds(start, row_count)]


def spread_kernel(point_ref, angles_ref):
    angle = point_ref[0].astype(jnp.float32) * (2.0 * math.pi / point_count)
    angles_ref[...] = jnp.full(angles_ref.shape, angle, jnp.float32)


def prepare_kernel(
    phase_hbm, amp_hbm, map_hbm, gxt_hbm, gyt_hbm, rows_hbm, full_hbm, recon_hbm,
    field_ref, rows_ref, full_ref, cells_ref, gx_ref, gy_ref, recon_ref, phase_ref, amp_ref,
    map_ref, gxt_ref, gyt_ref, floats, semaphores,
):
    actuators, gxt, gyt, phase, amp, rows, full, recon = copies(
        [
            (map_hbm, map_ref), (gxt_hbm, gxt_ref), (gyt_hbm, gyt_ref), (phase_hbm, phase_ref), (amp_hbm, amp_ref),
            (own_rows(rows_hbm, rows_ref.shape[0]), rows_ref), (full_hbm, full_ref),
            (recon_hbm.at[: recon_ref.shape[0]], recon_ref),
        ],
        semaphores,
    )
    grid_rows, grid_columns = gxt_ref.shape[0], gyt_ref.shape[0]
    packed = cells_ref.shape[0]
    actuators.wait()
    floats[...] = map_ref[...].astype(jnp.float32)
    lane = lax.broadcasted_iota(jnp.int32, cells_ref.shape, 1)
    cell = (lane % grid_rows) * grid_columns + (lane // grid_rows) * packed
    cell = cell + lax.broadcasted_iota(jnp.int32, cells_ref.shape, 0)
    cells_ref[...] = look_up(*runs(floats), cell).astype(jnp.int32)
    gxt.wait()
    high, low = halves(gxt_ref[...].T)
    gx_ref[...] = jnp.concatenate([high, low, high, jnp.zeros_like(high)], 1)
    gyt.wait()
    high, low = halves(gyt_ref[...].T)
    gy_ref[...] = jnp.concatenate([high, low, high], 1)
    phase.wait()
    amp.wait()
    field_ref[...] = jnp.concatenate(field_parts(phase_ref[...], amp_ref[...]), 1)
    rows.wait()
    full.wait()
    recon.wait()


def mirror_surface(grid, gx_ref, gy_ref):
    f32 = jnp.float32
    lanes_used = gx_ref.shape[1] // 4
    if lanes_used == LANES:
        spread = [grid]
    else:
        lane = lax.broadcasted_iota(jnp.int32, grid.shape, 1)
        other = pltpu.roll(grid, lanes_used, 1)
        spread = [jnp.where(lane < lanes_used, grid, other), jnp.where(lane < lanes_used, other, grid)]
    transposed = jnp.concatenate(spread, 0)
    high = transposed.astype(jnp.bfloat16).astype(f32)
    parts = jnp.concatenate([high, high, transposed - high], 0).astype(jnp.bfloat16)
    high, low = halves(jnp.dot(gy_ref[...], parts, preferred_element_type=f32))
    return lax.dot_general(
        gx_ref[...], jnp.concatenate([high, low], 1), (((1,), (1,)), ((), ())), preferred_element_type=f32
    )


def tilt_factors(angles_ref, pupil, length):
    sin_a, cos_a = sin_cos(angles_ref[...])
    spread = pupil // LANES
    sin_a = jnp.concatenate([sin_a] * spread, 1)
    cos_a = jnp.concatenate([cos_a] * spread, 1)
    place = (lax.broadcasted_iota(jnp.int32, sin_a.shape, 1) - pupil // 2).astype(jnp.float32)
    place = place * (2.0 * math.pi * radius_pixels / length)
    return sin_cos(place * cos_a) + sin_cos(place * sin_a)


def turned(real, imag, sine, cosine):
    sine, cosine = sine[:, None, :], cosine[:, None, :]
    return real * cosine - imag * sine, real * sine + imag * cosine


def left_rows(rows, sine, cosine):
    count, pupil = sine.shape
    left = jnp.concatenate(turned(rows[None, :, :pupil], rows[None, :, pupil:], sine, cosine), 2)
    return left.reshape(count * rows.shape[0], 2 * pupil).astype(jnp.bfloat16)


def half_way(left, field, sine, cosine):
    count, pupil = sine.shape
    rows = left.shape[0]
    half = jnp.dot(left, field, preferred_element_type=jnp.float32)
    half = half.reshape(count, rows // count, 2 * pupil)
    real, imag = turned(half[:, :, :pupil], half[:, :, pupil:], sine, cosine)
    real = real.reshape(rows, pupil).astype(jnp.bfloat16)
    imag = imag.reshape(rows, pupil).astype(jnp.bfloat16)
    return jnp.concatenate([jnp.concatenate([real, -imag], 1), jnp.concatenate([imag, real], 1)], 0)


def detect(left, field, full_ref, sine, cosine, frame_ref):
    row_count, length = frame_ref.shape
    count = sine.shape[0]
    both = half_way(left, field, sine, cosine)
    detector = jnp.dot(both, full_ref[...], preferred_element_type=jnp.float32)
    squares = (detector * detector).reshape(2 * count, row_count, length)
    frame_ref[...] = jnp.sum(squares, 0) * (1.0 / count)


def read_signals(frame_ref, pixels):
    row_count, length = frame_ref.shape
    per_row = length // LANES
    own = pixels - lax.axis_index("mod") * (row_count * length)
    low = own & (LANES - 1)
    run = (own >> 7) & (per_row - 1)
    row = own >> (per_row * LANES).bit_length() - 1
    rows = []
    for i in range(row_count):
        picked = []
        for j in range(per_row):
            spread = jnp.broadcast_to(frame_ref[i : i + 1, j * LANES : (j + 1) * LANES], pixels.shape)
            picked.append(jnp.take_along_axis(spread, low, axis=1, mode="promise_in_bounds"))
        rows.append(choose(picked, run))
    total = choose(rows, row)
    return total.astype(jnp.bfloat16).astype(jnp.float32)


def first_kernel(
    angles_ref, field_ref, rows_ref, full_ref, pixels_hbm, recon_hbm, signal_ref, tilt_ref, left_ref, recon_ref,
    pixels_ref, frame_ref, semaphores,
):
    length = frame_ref.shape[1]
    pupil = length // 2
    pixels, recon = copies(
        [(pixels_hbm, pixels_ref), (recon_hbm.at[recon_hbm.shape[0] - recon_ref.shape[0] :], recon_ref)], semaphores
    )
    tilts = tilt_factors(angles_ref, pupil, length)
    tilt_ref[0], tilt_ref[1] = tilts[2:]
    left = left_rows(rows_ref[...], *tilts[:2])
    left_ref[...] = left
    field = field_matrix(field_ref[:, :pupil], field_ref[:, pupil:])
    detect(left, field, full_ref, *tilts[2:], frame_ref)
    pixels.wait()
    signal_ref[...] = read_signals(frame_ref, pixels_ref[...])
    recon.wait()


def add_commands(parts_ref, total_ref, out_ref):
    messages, pieces, _ = parts_ref.shape
    cases = out_ref.shape[0] // pieces
    each = messages // cases
    sums = [jnp.sum(parts_ref[i * each : (i + 1) * each].astype(jnp.float32), 0) for i in range(cases)]
    sums = loop_gain * jnp.concatenate(sums, 0)
    out_ref[...] = sums if total_ref is None else total_ref[...] + sums


def later_kernel(
    parts_ref, tilt_ref, cells_ref, gx_ref, gy_ref, left_ref, full_ref, phase_ref, amp_ref, pixels_hbm, recon_hbm,
    *refs
):
    old_total, refs = (None, refs) if len(refs) == 6 else (refs[0], refs[1:])
    frame_ref, signal_ref, new_total_ref, recon_ref, pixels_ref, semaphores = refs
    pixels, recon = copies(
        [(pixels_hbm, pixels_ref), (recon_hbm.at[recon_hbm.shape[0] - recon_ref.shape[0] :], recon_ref)], semaphores
    )
    add_commands(parts_ref, old_total, new_total_ref)
    grid = look_up(*runs(new_total_ref), cells_ref[...])
    surface = mirror_surface(grid, gx_ref, gy_ref)
    pixels.wait()
    field = field_matrix(*field_parts(phase_ref[...] - surface, amp_ref[...]))

    detect(left_ref[...], field, full_ref, tilt_ref[0], tilt_ref[1], frame_ref)
    signal_ref[...] = read_signals(frame_ref, pixels_ref[...])
    recon.wait()


def command_kernel(*refs):
    signal_refs, recon_refs, out_ref = refs[:-3], refs[-3:-1], refs[-1]
    cases = len(signal_refs)
    own_case = lax.axis_index("case")
    received = [ref[...] for ref in signal_refs]
    ordered = []
    for case in range(cases):
        values = received[0]
        for j in range(1, cases):
            values = jnp.where((own_case ^ j) == case, received[j], values)
        ordered.append(values)
    groups = received[0].shape[0]
    signals = jnp.concatenate(
        [jnp.concatenate([values[g : g + 1] for values in ordered], 0) for g in range(groups)], 1
    ).astype(jnp.bfloat16)
    partial = jnp.concatenate(
        [
            lax.dot_general(signals, ref[...], (((1,), (1,)), ((), ())), preferred_element_type=jnp.float32)
            for ref in recon_refs
        ],
        1,
    )
    messages, pieces, width = out_ref.shape
    copies_each = messages // cases
    for case in range(cases):
        message = jnp.concatenate(
            [partial[case : case + 1, i * width : (i + 1) * width] for i in range(pieces)], 0
        ).astype(jnp.bfloat16)
        for i in range(copies_each):
            out_ref[case * copies_each + i] = message


def last_kernel(parts_ref, total_ref, frame_ref, total_hbm, frame_hbm, sums_ref, out_ref, semaphores):
    frame_out = pltpu.make_async_copy(frame_ref, frame_hbm, semaphores.at[0])
    frame_out.start()
    add_commands(parts_ref, total_ref, sums_ref)
    rows, width = sums_ref.shape
    for i in range(rows):
        out_ref[:, i * width : (i + 1) * width] = sums_ref[i : i + 1, :]
    total_out = pltpu.make_async_copy(out_ref, total_hbm, semaphores.at[1])
    total_out.start()
    frame_out.wait()
    total_out.wait()


def body(turbulence, pupil_amp, mod_points, valid_pix, recon, gx, gy, act_map):
    pupil = pupil_amp.shape[0]
    length = 2 * pupil
    cases = lax.axis_size("case")
    devices_mod = lax.axis_size("mod")
    count = devices_mod * mod_points.shape[0]
    row_count = length // devices_mod
    block = recon.shape[0]
    pieces = 2
    width = block // pieces
    signal_rows = valid_pix.shape[0] // LANES
    grid_rows, grid_columns = gx.shape[1], gy.shape[1]
    packed = grid_columns * grid_rows // LANES
    screen = turbulence[0]
    pixels = valid_pix.reshape(signal_rows, LANES)
    f32, bf16 = jnp.float32, jnp.bfloat16
    shape = jax.ShapeDtypeStruct
    hbm = pl.BlockSpec(memory_space=pltpu.HBM)
    vmem = pl.BlockSpec(memory_space=pltpu.VMEM)
    smem = pl.BlockSpec(memory_space=pltpu.SMEM)

    def call(kernel, name, outs, out_specs, in_specs, scratch, *operands):
        operands = [
            pltpu.with_memory_space_constraint(operand, pltpu.HBM) if spec is hbm else operand
            for operand, spec in zip(operands, in_specs)
        ]
        if isinstance(outs, tuple):
            outs = tuple(
                pltpu.HBM(out.shape, out.dtype) if spec is hbm else out for out, spec in zip(outs, out_specs)
            )
        return pl.pallas_call(
            kernel,
            out_shape=outs,
            in_specs=in_specs,
            out_specs=out_specs,
            scratch_shapes=scratch,
            compiler_params=pltpu.CompilerParams(vmem_limit_bytes=VMEM_LIMIT),
            name=name,
        )(*operands)

    def like(*arrays):
        return [pltpu.VMEM(array.shape, array.dtype) for array in arrays]

    def done(count):
        return pltpu.SemaphoreType.DMA((count,))

    table = pyramid_table(pupil, length)
    rows_table = jnp.asarray(np.concatenate([table.real, table.imag], 1).astype(np.float32))
    full_table = jnp.asarray(np.concatenate([table.real.T, table.imag.T], 0).astype(jnp.bfloat16))

    with jax.named_scope("modulation_angles"):
        angles = call(
            spread_kernel, "spread", shape((devices_mod, 1, LANES), f32), vmem, [smem], [], mod_points
        )
        angles = lax.all_to_all(angles, "mod", 0, 0, tiled=True).reshape(count, LANES)

    recon_early = block // LANES * 6 // 10 * LANES
    late_shape = shape((block - recon_early, recon.shape[1]), bf16)
    map_shape = (act_map.shape[0] // LANES, LANES)
    field, rows, full, cells, gx_parts, gy_parts, recon_first, phase, amplitude = call(
        prepare_kernel,
        "prepare",
        (
            shape((pupil, 2 * pupil), bf16),
            shape((row_count, 2 * pupil), f32),
            shape(full_table.shape, bf16),
            shape((packed, LANES), jnp.int32),
            shape((pupil, 4 * grid_rows), bf16),
            shape((pupil, 3 * grid_columns), bf16),
            shape((recon_early, recon.shape[1]), bf16),
            shape(screen.shape, f32),
            shape(pupil_amp.shape, f32),
        ),
        (vmem,) * 9,
        [hbm] * 8,
        [
            pltpu.VMEM(map_shape, jnp.int32),
            pltpu.VMEM(gx.shape[::-1], f32),
            pltpu.VMEM(gy.shape[::-1], f32),
            pltpu.VMEM(map_shape, f32),
            done(8),
        ],
        screen, pupil_amp, act_map.reshape(map_shape), gx.T, gy.T, rows_table, full_table, recon,
    )

    def commands(signal, recon_late):
        signals = [signal]
        for j in range(1, cases):
            signals.append(lax.ppermute(signal, "case", [(i, i ^ j) for i in range(cases)]))
        partial = call(
            command_kernel, "commands", shape((cases * devices_mod, pieces, width), bf16), vmem,
            [vmem] * (cases + 2), [], *signals, recon_first, recon_late,
        )
        return lax.all_to_all(partial, ("case", "mod"), 0, 0, tiled=True)

    frame_shape = shape((row_count, length), f32)
    signal_shape = shape((signal_rows, LANES), f32)
    total_shape = shape((cases * pieces, width), f32)
    left_shape = shape((count * row_count, 2 * pupil), bf16)
    signal, tilts, left, recon_late = call(
        first_kernel,
        "first_frame",
        (signal_shape, shape((2, count, pupil), f32), left_shape, late_shape),
        (vmem, vmem, vmem, vmem),
        [vmem, vmem, vmem, vmem, hbm, hbm],
        like(pixels, frame_shape) + [done(2)],
        angles, field, rows, full, pixels, recon,
    )
    totals = ()
    for iteration in range(1, STEPS):
        parts = commands(signal, recon_late)
        frame, signal, *totals, recon_late = call(
            later_kernel,
            "next_frame",
            (frame_shape, signal_shape, total_shape, late_shape),
            (vmem, vmem, vmem, vmem),
            [vmem] * 9 + [hbm] * 2 + [vmem] * len(totals),
            like(pixels) + [done(2)],
            parts, tilts, cells, gx_parts, gy_parts, left, full, phase, amplitude, pixels, recon, *totals,
        )
    parts = commands(signal, recon_late)
    command_shape = shape((1, cases * block), f32)
    command_total, frame = call(
        last_kernel,
        "total",
        (command_shape, frame_shape),
        (hbm, hbm),
        [vmem, vmem, vmem],
        like(total_shape, command_shape) + [done(2)],
        parts, *totals, frame,
    )
    return (command_total, frame[None])


def solution(mesh):
    return jax.shard_map(
        body,
        mesh=mesh,
        in_specs=(P("case", None, None), P(), P("mod"), P("mod"), P("case", "mod"), P(), P(), P()),
        out_specs=(P("case", None), P("case", "mod", None)),
        check_vma=False,
    )
```

```python
import math

import jax
import jax.numpy as jnp
import numpy as np
from jax import lax
from jax.experimental import pallas as pl
from jax.experimental.pallas import tpu as pltpu
from jax.sharding import PartitionSpec as P

STEPS = 2


loop_gain = 0.5
radius_pixels = 6.0
point_count = 256
LANES = 128
VMEM_LIMIT = 16 * 1024 * 1024


def rounded_table(angle, length, sign):
    scale = 1.0 / math.sqrt(length)
    real = (np.cos(angle) * scale).astype(np.float32).astype(jnp.bfloat16).astype(np.float64)
    imag = (sign * np.sin(angle) * scale).astype(np.float32).astype(jnp.bfloat16).astype(np.float64)
    return real + 1j * imag


def pyramid_table(pupil_size, length):
    centred = np.arange(length) - length // 2
    forward = np.mod(centred[:, None] * np.arange(pupil_size)[None, :], length) * (2.0 * math.pi / length)
    inverse = np.mod(np.arange(length)[:, None] * centred[None, :], length) * (2.0 * math.pi / length)
    mask = np.array([1, 1j, -1, -1j])[np.abs(centred) % 4]
    return rounded_table(inverse, length, 1.0) @ (mask[:, None] * rounded_table(forward, length, -1.0))


def half_angle(angle):
    turns = angle * (0.5 / math.pi)
    rest = turns - jnp.floor(turns + 0.5)
    square = rest * rest
    sine = rest * polynomial(square, (4.442867756, -7.307443618, 3.594788074, -0.784373999))
    cosine = polynomial(square, (1.414213538, -6.978850841, 5.739460945, -1.883563042, 0.310698181))
    return sine, cosine


def sin_cos(angle):
    sine, cosine = half_angle(angle)
    return sine * cosine, 1.0 - sine * sine


def field_parts(phase, amplitude):
    sine, cosine = half_angle(phase)
    lead = amplitude * sine
    return (amplitude - lead * sine).astype(jnp.bfloat16), (lead * cosine).astype(jnp.bfloat16)


def polynomial(x, coefficients):
    value = coefficients[-1]
    for coefficient in coefficients[-2::-1]:
        value = value * x + coefficient
    return value


def field_matrix(real, imag):
    return jnp.concatenate([jnp.concatenate([real, imag], 1), jnp.concatenate([-imag, real], 1)], 0)


def halves(values):
    high = values.astype(jnp.bfloat16)
    low = (values - high.astype(jnp.float32)).astype(jnp.bfloat16)
    return high, low


def choose(picked, index):
    while len(picked) > 1:
        odd = index & 1 == 1
        rest = picked[len(picked) - 1 :] if len(picked) % 2 else []
        picked = [jnp.where(odd, picked[j + 1], picked[j]) for j in range(0, len(picked) - 1, 2)] + rest
        index = index >> 1
    return picked[0]


def look_up(count, row, index):
    blocks = []
    for start in range(0, index.shape[0], 8):
        block = index[start : start + 8]
        high = block >> 7
        low = block & (LANES - 1)
        picked = []
        for i in range(count):
            spread = jnp.broadcast_to(row(i), block.shape)
            picked.append(jnp.take_along_axis(spread, low, axis=1, mode="promise_in_bounds"))
        blocks.append(choose(picked, high))
    return jnp.concatenate(blocks, 0) if len(blocks) > 1 else blocks[0]


def runs(ref):
    per_row = ref.shape[1] // LANES

    def row(i):
        column = (i % per_row) * LANES
        return ref[i // per_row : i // per_row + 1, column : column + LANES]

    return ref.shape[0] * per_row, row


def copies(pairs, semaphores):
    started = [pltpu.make_async_copy(*pair, semaphores.at[i]) for i, pair in enumerate(pairs)]
    for copy in started:
        copy.start()
    return started


def own_rows(rows_hbm, row_count):
    start = pl.multiple_of(lax.axis_index("mod") * row_count, row_count)
    return rows_hbm.at[pl.ds(start, row_count)]


def spread_kernel(point_ref, angles_ref):
    angle = point_ref[0].astype(jnp.float32) * (2.0 * math.pi / point_count)
    angles_ref[...] = jnp.full(angles_ref.shape, angle, jnp.float32)


def prepare_kernel(
    phase_hbm, amp_hbm, map_hbm, gxt_hbm, gyt_hbm, rows_hbm, full_hbm, recon_hbm,
    field_ref, rows_ref, full_ref, cells_ref, gx_ref, gy_ref, recon_ref, phase_ref, amp_ref,
    map_ref, gxt_ref, gyt_ref, floats, semaphores,
):
    actuators, gxt, gyt, phase, amp, rows, full, recon = copies(
        [
            (map_hbm, map_ref), (gxt_hbm, gxt_ref), (gyt_hbm, gyt_ref), (phase_hbm, phase_ref), (amp_hbm, amp_ref),
            (own_rows(rows_hbm, rows_ref.shape[0]), rows_ref), (full_hbm, full_ref),
            (recon_hbm.at[: recon_ref.shape[0]], recon_ref),
        ],
        semaphores,
    )
    grid_rows, grid_columns = gxt_ref.shape[0], gyt_ref.shape[0]
    packed = cells_ref.shape[0]
    actuators.wait()
    floats[...] = map_ref[...].astype(jnp.float32)
    lane = lax.broadcasted_iota(jnp.int32, cells_ref.shape, 1)
    cell = (lane % grid_rows) * grid_columns + (lane // grid_rows) * packed
    cell = cell + lax.broadcasted_iota(jnp.int32, cells_ref.shape, 0)
    cells_ref[...] = look_up(*runs(floats), cell).astype(jnp.int32)
    gxt.wait()
    high, low = halves(gxt_ref[...].T)
    gx_ref[...] = jnp.concatenate([high, low, high, jnp.zeros_like(high)], 1)
    gyt.wait()
    high, low = halves(gyt_ref[...].T)
    gy_ref[...] = jnp.concatenate([high, low, high], 1)
    phase.wait()
    amp.wait()
    field_ref[...] = jnp.concatenate(field_parts(phase_ref[...], amp_ref[...]), 1)
    rows.wait()
    full.wait()
    recon.wait()


def mirror_surface(grid, gx_ref, gy_ref):
    f32 = jnp.float32
    lanes_used = gx_ref.shape[1] // 4
    if lanes_used == LANES:
        spread = [grid]
    else:
        lane = lax.broadcasted_iota(jnp.int32, grid.shape, 1)
        other = pltpu.roll(grid, lanes_used, 1)
        spread = [jnp.where(lane < lanes_used, grid, other), jnp.where(lane < lanes_used, other, grid)]
    transposed = jnp.concatenate(spread, 0)
    high = transposed.astype(jnp.bfloat16).astype(f32)
    parts = jnp.concatenate([high, high, transposed - high], 0).astype(jnp.bfloat16)
    high, low = halves(jnp.dot(gy_ref[...], parts, preferred_element_type=f32))
    return lax.dot_general(
        gx_ref[...], jnp.concatenate([high, low], 1), (((1,), (1,)), ((), ())), preferred_element_type=f32
    )


def tilt_factors(angles_ref, pupil, length):
    sin_a, cos_a = sin_cos(angles_ref[...])
    spread = pupil // LANES
    sin_a = jnp.concatenate([sin_a] * spread, 1)
    cos_a = jnp.concatenate([cos_a] * spread, 1)
    place = (lax.broadcasted_iota(jnp.int32, sin_a.shape, 1) - pupil // 2).astype(jnp.float32)
    place = place * (2.0 * math.pi * radius_pixels / length)
    return sin_cos(place * cos_a) + sin_cos(place * sin_a)


def turned(real, imag, sine, cosine):
    sine, cosine = sine[:, None, :], cosine[:, None, :]
    return real * cosine - imag * sine, real * sine + imag * cosine


def left_rows(rows, sine, cosine):
    count, pupil = sine.shape
    left = jnp.concatenate(turned(rows[None, :, :pupil], rows[None, :, pupil:], sine, cosine), 2)
    return left.reshape(count * rows.shape[0], 2 * pupil).astype(jnp.bfloat16)


def half_way(left, field, sine, cosine):
    count, pupil = sine.shape
    rows = left.shape[0]
    half = jnp.dot(left, field, preferred_element_type=jnp.float32)
    half = half.reshape(count, rows // count, 2 * pupil)
    real, imag = turned(half[:, :, :pupil], half[:, :, pupil:], sine, cosine)
    real = real.reshape(rows, pupil).astype(jnp.bfloat16)
    imag = imag.reshape(rows, pupil).astype(jnp.bfloat16)
    return jnp.concatenate([jnp.concatenate([real, -imag], 1), jnp.concatenate([imag, real], 1)], 0)


def detect(left, field, full_ref, sine, cosine, frame_ref):
    row_count, length = frame_ref.shape
    count = sine.shape[0]
    both = half_way(left, field, sine, cosine)
    detector = jnp.dot(both, full_ref[...], preferred_element_type=jnp.float32)
    squares = (detector * detector).reshape(2 * count, row_count, length)
    frame_ref[...] = jnp.sum(squares, 0) * (1.0 / count)


def read_signals(frame_ref, pixels):
    row_count, length = frame_ref.shape
    per_row = length // LANES
    own = pixels - lax.axis_index("mod") * (row_count * length)
    low = own & (LANES - 1)
    run = (own >> 7) & (per_row - 1)
    row = own >> (per_row * LANES).bit_length() - 1
    rows = []
    for i in range(row_count):
        picked = []
        for j in range(per_row):
            spread = jnp.broadcast_to(frame_ref[i : i + 1, j * LANES : (j + 1) * LANES], pixels.shape)
            picked.append(jnp.take_along_axis(spread, low, axis=1, mode="promise_in_bounds"))
        rows.append(choose(picked, run))
    total = choose(rows, row)
    return total.astype(jnp.bfloat16).astype(jnp.float32)


def first_kernel(
    angles_ref, field_ref, rows_ref, full_ref, pixels_hbm, signal_ref, tilt_ref, left_ref,
    pixels_ref, frame_ref, semaphores,
):
    length = frame_ref.shape[1]
    pupil = length // 2
    (pixels,) = copies([(pixels_hbm, pixels_ref)], semaphores)
    tilts = tilt_factors(angles_ref, pupil, length)
    tilt_ref[0], tilt_ref[1] = tilts[2:]
    left = left_rows(rows_ref[...], *tilts[:2])
    left_ref[...] = left
    field = field_matrix(field_ref[:, :pupil], field_ref[:, pupil:])
    detect(left, field, full_ref, *tilts[2:], frame_ref)
    pixels.wait()
    signal_ref[...] = read_signals(frame_ref, pixels_ref[...])


def fetch_kernel(tilt_ref, recon_hbm, recon_ref, semaphores):
    copies([(recon_hbm.at[recon_hbm.shape[0] - recon_ref.shape[0] :], recon_ref)], semaphores)[0].wait()


def add_commands(parts_ref, total_ref, out_ref):
    messages, pieces, _ = parts_ref.shape
    cases = out_ref.shape[0] // pieces
    each = messages // cases
    sums = [jnp.sum(parts_ref[i * each : (i + 1) * each].astype(jnp.float32), 0) for i in range(cases)]
    sums = loop_gain * jnp.concatenate(sums, 0)
    out_ref[...] = sums if total_ref is None else total_ref[...] + sums


def later_kernel(
    parts_ref, tilt_ref, cells_ref, gx_ref, gy_ref, left_ref, full_ref, phase_ref, amp_ref, pixels_hbm, recon_hbm,
    *refs
):
    old_total, refs = (None, refs) if len(refs) == 6 else (refs[0], refs[1:])
    frame_ref, signal_ref, new_total_ref, recon_ref, pixels_ref, semaphores = refs
    pixels, recon = copies(
        [(pixels_hbm, pixels_ref), (recon_hbm.at[recon_hbm.shape[0] - recon_ref.shape[0] :], recon_ref)], semaphores
    )
    add_commands(parts_ref, old_total, new_total_ref)
    grid = look_up(*runs(new_total_ref), cells_ref[...])
    surface = mirror_surface(grid, gx_ref, gy_ref)
    pixels.wait()
    field = field_matrix(*field_parts(phase_ref[...] - surface, amp_ref[...]))

    detect(left_ref[...], field, full_ref, tilt_ref[0], tilt_ref[1], frame_ref)
    signal_ref[...] = read_signals(frame_ref, pixels_ref[...])
    recon.wait()


def command_kernel(*refs):
    signal_refs, recon_refs, out_ref = refs[:-3], refs[-3:-1], refs[-1]
    cases = len(signal_refs)
    own_case = lax.axis_index("case")
    received = [ref[...] for ref in signal_refs]
    ordered = []
    for case in range(cases):
        values = received[0]
        for j in range(1, cases):
            values = jnp.where((own_case ^ j) == case, received[j], values)
        ordered.append(values)
    groups = received[0].shape[0]
    signals = jnp.concatenate(
        [jnp.concatenate([values[g : g + 1] for values in ordered], 0) for g in range(groups)], 1
    ).astype(jnp.bfloat16)
    partial = jnp.concatenate(
        [
            lax.dot_general(signals, ref[...], (((1,), (1,)), ((), ())), preferred_element_type=jnp.float32)
            for ref in recon_refs
        ],
        1,
    )
    messages, pieces, width = out_ref.shape
    copies_each = messages // cases
    for case in range(cases):
        message = jnp.concatenate(
            [partial[case : case + 1, i * width : (i + 1) * width] for i in range(pieces)], 0
        ).astype(jnp.bfloat16)
        for i in range(copies_each):
            out_ref[case * copies_each + i] = message


def last_kernel(parts_ref, total_ref, frame_ref, total_hbm, frame_hbm, sums_ref, out_ref, semaphores):
    frame_out = pltpu.make_async_copy(frame_ref, frame_hbm, semaphores.at[0])
    frame_out.start()
    add_commands(parts_ref, total_ref, sums_ref)
    rows, width = sums_ref.shape
    for i in range(rows):
        out_ref[:, i * width : (i + 1) * width] = sums_ref[i : i + 1, :]
    total_out = pltpu.make_async_copy(out_ref, total_hbm, semaphores.at[1])
    total_out.start()
    frame_out.wait()
    total_out.wait()


def body(turbulence, pupil_amp, mod_points, valid_pix, recon, gx, gy, act_map):
    pupil = pupil_amp.shape[0]
    length = 2 * pupil
    cases = lax.axis_size("case")
    devices_mod = lax.axis_size("mod")
    count = devices_mod * mod_points.shape[0]
    row_count = length // devices_mod
    block = recon.shape[0]
    pieces = 2
    width = block // pieces
    signal_rows = valid_pix.shape[0] // LANES
    grid_rows, grid_columns = gx.shape[1], gy.shape[1]
    packed = grid_columns * grid_rows // LANES
    screen = turbulence[0]
    pixels = valid_pix.reshape(signal_rows, LANES)
    f32, bf16 = jnp.float32, jnp.bfloat16
    shape = jax.ShapeDtypeStruct
    hbm = pl.BlockSpec(memory_space=pltpu.HBM)
    vmem = pl.BlockSpec(memory_space=pltpu.VMEM)
    smem = pl.BlockSpec(memory_space=pltpu.SMEM)

    def call(kernel, name, outs, out_specs, in_specs, scratch, *operands, cost=None):
        operands = [
            pltpu.with_memory_space_constraint(operand, pltpu.HBM) if spec is hbm else operand
            for operand, spec in zip(operands, in_specs)
        ]
        if isinstance(outs, tuple):
            outs = tuple(
                pltpu.HBM(out.shape, out.dtype) if spec is hbm else out for out, spec in zip(outs, out_specs)
            )
        return pl.pallas_call(
            kernel,
            out_shape=outs,
            in_specs=in_specs,
            out_specs=out_specs,
            scratch_shapes=scratch,
            compiler_params=pltpu.CompilerParams(vmem_limit_bytes=VMEM_LIMIT),
            cost_estimate=cost,
            name=name,
        )(*operands)

    def like(*arrays):
        return [pltpu.VMEM(array.shape, array.dtype) for array in arrays]

    def done(count):
        return pltpu.SemaphoreType.DMA((count,))

    table = pyramid_table(pupil, length)
    rows_table = jnp.asarray(np.concatenate([table.real, table.imag], 1).astype(np.float32))
    full_table = jnp.asarray(np.concatenate([table.real.T, table.imag.T], 0).astype(jnp.bfloat16))

    with jax.named_scope("modulation_angles"):
        angles = call(
            spread_kernel, "spread", shape((devices_mod, 1, LANES), f32), vmem, [smem], [], mod_points
        )
        angles = lax.all_to_all(angles, "mod", 0, 0, tiled=True).reshape(count, LANES)

    recon_early = block // LANES * 6 // 10 * LANES
    late_shape = shape((block - recon_early, recon.shape[1]), bf16)
    map_shape = (act_map.shape[0] // LANES, LANES)
    field, rows, full, cells, gx_parts, gy_parts, recon_first, phase, amplitude = call(
        prepare_kernel,
        "prepare",
        (
            shape((pupil, 2 * pupil), bf16),
            shape((row_count, 2 * pupil), f32),
            shape(full_table.shape, bf16),
            shape((packed, LANES), jnp.int32),
            shape((pupil, 4 * grid_rows), bf16),
            shape((pupil, 3 * grid_columns), bf16),
            shape((recon_early, recon.shape[1]), bf16),
            shape(screen.shape, f32),
            shape(pupil_amp.shape, f32),
        ),
        (vmem,) * 9,
        [hbm] * 8,
        [
            pltpu.VMEM(map_shape, jnp.int32),
            pltpu.VMEM(gx.shape[::-1], f32),
            pltpu.VMEM(gy.shape[::-1], f32),
            pltpu.VMEM(map_shape, f32),
            done(8),
        ],
        screen, pupil_amp, act_map.reshape(map_shape), gx.T, gy.T, rows_table, full_table, recon,
    )

    def commands(signal, recon_late):
        signals = [signal]
        for j in range(1, cases):
            signals.append(lax.ppermute(signal, "case", [(i, i ^ j) for i in range(cases)]))
        partial = call(
            command_kernel, "commands", shape((cases * devices_mod, pieces, width), bf16), vmem,
            [vmem] * (cases + 2), [], *signals, recon_first, recon_late,
        )
        return lax.all_to_all(partial, ("case", "mod"), 0, 0, tiled=True)

    frame_shape = shape((row_count, length), f32)
    signal_shape = shape((signal_rows, LANES), f32)
    total_shape = shape((cases * pieces, width), f32)
    left_shape = shape((count * row_count, 2 * pupil), bf16)
    signal, tilts, left = call(
        first_kernel,
        "first_frame",
        (signal_shape, shape((2, count, pupil), f32), left_shape),
        (vmem, vmem, vmem),
        [vmem, vmem, vmem, vmem, hbm],
        like(pixels, frame_shape) + [done(1)],
        angles, field, rows, full, pixels,
    )
    recon_late = call(fetch_kernel, "fetch", late_shape, vmem, [vmem, hbm], [done(1)], tilts, recon, cost=pl.CostEstimate(flops=0, bytes_accessed=late_shape.size * 4, transcendentals=0))
    totals = ()
    for iteration in range(1, STEPS):
        parts = commands(signal, recon_late)
        frame, signal, *totals, recon_late = call(
            later_kernel,
            "next_frame",
            (frame_shape, signal_shape, total_shape, late_shape),
            (vmem, vmem, vmem, vmem),
            [vmem] * 9 + [hbm] * 2 + [vmem] * len(totals),
            like(pixels) + [done(2)],
            parts, tilts, cells, gx_parts, gy_parts, left, full, phase, amplitude, pixels, recon, *totals,
        )
    parts = commands(signal, recon_late)
    command_shape = shape((1, cases * block), f32)
    command_total, frame = call(
        last_kernel,
        "total",
        (command_shape, frame_shape),
        (hbm, hbm),
        [vmem, vmem, vmem],
        like(total_shape, command_shape) + [done(2)],
        parts, *totals, frame,
    )
    return (command_total, frame[None])


def solution(mesh):
    return jax.shard_map(
        body,
        mesh=mesh,
        in_specs=(P("case", None, None), P(), P("mod"), P("mod"), P("case", "mod"), P(), P(), P()),
        out_specs=(P("case", None), P("case", "mod", None)),
        check_vma=False,
    )
```

```python
import math

import jax
import jax.numpy as jnp
import numpy as np
from jax import lax
from jax.experimental import pallas as pl
from jax.experimental.pallas import tpu as pltpu
from jax.sharding import PartitionSpec as P

STEPS = 2


loop_gain = 0.5
radius_pixels = 6.0
point_count = 256
LANES = 128
VMEM_LIMIT = 16 * 1024 * 1024


def rounded_table(angle, length, sign):
    scale = 1.0 / math.sqrt(length)
    real = (np.cos(angle) * scale).astype(np.float32).astype(jnp.bfloat16).astype(np.float64)
    imag = (sign * np.sin(angle) * scale).astype(np.float32).astype(jnp.bfloat16).astype(np.float64)
    return real + 1j * imag


def pyramid_table(pupil_size, length):
    centred = np.arange(length) - length // 2
    forward = np.mod(centred[:, None] * np.arange(pupil_size)[None, :], length) * (2.0 * math.pi / length)
    inverse = np.mod(np.arange(length)[:, None] * centred[None, :], length) * (2.0 * math.pi / length)
    mask = np.array([1, 1j, -1, -1j])[np.abs(centred) % 4]
    return rounded_table(inverse, length, 1.0) @ (mask[:, None] * rounded_table(forward, length, -1.0))


def half_angle(angle):
    turns = angle * (0.5 / math.pi)
    rest = turns - jnp.floor(turns + 0.5)
    square = rest * rest
    sine = rest * polynomial(square, (4.442867756, -7.307443618, 3.594788074, -0.784373999))
    cosine = polynomial(square, (1.414213538, -6.978850841, 5.739460945, -1.883563042, 0.310698181))
    return sine, cosine


def sin_cos(angle):
    sine, cosine = half_angle(angle)
    return sine * cosine, 1.0 - sine * sine


def field_parts(phase, amplitude):
    sine, cosine = half_angle(phase)
    lead = amplitude * sine
    return (amplitude - lead * sine).astype(jnp.bfloat16), (lead * cosine).astype(jnp.bfloat16)


def polynomial(x, coefficients):
    value = coefficients[-1]
    for coefficient in coefficients[-2::-1]:
        value = value * x + coefficient
    return value


def field_matrix(real, imag):
    return jnp.concatenate([jnp.concatenate([real, imag], 1), jnp.concatenate([-imag, real], 1)], 0)


def halves(values):
    high = values.astype(jnp.bfloat16)
    low = (values - high.astype(jnp.float32)).astype(jnp.bfloat16)
    return high, low


def choose(picked, index):
    while len(picked) > 1:
        odd = index & 1 == 1
        rest = picked[len(picked) - 1 :] if len(picked) % 2 else []
        picked = [jnp.where(odd, picked[j + 1], picked[j]) for j in range(0, len(picked) - 1, 2)] + rest
        index = index >> 1
    return picked[0]


def look_up(count, row, index):
    blocks = []
    for start in range(0, index.shape[0], 8):
        block = index[start : start + 8]
        high = block >> 7
        low = block & (LANES - 1)
        picked = []
        for i in range(count):
            spread = jnp.broadcast_to(row(i), block.shape)
            picked.append(jnp.take_along_axis(spread, low, axis=1, mode="promise_in_bounds"))
        blocks.append(choose(picked, high))
    return jnp.concatenate(blocks, 0) if len(blocks) > 1 else blocks[0]


def runs(ref):
    per_row = ref.shape[1] // LANES

    def row(i):
        column = (i % per_row) * LANES
        return ref[i // per_row : i // per_row + 1, column : column + LANES]

    return ref.shape[0] * per_row, row


def copies(pairs, semaphores):
    started = [pltpu.make_async_copy(*pair, semaphores.at[i]) for i, pair in enumerate(pairs)]
    for copy in started:
        copy.start()
    return started


def own_rows(rows_hbm, row_count):
    start = pl.multiple_of(lax.axis_index("mod") * row_count, row_count)
    return rows_hbm.at[pl.ds(start, row_count)]


def spread_kernel(point_ref, angles_ref):
    angle = point_ref[0].astype(jnp.float32) * (2.0 * math.pi / point_count)
    angles_ref[...] = jnp.full(angles_ref.shape, angle, jnp.float32)


def prepare_kernel(
    phase_hbm, amp_hbm, map_hbm, gxt_hbm, gyt_hbm, rows_hbm, full_hbm, recon_hbm,
    field_ref, rows_ref, full_ref, cells_ref, gx_ref, gy_ref, recon_ref, phase_ref, amp_ref,
    map_ref, gxt_ref, gyt_ref, floats, semaphores,
):
    actuators, gxt, gyt, phase, amp, rows, full, recon = copies(
        [
            (map_hbm, map_ref), (gxt_hbm, gxt_ref), (gyt_hbm, gyt_ref), (phase_hbm, phase_ref), (amp_hbm, amp_ref),
            (own_rows(rows_hbm, rows_ref.shape[0]), rows_ref), (full_hbm, full_ref),
            (recon_hbm.at[: recon_ref.shape[0]], recon_ref),
        ],
        semaphores,
    )
    grid_rows, grid_columns = gxt_ref.shape[0], gyt_ref.shape[0]
    packed = cells_ref.shape[0]
    actuators.wait()
    floats[...] = map_ref[...].astype(jnp.float32)
    lane = lax.broadcasted_iota(jnp.int32, cells_ref.shape, 1)
    cell = (lane % grid_rows) * grid_columns + (lane // grid_rows) * packed
    cell = cell + lax.broadcasted_iota(jnp.int32, cells_ref.shape, 0)
    cells_ref[...] = look_up(*runs(floats), cell).astype(jnp.int32)
    gxt.wait()
    high, low = halves(gxt_ref[...].T)
    gx_ref[...] = jnp.concatenate([high, low, high, jnp.zeros_like(high)], 1)
    gyt.wait()
    high, low = halves(gyt_ref[...].T)
    gy_ref[...] = jnp.concatenate([high, low, high], 1)
    phase.wait()
    amp.wait()
    field_ref[...] = jnp.concatenate(field_parts(phase_ref[...], amp_ref[...]), 1)
    rows.wait()
    full.wait()
    recon.wait()


def mirror_surface(grid, gx_ref, gy_ref):
    f32 = jnp.float32
    lanes_used = gx_ref.shape[1] // 4
    if lanes_used == LANES:
        spread = [grid]
    else:
        lane = lax.broadcasted_iota(jnp.int32, grid.shape, 1)
        other = pltpu.roll(grid, lanes_used, 1)
        spread = [jnp.where(lane < lanes_used, grid, other), jnp.where(lane < lanes_used, other, grid)]
    transposed = jnp.concatenate(spread, 0)
    high = transposed.astype(jnp.bfloat16).astype(f32)
    parts = jnp.concatenate([high, high, transposed - high], 0).astype(jnp.bfloat16)
    out = []
    step = gy_ref.shape[0] // 2
    for start in range(0, gy_ref.shape[0], step):
        high, low = halves(jnp.dot(gy_ref[start : start + step, :], parts, preferred_element_type=f32))
        out.append(
            lax.dot_general(
                gx_ref[...], jnp.concatenate([high, low], 1), (((1,), (1,)), ((), ())), preferred_element_type=f32
            )
        )
    return jnp.concatenate(out, 1)


def tilt_factors(angles_ref, pupil, length):
    sin_a, cos_a = sin_cos(angles_ref[...])
    spread = pupil // LANES
    sin_a = jnp.concatenate([sin_a] * spread, 1)
    cos_a = jnp.concatenate([cos_a] * spread, 1)
    place = (lax.broadcasted_iota(jnp.int32, sin_a.shape, 1) - pupil // 2).astype(jnp.float32)
    place = place * (2.0 * math.pi * radius_pixels / length)
    return sin_cos(place * cos_a) + sin_cos(place * sin_a)


def turned(real, imag, sine, cosine):
    sine, cosine = sine[:, None, :], cosine[:, None, :]
    return real * cosine - imag * sine, real * sine + imag * cosine


def left_rows(rows, sine, cosine):
    count, pupil = sine.shape
    left = jnp.concatenate(turned(rows[None, :, :pupil], rows[None, :, pupil:], sine, cosine), 2)
    return left.reshape(count * rows.shape[0], 2 * pupil).astype(jnp.bfloat16)


def half_way(left, field, sine, cosine):
    count, pupil = sine.shape
    rows = left.shape[0]
    half = jnp.dot(left, field, preferred_element_type=jnp.float32)
    half = half.reshape(count, rows // count, 2 * pupil)
    real, imag = turned(half[:, :, :pupil], half[:, :, pupil:], sine, cosine)
    real = real.reshape(rows, pupil).astype(jnp.bfloat16)
    imag = imag.reshape(rows, pupil).astype(jnp.bfloat16)
    return jnp.concatenate([jnp.concatenate([real, -imag], 1), jnp.concatenate([imag, real], 1)], 0)


def detect(left, field, full_ref, sine, cosine, frame_ref):
    row_count, length = frame_ref.shape
    count = sine.shape[0]
    both = half_way(left, field, sine, cosine)
    detector = jnp.dot(both, full_ref[...], preferred_element_type=jnp.float32)
    squares = (detector * detector).reshape(2 * count, row_count, length)
    frame_ref[...] = jnp.sum(squares, 0) * (1.0 / count)


def read_signals(frame_ref, pixels):
    row_count, length = frame_ref.shape
    per_row = length // LANES
    own = pixels - lax.axis_index("mod") * (row_count * length)
    low = own & (LANES - 1)
    run = (own >> 7) & (per_row - 1)
    row = own >> (per_row * LANES).bit_length() - 1
    rows = []
    for i in range(row_count):
        picked = []
        for j in range(per_row):
            spread = jnp.broadcast_to(frame_ref[i : i + 1, j * LANES : (j + 1) * LANES], pixels.shape)
            picked.append(jnp.take_along_axis(spread, low, axis=1, mode="promise_in_bounds"))
        rows.append(choose(picked, run))
    total = choose(rows, row)
    return total.astype(jnp.bfloat16).astype(jnp.float32)


def first_kernel(
    angles_ref, field_ref, rows_ref, full_ref, pixels_hbm, signal_ref, tilt_ref, left_ref,
    pixels_ref, frame_ref, semaphores,
):
    length = frame_ref.shape[1]
    pupil = length // 2
    (pixels,) = copies([(pixels_hbm, pixels_ref)], semaphores)
    tilts = tilt_factors(angles_ref, pupil, length)
    tilt_ref[0], tilt_ref[1] = tilts[2:]
    left = left_rows(rows_ref[...], *tilts[:2])
    left_ref[...] = left
    field = field_matrix(field_ref[:, :pupil], field_ref[:, pupil:])
    detect(left, field, full_ref, *tilts[2:], frame_ref)
    pixels.wait()
    signal_ref[...] = read_signals(frame_ref, pixels_ref[...])


def fetch_kernel(tilt_ref, recon_hbm, recon_ref, semaphores):
    copies([(recon_hbm.at[recon_hbm.shape[0] - recon_ref.shape[0] :], recon_ref)], semaphores)[0].wait()


def add_commands(parts_ref, total_ref, out_ref):
    messages, pieces, _ = parts_ref.shape
    cases = out_ref.shape[0] // pieces
    each = messages // cases
    sums = [jnp.sum(parts_ref[i * each : (i + 1) * each].astype(jnp.float32), 0) for i in range(cases)]
    sums = loop_gain * jnp.concatenate(sums, 0)
    out_ref[...] = sums if total_ref is None else total_ref[...] + sums


def later_kernel(
    parts_ref, tilt_ref, cells_ref, gx_ref, gy_ref, left_ref, full_ref, phase_ref, amp_ref, pixels_hbm, recon_hbm,
    *refs
):
    old_total, refs = (None, refs) if len(refs) == 6 else (refs[0], refs[1:])
    frame_ref, signal_ref, new_total_ref, recon_ref, pixels_ref, semaphores = refs
    pixels, recon = copies(
        [(pixels_hbm, pixels_ref), (recon_hbm.at[recon_hbm.shape[0] - recon_ref.shape[0] :], recon_ref)], semaphores
    )
    add_commands(parts_ref, old_total, new_total_ref)
    grid = look_up(*runs(new_total_ref), cells_ref[...])
    surface = mirror_surface(grid, gx_ref, gy_ref)
    pixels.wait()
    field = field_matrix(*field_parts(phase_ref[...] - surface, amp_ref[...]))

    detect(left_ref[...], field, full_ref, tilt_ref[0], tilt_ref[1], frame_ref)
    signal_ref[...] = read_signals(frame_ref, pixels_ref[...])
    recon.wait()


def command_kernel(*refs):
    signal_refs, recon_refs, out_ref = refs[:-3], refs[-3:-1], refs[-1]
    cases = len(signal_refs)
    own_case = lax.axis_index("case")
    received = [ref[...] for ref in signal_refs]
    ordered = []
    for case in range(cases):
        values = received[0]
        for j in range(1, cases):
            values = jnp.where((own_case ^ j) == case, received[j], values)
        ordered.append(values)
    groups = received[0].shape[0]
    signals = jnp.concatenate(
        [jnp.concatenate([values[g : g + 1] for values in ordered], 0) for g in range(groups)], 1
    ).astype(jnp.bfloat16)
    partial = jnp.concatenate(
        [
            lax.dot_general(signals, ref[...], (((1,), (1,)), ((), ())), preferred_element_type=jnp.float32)
            for ref in recon_refs
        ],
        1,
    )
    messages, pieces, width = out_ref.shape
    copies_each = messages // cases
    for case in range(cases):
        message = jnp.concatenate(
            [partial[case : case + 1, i * width : (i + 1) * width] for i in range(pieces)], 0
        ).astype(jnp.bfloat16)
        for i in range(copies_each):
            out_ref[case * copies_each + i] = message


def last_kernel(parts_ref, total_ref, frame_ref, total_hbm, frame_hbm, sums_ref, out_ref, semaphores):
    frame_out = pltpu.make_async_copy(frame_ref, frame_hbm, semaphores.at[0])
    frame_out.start()
    add_commands(parts_ref, total_ref, sums_ref)
    rows, width = sums_ref.shape
    for i in range(rows):
        out_ref[:, i * width : (i + 1) * width] = sums_ref[i : i + 1, :]
    total_out = pltpu.make_async_copy(out_ref, total_hbm, semaphores.at[1])
    total_out.start()
    frame_out.wait()
    total_out.wait()


def body(turbulence, pupil_amp, mod_points, valid_pix, recon, gx, gy, act_map):
    pupil = pupil_amp.shape[0]
    length = 2 * pupil
    cases = lax.axis_size("case")
    devices_mod = lax.axis_size("mod")
    count = devices_mod * mod_points.shape[0]
    row_count = length // devices_mod
    block = recon.shape[0]
    pieces = 2
    width = block // pieces
    signal_rows = valid_pix.shape[0] // LANES
    grid_rows, grid_columns = gx.shape[1], gy.shape[1]
    packed = grid_columns * grid_rows // LANES
    screen = turbulence[0]
    pixels = valid_pix.reshape(signal_rows, LANES)
    f32, bf16 = jnp.float32, jnp.bfloat16
    shape = jax.ShapeDtypeStruct
    hbm = pl.BlockSpec(memory_space=pltpu.HBM)
    vmem = pl.BlockSpec(memory_space=pltpu.VMEM)
    smem = pl.BlockSpec(memory_space=pltpu.SMEM)

    def call(kernel, name, outs, out_specs, in_specs, scratch, *operands, cost=None):
        operands = [
            pltpu.with_memory_space_constraint(operand, pltpu.HBM) if spec is hbm else operand
            for operand, spec in zip(operands, in_specs)
        ]
        if isinstance(outs, tuple):
            outs = tuple(
                pltpu.HBM(out.shape, out.dtype) if spec is hbm else out for out, spec in zip(outs, out_specs)
            )
        return pl.pallas_call(
            kernel,
            out_shape=outs,
            in_specs=in_specs,
            out_specs=out_specs,
            scratch_shapes=scratch,
            compiler_params=pltpu.CompilerParams(vmem_limit_bytes=VMEM_LIMIT),
            cost_estimate=cost,
            name=name,
        )(*operands)

    def like(*arrays):
        return [pltpu.VMEM(array.shape, array.dtype) for array in arrays]

    def done(count):
        return pltpu.SemaphoreType.DMA((count,))

    table = pyramid_table(pupil, length)
    rows_table = jnp.asarray(np.concatenate([table.real, table.imag], 1).astype(np.float32))
    full_table = jnp.asarray(np.concatenate([table.real.T, table.imag.T], 0).astype(jnp.bfloat16))

    with jax.named_scope("modulation_angles"):
        angles = call(
            spread_kernel, "spread", shape((devices_mod, 1, LANES), f32), vmem, [smem], [], mod_points
        )
        angles = lax.all_to_all(angles, "mod", 0, 0, tiled=True).reshape(count, LANES)

    recon_early = block // LANES * 6 // 10 * LANES
    late_shape = shape((block - recon_early, recon.shape[1]), bf16)
    map_shape = (act_map.shape[0] // LANES, LANES)
    field, rows, full, cells, gx_parts, gy_parts, recon_first, phase, amplitude = call(
        prepare_kernel,
        "prepare",
        (
            shape((pupil, 2 * pupil), bf16),
            shape((row_count, 2 * pupil), f32),
            shape(full_table.shape, bf16),
            shape((packed, LANES), jnp.int32),
            shape((pupil, 4 * grid_rows), bf16),
            shape((pupil, 3 * grid_columns), bf16),
            shape((recon_early, recon.shape[1]), bf16),
            shape(screen.shape, f32),
            shape(pupil_amp.shape, f32),
        ),
        (vmem,) * 9,
        [hbm] * 8,
        [
            pltpu.VMEM(map_shape, jnp.int32),
            pltpu.VMEM(gx.shape[::-1], f32),
            pltpu.VMEM(gy.shape[::-1], f32),
            pltpu.VMEM(map_shape, f32),
            done(8),
        ],
        screen, pupil_amp, act_map.reshape(map_shape), gx.T, gy.T, rows_table, full_table, recon,
    )

    def commands(signal, recon_late):
        signals = [signal]
        for j in range(1, cases):
            signals.append(lax.ppermute(signal, "case", [(i, i ^ j) for i in range(cases)]))
        partial = call(
            command_kernel, "commands", shape((cases * devices_mod, pieces, width), bf16), vmem,
            [vmem] * (cases + 2), [], *signals, recon_first, recon_late,
        )
        return lax.all_to_all(partial, ("case", "mod"), 0, 0, tiled=True)

    frame_shape = shape((row_count, length), f32)
    signal_shape = shape((signal_rows, LANES), f32)
    total_shape = shape((cases * pieces, width), f32)
    left_shape = shape((count * row_count, 2 * pupil), bf16)
    signal, tilts, left = call(
        first_kernel,
        "first_frame",
        (signal_shape, shape((2, count, pupil), f32), left_shape),
        (vmem, vmem, vmem),
        [vmem, vmem, vmem, vmem, hbm],
        like(pixels, frame_shape) + [done(1)],
        angles, field, rows, full, pixels,
    )
    recon_late = call(fetch_kernel, "fetch", late_shape, vmem, [vmem, hbm], [done(1)], tilts, recon, cost=pl.CostEstimate(flops=0, bytes_accessed=late_shape.size * 4, transcendentals=0))
    totals = ()
    for iteration in range(1, STEPS):
        parts = commands(signal, recon_late)
        frame, signal, *totals, recon_late = call(
            later_kernel,
            "next_frame",
            (frame_shape, signal_shape, total_shape, late_shape),
            (vmem, vmem, vmem, vmem),
            [vmem] * 9 + [hbm] * 2 + [vmem] * len(totals),
            like(pixels) + [done(2)],
            parts, tilts, cells, gx_parts, gy_parts, left, full, phase, amplitude, pixels, recon, *totals,
        )
    parts = commands(signal, recon_late)
    command_shape = shape((1, cases * block), f32)
    command_total, frame = call(
        last_kernel,
        "total",
        (command_shape, frame_shape),
        (hbm, hbm),
        [vmem, vmem, vmem],
        like(total_shape, command_shape) + [done(2)],
        parts, *totals, frame,
    )
    return (command_total, frame[None])


def solution(mesh):
    return jax.shard_map(
        body,
        mesh=mesh,
        in_specs=(P("case", None, None), P(), P("mod"), P("mod"), P("case", "mod"), P(), P(), P()),
        out_specs=(P("case", None), P("case", "mod", None)),
        check_vma=False,
    )
```

```python
import math

import jax
import jax.numpy as jnp
import numpy as np
from jax import lax
from jax.experimental import pallas as pl
from jax.experimental.pallas import tpu as pltpu
from jax.sharding import PartitionSpec as P

STEPS = 2


loop_gain = 0.5
radius_pixels = 6.0
point_count = 256
LANES = 128
VMEM_LIMIT = 16 * 1024 * 1024


def rounded_table(angle, length, sign):
    scale = 1.0 / math.sqrt(length)
    real = (np.cos(angle) * scale).astype(np.float32).astype(jnp.bfloat16).astype(np.float64)
    imag = (sign * np.sin(angle) * scale).astype(np.float32).astype(jnp.bfloat16).astype(np.float64)
    return real + 1j * imag


def pyramid_table(pupil_size, length):
    centred = np.arange(length) - length // 2
    forward = np.mod(centred[:, None] * np.arange(pupil_size)[None, :], length) * (2.0 * math.pi / length)
    inverse = np.mod(np.arange(length)[:, None] * centred[None, :], length) * (2.0 * math.pi / length)
    mask = np.array([1, 1j, -1, -1j])[np.abs(centred) % 4]
    return rounded_table(inverse, length, 1.0) @ (mask[:, None] * rounded_table(forward, length, -1.0))


def half_angle(angle):
    turns = angle * (0.5 / math.pi)
    rest = turns - jnp.floor(turns + 0.5)
    square = rest * rest
    sine = rest * polynomial(square, (4.442867756, -7.307443618, 3.594788074, -0.784373999))
    cosine = polynomial(square, (1.414213538, -6.978850841, 5.739460945, -1.883563042, 0.310698181))
    return sine, cosine


def sin_cos(angle):
    sine, cosine = half_angle(angle)
    return sine * cosine, 1.0 - sine * sine


def field_parts(phase, amplitude):
    sine, cosine = half_angle(phase)
    lead = amplitude * sine
    return (amplitude - lead * sine).astype(jnp.bfloat16), (lead * cosine).astype(jnp.bfloat16)


def polynomial(x, coefficients):
    value = coefficients[-1]
    for coefficient in coefficients[-2::-1]:
        value = value * x + coefficient
    return value


def field_matrix(real, imag):
    return jnp.concatenate([jnp.concatenate([real, imag], 1), jnp.concatenate([-imag, real], 1)], 0)


def halves(values):
    high = values.astype(jnp.bfloat16)
    low = (values - high.astype(jnp.float32)).astype(jnp.bfloat16)
    return high, low


def choose(picked, index):
    while len(picked) > 1:
        odd = index & 1 == 1
        rest = picked[len(picked) - 1 :] if len(picked) % 2 else []
        picked = [jnp.where(odd, picked[j + 1], picked[j]) for j in range(0, len(picked) - 1, 2)] + rest
        index = index >> 1
    return picked[0]


def look_up(count, row, index):
    blocks = []
    for start in range(0, index.shape[0], 8):
        block = index[start : start + 8]
        high = block >> 7
        low = block & (LANES - 1)
        picked = []
        for i in range(count):
            spread = jnp.broadcast_to(row(i), block.shape)
            picked.append(jnp.take_along_axis(spread, low, axis=1, mode="promise_in_bounds"))
        blocks.append(choose(picked, high))
    return jnp.concatenate(blocks, 0) if len(blocks) > 1 else blocks[0]


def runs(ref):
    per_row = ref.shape[1] // LANES

    def row(i):
        column = (i % per_row) * LANES
        return ref[i // per_row : i // per_row + 1, column : column + LANES]

    return ref.shape[0] * per_row, row


def copies(pairs, semaphores):
    started = [pltpu.make_async_copy(*pair, semaphores.at[i]) for i, pair in enumerate(pairs)]
    for copy in started:
        copy.start()
    return started


def own_rows(rows_hbm, row_count):
    start = pl.multiple_of(lax.axis_index("mod") * row_count, row_count)
    return rows_hbm.at[pl.ds(start, row_count)]


def spread_kernel(point_ref, angles_ref):
    angle = point_ref[0].astype(jnp.float32) * (2.0 * math.pi / point_count)
    angles_ref[...] = jnp.full(angles_ref.shape, angle, jnp.float32)


def prepare_kernel(
    phase_hbm, amp_hbm, map_hbm, gxt_hbm, gyt_hbm, rows_hbm, full_hbm, recon_hbm,
    field_ref, rows_ref, full_ref, cells_ref, gx_ref, gy_ref, recon_ref, phase_ref, amp_ref,
    map_ref, gxt_ref, gyt_ref, floats, semaphores,
):
    actuators, gxt, gyt, phase, amp, rows, full, recon = copies(
        [
            (map_hbm, map_ref), (gxt_hbm, gxt_ref), (gyt_hbm, gyt_ref), (phase_hbm, phase_ref), (amp_hbm, amp_ref),
            (own_rows(rows_hbm, rows_ref.shape[0]), rows_ref), (full_hbm, full_ref),
            (recon_hbm.at[: recon_ref.shape[0]], recon_ref),
        ],
        semaphores,
    )
    grid_rows, grid_columns = gxt_ref.shape[0], gyt_ref.shape[0]
    packed = cells_ref.shape[0]
    actuators.wait()
    floats[...] = map_ref[...].astype(jnp.float32)
    lane = lax.broadcasted_iota(jnp.int32, cells_ref.shape, 1)
    cell = (lane % grid_rows) * grid_columns + (lane // grid_rows) * packed
    cell = cell + lax.broadcasted_iota(jnp.int32, cells_ref.shape, 0)
    cells_ref[...] = look_up(*runs(floats), cell).astype(jnp.int32)
    gxt.wait()
    high, low = halves(gxt_ref[...].T)
    gx_ref[...] = jnp.concatenate([high, low, high, jnp.zeros_like(high)], 1)
    gyt.wait()
    high, low = halves(gyt_ref[...].T)
    gy_ref[...] = jnp.concatenate([high, low, high], 1)
    phase.wait()
    amp.wait()
    field_ref[...] = jnp.concatenate(field_parts(phase_ref[...], amp_ref[...]), 1)
    rows.wait()
    full.wait()
    recon.wait()


def mirror_surface(grid, gx_ref, gy_ref):
    f32 = jnp.float32
    lanes_used = gx_ref.shape[1] // 4
    if lanes_used == LANES:
        spread = [grid]
    else:
        lane = lax.broadcasted_iota(jnp.int32, grid.shape, 1)
        other = pltpu.roll(grid, lanes_used, 1)
        spread = [jnp.where(lane < lanes_used, grid, other), jnp.where(lane < lanes_used, other, grid)]
    transposed = jnp.concatenate(spread, 0)
    high = transposed.astype(jnp.bfloat16).astype(f32)
    parts = jnp.concatenate([high, high, transposed - high], 0).astype(jnp.bfloat16)
    out = []
    step = gy_ref.shape[0] // 2
    for start in range(0, gy_ref.shape[0], step):
        high, low = halves(jnp.dot(gy_ref[start : start + step, :], parts, preferred_element_type=f32))
        out.append(
            lax.dot_general(
                gx_ref[...], jnp.concatenate([high, low], 1), (((1,), (1,)), ((), ())), preferred_element_type=f32
            )
        )
    return jnp.concatenate(out, 1)


def tilt_factors(angles_ref, pupil, length):
    sin_a, cos_a = sin_cos(angles_ref[...])
    spread = pupil // LANES
    sin_a = jnp.concatenate([sin_a] * spread, 1)
    cos_a = jnp.concatenate([cos_a] * spread, 1)
    place = (lax.broadcasted_iota(jnp.int32, sin_a.shape, 1) - pupil // 2).astype(jnp.float32)
    place = place * (2.0 * math.pi * radius_pixels / length)
    return sin_cos(place * cos_a) + sin_cos(place * sin_a)


def turned(real, imag, sine, cosine):
    sine, cosine = sine[:, None, :], cosine[:, None, :]
    return real * cosine - imag * sine, real * sine + imag * cosine


def left_rows(rows, sine, cosine):
    count, pupil = sine.shape
    left = jnp.concatenate(turned(rows[None, :, :pupil], rows[None, :, pupil:], sine, cosine), 2)
    return left.reshape(count * rows.shape[0], 2 * pupil).astype(jnp.bfloat16)


def half_way(left, field, sine, cosine):
    count, pupil = sine.shape
    rows = left.shape[0]
    half = jnp.dot(left, field, preferred_element_type=jnp.float32)
    half = half.reshape(count, rows // count, 2 * pupil)
    real, imag = turned(half[:, :, :pupil], half[:, :, pupil:], sine, cosine)
    real = real.reshape(rows, pupil).astype(jnp.bfloat16)
    imag = imag.reshape(rows, pupil).astype(jnp.bfloat16)
    return jnp.concatenate([jnp.concatenate([real, -imag], 1), jnp.concatenate([imag, real], 1)], 0)


def detect(left, field, full_ref, sine, cosine, frame_ref):
    row_count, length = frame_ref.shape
    count = sine.shape[0]
    both = half_way(left, field, sine, cosine)
    detector = jnp.dot(both, full_ref[...], preferred_element_type=jnp.float32)
    squares = (detector * detector).reshape(2 * count, row_count, length)
    frame_ref[...] = jnp.sum(squares, 0) * (1.0 / count)


def read_signals(frame_ref, pixels):
    row_count, length = frame_ref.shape
    per_row = length // LANES
    own = pixels - lax.axis_index("mod") * (row_count * length)
    low = own & (LANES - 1)
    run = (own >> 7) & (per_row - 1)
    row = own >> (per_row * LANES).bit_length() - 1
    rows = []
    for i in range(row_count):
        picked = []
        for j in range(per_row):
            spread = jnp.broadcast_to(frame_ref[i : i + 1, j * LANES : (j + 1) * LANES], pixels.shape)
            picked.append(jnp.take_along_axis(spread, low, axis=1, mode="promise_in_bounds"))
        rows.append(choose(picked, run))
    total = choose(rows, row)
    return total.astype(jnp.bfloat16).astype(jnp.float32)


def first_kernel(
    angles_ref, field_ref, rows_ref, full_ref, pixels_hbm, signal_ref, tilt_ref, left_ref,
    pixels_ref, frame_ref, semaphores,
):
    length = frame_ref.shape[1]
    pupil = length // 2
    (pixels,) = copies([(pixels_hbm, pixels_ref)], semaphores)
    tilts = tilt_factors(angles_ref, pupil, length)
    tilt_ref[0], tilt_ref[1] = tilts[2:]
    left = left_rows(rows_ref[...], *tilts[:2])
    left_ref[...] = left
    field = field_matrix(field_ref[:, :pupil], field_ref[:, pupil:])
    detect(left, field, full_ref, *tilts[2:], frame_ref)
    pixels.wait()
    signal_ref[...] = read_signals(frame_ref, pixels_ref[...])


def fetch_kernel(tilt_ref, recon_hbm, recon_ref, semaphores):
    copies([(recon_hbm.at[recon_hbm.shape[0] - recon_ref.shape[0] :], recon_ref)], semaphores)[0].wait()


def add_commands(parts_ref, total_ref, out_ref):
    messages, pieces, _ = parts_ref.shape
    cases = out_ref.shape[0] // pieces
    each = messages // cases
    sums = [jnp.sum(parts_ref[i * each : (i + 1) * each].astype(jnp.float32), 0) for i in range(cases)]
    sums = loop_gain * jnp.concatenate(sums, 0)
    out_ref[...] = sums if total_ref is None else total_ref[...] + sums


def later_kernel(
    parts_ref, tilt_ref, cells_ref, gx_ref, gy_ref, left_ref, full_ref, phase_ref, amp_ref, pixels_hbm, recon_hbm,
    *refs
):
    old_total, refs = (None, refs) if len(refs) == 6 else (refs[0], refs[1:])
    frame_ref, signal_ref, new_total_ref, recon_ref, pixels_ref, semaphores = refs
    pixels, recon = copies(
        [(pixels_hbm, pixels_ref), (recon_hbm.at[recon_hbm.shape[0] - recon_ref.shape[0] :], recon_ref)], semaphores
    )
    add_commands(parts_ref, old_total, new_total_ref)
    grid = look_up(*runs(new_total_ref), cells_ref[...])
    surface = mirror_surface(grid, gx_ref, gy_ref)
    pixels.wait()
    field = field_matrix(*field_parts(phase_ref[...] - surface, amp_ref[...]))

    detect(left_ref[...], field, full_ref, tilt_ref[0], tilt_ref[1], frame_ref)
    signal_ref[...] = read_signals(frame_ref, pixels_ref[...])
    recon.wait()


def command_kernel(*refs):
    signal_refs, recon_refs, out_ref = refs[:-3], refs[-3:-1], refs[-1]
    cases = len(signal_refs)
    own_case = lax.axis_index("case")
    received = [ref[...] for ref in signal_refs]
    ordered = []
    for case in range(cases):
        values = received[0]
        for j in range(1, cases):
            values = jnp.where((own_case ^ j) == case, received[j], values)
        ordered.append(values)
    groups = received[0].shape[0]
    signals = jnp.concatenate(
        [jnp.concatenate([values[g : g + 1] for values in ordered], 0) for g in range(groups)], 1
    ).astype(jnp.bfloat16)
    partial = jnp.concatenate(
        [
            lax.dot_general(signals, ref[...], (((1,), (1,)), ((), ())), preferred_element_type=jnp.float32)
            for ref in recon_refs
        ],
        1,
    )
    messages, pieces, width = out_ref.shape
    copies_each = messages // cases
    for case in range(cases):
        message = jnp.concatenate(
            [partial[case : case + 1, i * width : (i + 1) * width] for i in range(pieces)], 0
        ).astype(jnp.bfloat16)
        for i in range(copies_each):
            out_ref[case * copies_each + i] = message


def last_kernel(parts_ref, total_ref, frame_ref, total_hbm, frame_hbm, sums_ref, out_ref, semaphores):
    frame_out = pltpu.make_async_copy(frame_ref, frame_hbm, semaphores.at[0])
    frame_out.start()
    add_commands(parts_ref, total_ref, sums_ref)
    rows, width = sums_ref.shape
    for i in range(rows):
        out_ref[:, i * width : (i + 1) * width] = sums_ref[i : i + 1, :]
    total_out = pltpu.make_async_copy(out_ref, total_hbm, semaphores.at[1])
    total_out.start()
    frame_out.wait()
    total_out.wait()


def body(turbulence, pupil_amp, mod_points, valid_pix, recon, gx, gy, act_map):
    pupil = pupil_amp.shape[0]
    length = 2 * pupil
    cases = lax.axis_size("case")
    devices_mod = lax.axis_size("mod")
    count = devices_mod * mod_points.shape[0]
    row_count = length // devices_mod
    block = recon.shape[0]
    pieces = 2
    width = block // pieces
    signal_rows = valid_pix.shape[0] // LANES
    grid_rows, grid_columns = gx.shape[1], gy.shape[1]
    packed = grid_columns * grid_rows // LANES
    screen = turbulence[0]
    pixels = valid_pix.reshape(signal_rows, LANES)
    f32, bf16 = jnp.float32, jnp.bfloat16
    shape = jax.ShapeDtypeStruct
    hbm = pl.BlockSpec(memory_space=pltpu.HBM)
    vmem = pl.BlockSpec(memory_space=pltpu.VMEM)
    smem = pl.BlockSpec(memory_space=pltpu.SMEM)

    def call(kernel, name, outs, out_specs, in_specs, scratch, *operands, cost=None):
        operands = [
            pltpu.with_memory_space_constraint(operand, pltpu.HBM) if spec is hbm else operand
            for operand, spec in zip(operands, in_specs)
        ]
        if isinstance(outs, tuple):
            outs = tuple(
                pltpu.HBM(out.shape, out.dtype) if spec is hbm else out for out, spec in zip(outs, out_specs)
            )
        return pl.pallas_call(
            kernel,
            out_shape=outs,
            in_specs=in_specs,
            out_specs=out_specs,
            scratch_shapes=scratch,
            compiler_params=pltpu.CompilerParams(vmem_limit_bytes=VMEM_LIMIT),
            cost_estimate=cost,
            name=name,
        )(*operands)

    def like(*arrays):
        return [pltpu.VMEM(array.shape, array.dtype) for array in arrays]

    def done(count):
        return pltpu.SemaphoreType.DMA((count,))

    table = pyramid_table(pupil, length)
    rows_table = jnp.asarray(np.concatenate([table.real, table.imag], 1).astype(np.float32))
    full_table = jnp.asarray(np.concatenate([table.real.T, table.imag.T], 0).astype(jnp.bfloat16))

    with jax.named_scope("modulation_angles"):
        angles = call(
            spread_kernel, "spread", shape((devices_mod, 1, LANES), f32), vmem, [smem], [], mod_points
        )
        angles = lax.all_to_all(angles, "mod", 0, 0, tiled=True).reshape(count, LANES)

    recon_early = block // LANES * 5 // 10 * LANES
    late_shape = shape((block - recon_early, recon.shape[1]), bf16)
    map_shape = (act_map.shape[0] // LANES, LANES)
    field, rows, full, cells, gx_parts, gy_parts, recon_first, phase, amplitude = call(
        prepare_kernel,
        "prepare",
        (
            shape((pupil, 2 * pupil), bf16),
            shape((row_count, 2 * pupil), f32),
            shape(full_table.shape, bf16),
            shape((packed, LANES), jnp.int32),
            shape((pupil, 4 * grid_rows), bf16),
            shape((pupil, 3 * grid_columns), bf16),
            shape((recon_early, recon.shape[1]), bf16),
            shape(screen.shape, f32),
            shape(pupil_amp.shape, f32),
        ),
        (vmem,) * 9,
        [hbm] * 8,
        [
            pltpu.VMEM(map_shape, jnp.int32),
            pltpu.VMEM(gx.shape[::-1], f32),
            pltpu.VMEM(gy.shape[::-1], f32),
            pltpu.VMEM(map_shape, f32),
            done(8),
        ],
        screen, pupil_amp, act_map.reshape(map_shape), gx.T, gy.T, rows_table, full_table, recon,
    )

    def commands(signal, recon_late):
        signals = [signal]
        for j in range(1, cases):
            signals.append(lax.ppermute(signal, "case", [(i, i ^ j) for i in range(cases)]))
        partial = call(
            command_kernel, "commands", shape((cases * devices_mod, pieces, width), bf16), vmem,
            [vmem] * (cases + 2), [], *signals, recon_first, recon_late,
        )
        return lax.all_to_all(partial, ("case", "mod"), 0, 0, tiled=True)

    frame_shape = shape((row_count, length), f32)
    signal_shape = shape((signal_rows, LANES), f32)
    total_shape = shape((cases * pieces, width), f32)
    left_shape = shape((count * row_count, 2 * pupil), bf16)
    signal, tilts, left = call(
        first_kernel,
        "first_frame",
        (signal_shape, shape((2, count, pupil), f32), left_shape),
        (vmem, vmem, vmem),
        [vmem, vmem, vmem, vmem, hbm],
        like(pixels, frame_shape) + [done(1)],
        angles, field, rows, full, pixels,
    )
    recon_late = call(fetch_kernel, "fetch", late_shape, vmem, [vmem, hbm], [done(1)], tilts, recon, cost=pl.CostEstimate(flops=0, bytes_accessed=late_shape.size * 4, transcendentals=0))
    totals = ()
    for iteration in range(1, STEPS):
        parts = commands(signal, recon_late)
        frame, signal, *totals, recon_late = call(
            later_kernel,
            "next_frame",
            (frame_shape, signal_shape, total_shape, late_shape),
            (vmem, vmem, vmem, vmem),
            [vmem] * 9 + [hbm] * 2 + [vmem] * len(totals),
            like(pixels) + [done(2)],
            parts, tilts, cells, gx_parts, gy_parts, left, full, phase, amplitude, pixels, recon, *totals,
        )
    parts = commands(signal, recon_late)
    command_shape = shape((1, cases * block), f32)
    command_total, frame = call(
        last_kernel,
        "total",
        (command_shape, frame_shape),
        (hbm, hbm),
        [vmem, vmem, vmem],
        like(total_shape, command_shape) + [done(2)],
        parts, *totals, frame,
    )
    return (command_total, frame[None])


def solution(mesh):
    return jax.shard_map(
        body,
        mesh=mesh,
        in_specs=(P("case", None, None), P(), P("mod"), P("mod"), P("case", "mod"), P(), P(), P()),
        out_specs=(P("case", None), P("case", "mod", None)),
        check_vma=False,
    )
```
